32 devices in a mesh: rows: 8 (over y, x, core), batch: 4 (over z).
Axes of the slice: x: 2, y: 2, z: 4, core: 2. Of those that a mesh axis runs over, the one named last changes fastest.
Arguments:
- inputs: bfloat16 [8, 16, 128, 512], P('batch', 'rows'), may hold values from -12 to 12
- image_counts: int32 [4], replicated, may hold values from 1 to 2, as said below
- w_down: bfloat16 [3, 3, 512, 1024], replicated, may hold values from -0.09375 to 0.09375
- w_short: bfloat16 [1024, 512], replicated, may hold values from -0.1875 to 0.1875
- w_main: bfloat16 [1024, 512], replicated, may hold values from -0.1875 to 0.1875
- w_inner: bfloat16 [512, 512], replicated, may hold values from -0.25 to 0.25
- w_spatial: bfloat16 [3, 3, 512, 512], replicated, may hold values from -0.09375 to 0.09375
- w_trans: bfloat16 [512, 512], replicated, may hold values from -0.25 to 0.25
- w_unite: bfloat16 [1024, 1024], replicated, may hold values from -0.1875 to 0.1875
- gains_wide: float32 [2, 1024], replicated, may hold values from 0.25 to 1.75
- gains_narrow: float32 [5, 512], replicated, may hold values from 0.25 to 1.75
- shifts_wide: float32 [2, 1024], replicated, may hold values from -3 to 3
- shifts_narrow: float32 [5, 512], replicated, may hold values from -3 to 3
- grad_output: bfloat16 [8, 8, 64, 1024], P('batch', 'rows'), may hold values from -6 to 6
Outputs:
- output: bfloat16 [8, 8, 64, 1024], P('batch', 'rows')
- grad_inputs: float32 [8, 16, 128, 512], P('batch', 'rows')
- grad_w_down: float32 [3, 3, 512, 1024], P(None, None, None, 'rows')
- grad_w_short: float32 [1024, 512], P(None, 'rows')
- grad_w_main: float32 [1024, 512], P(None, 'rows')
- grad_w_inner: float32 [512, 512], P(None, 'rows')
- grad_w_spatial: float32 [3, 3, 512, 512], P(None, None, None, 'rows')
- grad_w_trans: float32 [512, 512], P(None, 'rows')
- grad_w_unite: float32 [1024, 1024], P(None, 'rows')
- grad_gains_wide: float32 [2, 1024], replicated
- grad_gains_narrow: float32 [5, 512], replicated
- grad_shifts_wide: float32 [2, 1024], replicated
- grad_shifts_narrow: float32 [5, 512], replicated
The draws below stay inside these ranges and needn't reach their ends.
Inputs may be any that keep to these rules, and one draw needn't show every extreme that they name: `image_counts`: each batch group holds 1 to 2 images in its first slots; in every draw at least one group is full and one other holds a single image.
All inputs are finite; a program needn't handle non-finite values.
Results may differ from the reference program's by a relative error of at most 0.024.
Values may be sent and summed in bfloat16 or wider, within the bound.
No kernel may reach another device: no remote copies, remote signals or barrier semaphores. Data moves between devices by JAX's collectives and lax.ppermute only.
A program may use at most 192 MiB of HBM per device.

```python
import jax
import jax.numpy as jnp
from jax import lax

C_HALF = 512
C_OUT = 1024
IMG_GRP = 2
ROWS_DEV = 1
W = 64
GROUPS = 4
IMAGES = 8
H = 8
IN_H = 16
IN_W = 128
N_ROWS = 8


def draw_inputs(key, part):
    key = jax.random.fold_in(key, 11)
    row_index = jnp.arange(IN_H, dtype=jnp.float32)
    scale = (3.0 ** (row_index / max(IN_H - 1, 1)))[None, :, None, None]
    values = jax.random.truncated_normal(key, -4.0, 4.0, (IMAGES, IN_H, IN_W, C_HALF), jnp.float32) * scale
    return values.astype(jnp.bfloat16)


def draw_image_counts(key, part):
    key = jax.random.fold_in(key, 23)
    keys = jax.random.split(key, 3)
    counts = jax.random.randint(keys[0], (GROUPS,), 1, IMG_GRP + 1)
    fullest = jax.random.randint(keys[1], (), 0, GROUPS)
    single = (fullest + jax.random.randint(keys[2], (), 1, GROUPS)) % GROUPS
    places = jnp.arange(GROUPS, dtype=jnp.int32)
    counts = jnp.where(places == single, 1, counts)
    counts = jnp.where(places == fullest, IMG_GRP, counts)
    return counts.astype(jnp.int32)


def steps_of(own_key, dims, cuts, smallest, high):
    def one(position, blocks):
        heights = jax.random.uniform(jax.random.fold_in(jax.random.fold_in(own_key, 6), position), (blocks,), jnp.float32, smallest / len(cuts), high / len(cuts))
        return jnp.repeat(jnp.exp(heights), dims[position] // blocks).reshape((-1,) + (1,) * (len(dims) - position - 1))

    factor_of = one(*cuts[0])
    for cut in cuts[1:]:
        factor_of = factor_of * one(*cut)
    return factor_of


def gaussian(stream_key, extent, scale, bound, shards=(), kind=jnp.bfloat16):
    entries = jax.random.normal(stream_key, extent, jnp.float32) * scale
    if len(shards) > 0:
        entries = steps_of(stream_key, extent, shards, -0.22, 0.18) * entries
    return jnp.clip(entries, min=-bound, max=bound).astype(kind)


def setup_inputs(seed: int = 0) -> dict:
    key_list = jax.random.split(jax.random.key(seed), 15)
    inputs = draw_inputs(jax.random.fold_in(key_list[14], 71), 0)
    image_counts = draw_image_counts(jax.random.fold_in(key_list[14], 71), 0)
    w_down = gaussian(key_list[2], (3, 3, C_HALF, C_OUT), (9 * C_HALF) ** -0.5, 0.09375)
    w_short = gaussian(key_list[3], (C_OUT, C_HALF), C_OUT ** -0.5, 0.1875)
    w_main = gaussian(key_list[4], (C_OUT, C_HALF), C_OUT ** -0.5, 0.1875)
    w_inner = gaussian(key_list[5], (C_HALF, C_HALF), C_HALF ** -0.5, 0.25)
    w_spatial = gaussian(key_list[6], (3, 3, C_HALF, C_HALF), (9 * C_HALF) ** -0.5, 0.09375)
    w_trans = gaussian(key_list[7], (C_HALF, C_HALF), C_HALF ** -0.5, 0.25)
    w_unite = gaussian(key_list[8], (C_OUT, C_OUT), C_OUT ** -0.5, 0.1875)
    gains_wide = jnp.clip(1.0 + 0.15 * jax.random.normal(key_list[9], (2, C_OUT), jnp.float32), 0.25, 1.75)
    gains_narrow = jnp.clip(1.0 + 0.15 * jax.random.normal(key_list[10], (5, C_HALF), jnp.float32), 0.25, 1.75)
    shifts_wide = gaussian(key_list[11], (2, C_OUT), 0.5, 3.0, (), jnp.float32)
    shifts_narrow = gaussian(key_list[12], (5, C_HALF), 0.5, 3.0, (), jnp.float32)
    grad_output = gaussian(key_list[13], (IMAGES, H, W, C_OUT), 1.0, 6.0, ((0, 4), (1, 8)))
    return {"inputs": inputs, "image_counts": image_counts, "w_down": w_down, "w_short": w_short, "w_main": w_main, "w_inner": w_inner, "w_spatial": w_spatial, "w_trans": w_trans, "w_unite": w_unite, "gains_wide": gains_wide, "gains_narrow": gains_narrow, "shifts_wide": shifts_wide, "shifts_narrow": shifts_narrow, "grad_output": grad_output}


@jax.custom_vjp
def low(v):
    return lax.optimization_barrier(v.astype(jnp.bfloat16)).astype(jnp.float32)

@jax.custom_vjp
def low_back(v):
    return v

def low_keep(v):
    return (low(v), None)

def low_pass(kept, grad):
    return (grad,)

def back_keep(v):
    return (v, None)

def back_low(kept, grad):
    return (low(grad),)
low.defvjp(low_keep, low_pass)
low_back.defvjp(back_keep, back_low)
EPSILON = 1e-05
LAYOUT = ('NHWC', 'HWIO', 'NHWC')

def mish_act(values):
    return values * jnp.tanh(jax.nn.softplus(values))

def norm_act(pre_norm, weights, pixels, gain, offset):
    center = lax.optimization_barrier(jnp.sum(pre_norm * weights, axis=(0, 1, 2))) / pixels
    centered = pre_norm - center
    spread = lax.optimization_barrier(jnp.sum(centered * centered * weights, axis=(0, 1, 2))) / pixels
    return mish_act(centered * lax.rsqrt(spread + EPSILON) * gain + offset)

def pointwise(values, matrix):
    return jnp.einsum('bhwc,cd->bhwd', values, matrix, precision=lax.Precision.HIGHEST)

def window_conv(values, kernel, stride, padding):
    return lax.conv_general_dilated(values, kernel, (stride, stride), padding, dimension_numbers=LAYOUT, precision=lax.Precision.HIGHEST)

def forward(inputs, w_down, w_short, w_main, w_inner, w_spatial, w_trans, w_unite, gains_wide, gains_narrow, shifts_wide, shifts_narrow, weights, pixels):
    down_pre = low_back(window_conv(inputs, w_down, 2, ((1, 0), (1, 0))))
    sectioned = low(norm_act(down_pre, weights, pixels, gains_wide[0], shifts_wide[0]))
    short_pre = low_back(pointwise(sectioned, w_short))
    main_pre = low_back(pointwise(sectioned, w_main))
    shortcut = low(norm_act(short_pre, weights, pixels, gains_narrow[0], shifts_narrow[0]))
    mainline = low(norm_act(main_pre, weights, pixels, gains_narrow[1], shifts_narrow[1]))
    inner_pre = low_back(pointwise(mainline, w_inner))
    inner_act = low(norm_act(inner_pre, weights, pixels, gains_narrow[2], shifts_narrow[2]))
    spatial_pre = low_back(window_conv(inner_act, w_spatial, 1, ((1, 1), (1, 1))))
    merged = low(mainline + norm_act(spatial_pre, weights, pixels, gains_narrow[3], shifts_narrow[3]))
    trans_pre = low_back(pointwise(merged, w_trans))
    transition = low(norm_act(trans_pre, weights, pixels, gains_narrow[4], shifts_narrow[4]))
    unite_pre = low_back(pointwise(jnp.concatenate([shortcut, transition], axis=3), w_unite))
    return norm_act(unite_pre, weights, pixels, gains_wide[1], shifts_wide[1]) * weights

def reference(inputs, image_counts, w_down, w_short, w_main, w_inner, w_spatial, w_trans, w_unite, gains_wide, gains_narrow, shifts_wide, shifts_narrow, grad_output):
    slots = jnp.arange(IMG_GRP * GROUPS, dtype=jnp.int32)
    owners = slots // IMG_GRP
    filled = lax.optimization_barrier(jnp.sum(jnp.where(owners[:, None] == jnp.arange(GROUPS, dtype=jnp.int32)[None, :], image_counts[None, :], 0), axis=1))
    weights = (slots % IMG_GRP < filled).astype(jnp.float32).reshape(-1, 1, 1, 1)
    pixels = jnp.sum(image_counts).astype(jnp.float32) * (ROWS_DEV * N_ROWS * W)
    params = (inputs.astype(jnp.float32), w_down.astype(jnp.float32), w_short.astype(jnp.float32), w_main.astype(jnp.float32), w_inner.astype(jnp.float32), w_spatial.astype(jnp.float32), w_trans.astype(jnp.float32), w_unite.astype(jnp.float32), gains_wide.astype(jnp.float32), gains_narrow.astype(jnp.float32), shifts_wide.astype(jnp.float32), shifts_narrow.astype(jnp.float32))

    def wrapped(*values):
        return forward(*values, weights, pixels)
    result, pull = jax.vjp(wrapped, *params)
    grads = pull(grad_output.astype(jnp.float32))
    return (result.astype(jnp.bfloat16), grads[0], grads[1], grads[2], grads[3], grads[4], grads[5], grads[6], grads[7], grads[8], grads[9], grads[10], grads[11])
```

```python
import jax
import jax.numpy as jnp
from jax import lax
from jax.sharding import PartitionSpec as P

EPSILON = 1e-05
LAYOUT = ("NHWC", "HWIO", "NHWC")
FAR = 20.0


def mish(values):
    grown = jnp.exp(jnp.minimum(values, FAR))
    wide = grown * (grown + 2.0)
    return values * (wide / (wide + 2.0))


def mish_slope(values):
    grown = jnp.exp(jnp.minimum(values, FAR))
    wide = grown * (grown + 2.0)
    share = 1.0 / (wide + 2.0)
    return wide * share + 4.0 * values * (grown * (grown + 1.0) * share) * share


def tree_sum(parts):
    while len(parts) > 1:
        parts = [parts[i] + parts[i + 1] for i in range(0, len(parts), 2)]
    return parts[0]


class Plane:
    def __init__(self):
        self.rows = lax.axis_size("rows")
        self.groups = lax.axis_size("batch")
        self.chips = self.rows // 2
        self.place = lax.axis_index("rows")
        self.core = self.place % 2
        self.chip = self.place // 2

    def swap(self, value):
        return lax.ppermute(value, "rows", [(i, i ^ 1) for i in range(self.rows)])

    def chip_hop(self, value, step):
        return lax.ppermute(value, "rows", [(i, i ^ (2 * step)) for i in range(self.rows)])

    def plane_hop(self, value, step):
        return lax.ppermute(value, "batch", [(i, i ^ step) for i in range(self.groups)])

    def by_core(self, mine, got):
        first = self.core == 0
        return jnp.where(first, mine, got), jnp.where(first, got, mine)

    def image_of(self, block):
        mine = lax.dynamic_index_in_dim(block, self.core, 0, keepdims=False)
        other = lax.dynamic_index_in_dim(block, 1 - self.core, 0, keepdims=False)
        piece = jnp.concatenate(self.by_core(mine, self.swap(other)), axis=0)
        height = piece.shape[0]
        image = jnp.zeros((self.chips * height,) + piece.shape[1:], piece.dtype)
        for step in range(self.chips):
            part = piece if step == 0 else self.chip_hop(piece, step)
            image = lax.dynamic_update_slice_in_dim(image, part, (self.chip ^ step) * height, 0)
        return image

    def rows_of(self, mine, other):
        return jnp.stack(self.by_core(mine, self.swap(other)), axis=0)

    def group_sum(self, value):
        value = value + self.swap(value)
        return tree_sum(
            [value] + [self.plane_hop(value, step) for step in range(1, self.groups)]
        )

    def group_moments(self, sums, count_here, count_pair, pixels):
        got = self.swap(sums)
        total = sums[0] + got[0]
        count_there = count_pair - count_here
        gap = sums[0] / jnp.maximum(count_here, 1.0) - got[0] / jnp.maximum(count_there, 1.0)
        spread = sums[1] + got[1] + gap * gap * (count_here * count_there / count_pair)
        pair = jnp.stack([total, spread, total * total / count_pair])
        pairs = [pair[:2]] + [self.plane_hop(pair[:2], step) for step in range(1, self.groups)]
        counts = [count_pair] + [
            self.counts[lax.axis_index("batch") ^ step] for step in range(1, self.groups)
        ]
        center = tree_sum([p[0] for p in pairs]) / pixels
        total = tree_sum(
            [p[1] + n * jnp.square(p[0] / n - center) for p, n in zip(pairs, counts)]
        )
        return center, lax.rsqrt(total / pixels + EPSILON)


def moments(pre, weight):
    cells = pre.shape[0]
    total = jnp.sum(pre, axis=0)
    centered = pre - total / cells
    return jnp.stack([total, jnp.sum(centered * centered, axis=0)]) * weight


def dot(a, b):
    return jnp.dot(a, b, preferred_element_type=jnp.float32)


def dot_back(a, b):
    return lax.dot_general(a, b, (((1,), (1,)), ((), ())), preferred_element_type=jnp.float32)


def dot_cells(a, b):
    return lax.dot_general(a, b, (((0,), (0,)), ((), ())), preferred_element_type=jnp.float32)


def flipped(kernel):
    return jnp.swapaxes(jnp.flip(kernel, (0, 1)), 2, 3)


class Norm:
    def __init__(self, pre, center, rstd, gain, offset):
        self.pre, self.center, self.rstd, self.gain = pre, center, rstd, gain
        self.unit = (pre - center) * rstd
        self.shifted = self.unit * gain + offset

    def act(self):
        return mish(self.shifted)

    def incoming(self, grad):
        self.pushed = grad * mish_slope(self.shifted)
        return jnp.stack(
            [jnp.sum(self.pushed, axis=0), jnp.sum(self.pushed * self.unit, axis=0)]
        )

    def outgoing(self, sums, weight, pixels):
        return (
            weight
            * (self.gain * self.rstd)
            * (self.pushed - (sums[0] + self.unit * sums[1]) / pixels)
        ).astype(jnp.bfloat16)


def on_device(
    inputs,
    image_counts,
    w_down,
    w_short,
    w_main,
    w_inner,
    w_spatial,
    w_trans,
    w_unite,
    gains_wide,
    gains_narrow,
    shifts_wide,
    shifts_narrow,
    grad_output,
):
    half = w_short.shape[1]
    full = 2 * half
    slots, height_dev, width, _ = grad_output.shape
    here = Plane()
    height = here.rows * height_dev
    cells = height * width
    row_cells = height_dev * width
    batch = lax.axis_index("batch")
    own_count = image_counts[batch]
    pixels = jnp.sum(image_counts).astype(jnp.float32) * cells
    here.counts = image_counts.astype(jnp.float32) * cells
    weight = (here.core < own_count).astype(jnp.float32)
    count_here = weight * cells
    count_pair = here.counts[batch]

    below = [(i, i + 1) for i in range(here.rows - 1)]
    borrowed = lax.ppermute(inputs[:, -1:], "rows", below)
    down_source = jnp.pad(
        jnp.concatenate([borrowed, inputs], axis=1), ((0, 0), (0, 0), (1, 0), (0, 0))
    )
    down_rows = lax.conv_general_dilated(
        down_source,
        w_down,
        (2, 2),
        ((0, 0), (0, 0)),
        dimension_numbers=LAYOUT,
        preferred_element_type=jnp.float32,
    )
    slot_weight = (jnp.arange(slots) < own_count).astype(jnp.float32).reshape(-1, 1, 1, 1)
    group_rows = image_counts.astype(jnp.float32) * row_cells
    total = jnp.sum(down_rows * slot_weight, axis=(0, 1, 2))
    centered = down_rows - total / group_rows[batch]
    sums = jnp.stack([total, jnp.sum(centered * centered * slot_weight, axis=(0, 1, 2))])
    down_pre = here.image_of(down_rows.astype(jnp.bfloat16))
    devices = here.rows * here.groups
    spread_out = jnp.broadcast_to(sums[None], (devices,) + sums.shape)
    gathered = lax.all_to_all(spread_out, ("rows", "batch"), 0, 0, tiled=True)
    gathered = gathered.reshape(here.rows, here.groups, 2, full)
    center = jnp.sum(gathered[:, :, 0], axis=(0, 1)) / pixels
    gaps = gathered[:, :, 0] / group_rows[None, :, None] - center
    squares = jnp.sum(gathered[:, :, 1] + group_rows[None, :, None] * gaps * gaps, axis=(0, 1))
    rstd = lax.rsqrt(squares / pixels + EPSILON)
    down = Norm(
        down_pre.reshape(cells, full).astype(jnp.float32),
        center,
        rstd,
        gains_wide[0],
        shifts_wide[0],
    )
    grad_out = here.image_of(grad_output).reshape(cells, full)
    source = here.image_of(inputs)

    def normed(pre, gain, offset):
        sums = moments(pre, weight)
        return Norm(pre, *here.group_moments(sums, count_here, count_pair, pixels), gain, offset)

    sectioned = down.act().astype(jnp.bfloat16)
    split_pre = jnp.concatenate([dot(sectioned, w_short), dot(sectioned, w_main)], axis=1)
    split_sums = moments(split_pre, weight)
    split_center, split_rstd = here.group_moments(split_sums, count_here, count_pair, pixels)
    short = Norm(
        split_pre[:, :half], split_center[:half], split_rstd[:half], gains_narrow[0], shifts_narrow[0]
    )
    main = Norm(
        split_pre[:, half:], split_center[half:], split_rstd[half:], gains_narrow[1], shifts_narrow[1]
    )
    mainline = main.act().astype(jnp.bfloat16)
    inner = normed(dot(mainline, w_inner), gains_narrow[2], shifts_narrow[2])
    inner_act = inner.act().astype(jnp.bfloat16).reshape(height, width, half)
    rim = jnp.pad(inner_act, ((1, 1), (1, 1), (0, 0)))
    spatial_pre = lax.conv_general_dilated(
        rim[None],
        w_spatial,
        (1, 1),
        ((0, 0), (0, 0)),
        dimension_numbers=LAYOUT,
        preferred_element_type=jnp.float32,
    ).reshape(cells, half)
    spatial = normed(spatial_pre, gains_narrow[3], shifts_narrow[3])
    merged = (mainline.astype(jnp.float32) + spatial.act()).astype(jnp.bfloat16)
    trans = normed(dot(merged, w_trans), gains_narrow[4], shifts_narrow[4])
    joined = jnp.concatenate(
        [short.act().astype(jnp.bfloat16), trans.act().astype(jnp.bfloat16)], axis=1
    )
    unite = normed(dot(joined, w_unite), gains_wide[1], shifts_wide[1])
    out_image = (unite.act() * weight).astype(jnp.bfloat16).reshape(height, width, full)

    def own_rows(image, per_device):
        return [
            lax.dynamic_slice_in_dim(image, place * per_device, per_device, 0)
            for place in (here.place, here.place ^ 1)
        ]

    output = here.rows_of(*own_rows(out_image, height_dev))

    def share(values, grad):
        columns = grad.shape[1] // here.chips
        grad = lax.dynamic_slice_in_dim(grad, here.chip * columns, columns, 1)
        part = jnp.concatenate([dot_cells(v, grad) for v in values], axis=0)
        part = part.reshape(part.shape[0], 2, columns // 2)
        mine = lax.dynamic_index_in_dim(part, here.core, 1, keepdims=False)
        other = lax.dynamic_index_in_dim(part, 1 - here.core, 1, keepdims=False)
        return (mine + here.swap(other.astype(jnp.bfloat16)).astype(jnp.float32)).astype(
            jnp.bfloat16
        )

    unite_sums = here.group_sum(unite.incoming(grad_out.astype(jnp.float32) * weight))
    grad_unite_pre = unite.outgoing(unite_sums, weight, pixels)
    grad_joined = dot_back(grad_unite_pre, w_unite)
    pair_sums = here.group_sum(
        jnp.stack([short.incoming(grad_joined[:, :half]), trans.incoming(grad_joined[:, half:])])
    )
    short_sums, trans_sums = pair_sums[0], pair_sums[1]
    grad_short_pre = short.outgoing(short_sums, weight, pixels)
    grad_trans_pre = trans.outgoing(trans_sums, weight, pixels)
    grad_merged = dot_back(grad_trans_pre, w_trans)
    spatial_sums = here.group_sum(spatial.incoming(grad_merged))
    grad_spatial_pre = spatial.outgoing(spatial_sums, weight, pixels)
    grad_inner_act = lax.conv_general_dilated(
        grad_spatial_pre.reshape(1, height, width, half),
        flipped(w_spatial),
        (1, 1),
        ((1, 1), (1, 1)),
        dimension_numbers=LAYOUT,
        preferred_element_type=jnp.float32,
    ).reshape(cells, half)
    inner_sums = here.group_sum(inner.incoming(grad_inner_act))
    grad_inner_pre = inner.outgoing(inner_sums, weight, pixels)
    grad_mainline = grad_merged + dot_back(grad_inner_pre, w_inner)
    main_sums = here.group_sum(main.incoming(grad_mainline))
    grad_main_pre = main.outgoing(main_sums, weight, pixels)

    windows = [
        rim[i : i + height, j : j + width].reshape(cells, half) for i in range(3) for j in range(3)
    ]
    early = lax.psum(
        (
            share([sectioned], grad_short_pre),
            share([sectioned], grad_main_pre),
            share([mainline], grad_inner_pre),
            share(windows, grad_spatial_pre),
            share([merged], grad_trans_pre),
            share([joined], grad_unite_pre),
        ),
        "batch",
    )
    early = [e.astype(jnp.float32) for e in early]

    grad_sectioned = dot_back(grad_short_pre, w_short) + dot_back(grad_main_pre, w_main)
    down_sums = here.group_sum(down.incoming(grad_sectioned))
    grad_down_pre = down.outgoing(down_sums, weight, pixels)

    frame = jnp.pad(source, ((1, 0), (1, 0), (0, 0)))
    taps = [
        lax.slice(
            frame,
            (i, j, 0),
            (i + 2 * (height - 1) + 1, j + 2 * (width - 1) + 1, half),
            (2, 2, 1),
        ).reshape(cells, half)
        for i in range(3)
        for j in range(3)
    ]
    grad_w_down = lax.psum(share(taps, grad_down_pre), "batch").astype(jnp.float32)

    pair_rows = 2 * height_dev
    grad_image = jnp.pad(grad_down_pre.reshape(height, width, full), ((0, 1), (0, 0), (0, 0)))
    grad_block = lax.dynamic_slice_in_dim(grad_image, here.chip * pair_rows, pair_rows + 1, 0)
    widened = lax.conv_general_dilated(
        grad_block[None],
        flipped(w_down),
        (1, 1),
        ((1, 0), (1, 2)),
        lhs_dilation=(2, 2),
        dimension_numbers=LAYOUT,
        preferred_element_type=jnp.float32,
    )[0]
    mine = lax.dynamic_slice_in_dim(widened, here.core * pair_rows, pair_rows, 0)
    other = lax.dynamic_slice_in_dim(widened, (1 - here.core) * pair_rows, pair_rows, 0)
    grad_inputs = here.rows_of(mine, other)

    return (
        output,
        grad_inputs,
        grad_w_down.reshape(3, 3, half, -1),
        early[0],
        early[1],
        early[2],
        early[3].reshape(3, 3, half, -1),
        early[4],
        early[5],
        jnp.stack([down_sums[1], unite_sums[1]]),
        jnp.stack([short_sums[1], main_sums[1], inner_sums[1], spatial_sums[1], trans_sums[1]]),
        jnp.stack([down_sums[0], unite_sums[0]]),
        jnp.stack([short_sums[0], main_sums[0], inner_sums[0], spatial_sums[0], trans_sums[0]]),
    )


def solution(mesh):
    placed = (P("batch", "rows", None, None),) + (P(),) * 12 + (P("batch", "rows", None, None),)
    return jax.shard_map(
        on_device,
        mesh=mesh,
        in_specs=placed,
        out_specs=(
            P("batch", "rows", None, None),
            P("batch", "rows", None, None),
            P(None, None, None, "rows"),
            P(None, "rows"),
            P(None, "rows"),
            P(None, "rows"),
            P(None, None, None, "rows"),
            P(None, "rows"),
            P(None, "rows"),
            P(),
            P(),
            P(),
            P(),
        ),
        check_vma=False,
    )
```

```python
import functools

import jax
import jax.numpy as jnp
from jax import lax
from jax.experimental import pallas as pl
from jax.experimental.pallas import tpu as pltpu
from jax.sharding import PartitionSpec as P

EPSILON = 1e-05
FAR = 20.0
CHUNK = 32
COLS = 256
BF = jnp.bfloat16
F32 = jnp.float32


def mish(values):
    grown = jnp.exp(jnp.minimum(values, FAR))
    wide = grown * (grown + 2.0)
    return values * (wide / (wide + 2.0))


def mish_slope(values):
    grown = jnp.exp(jnp.minimum(values, FAR))
    wide = grown * (grown + 2.0)
    share = 1.0 / (wide + 2.0)
    return wide * share + 4.0 * values * (grown * (grown + 1.0) * share) * share


def tree_sum(parts):
    while len(parts) > 1:
        parts = [parts[i] + parts[i + 1] for i in range(0, len(parts), 2)]
    return parts[0]


def dot(a, b):
    return jnp.dot(a, b, preferred_element_type=F32)


def dot_back(a, b):
    return lax.dot_general(a, b, (((1,), (1,)), ((), ())), preferred_element_type=F32)


def dot_cells(a, b):
    return lax.dot_general(a, b, (((0,), (0,)), ((), ())), preferred_element_type=F32)


class Plane:
    def __init__(self):
        self.rows = lax.axis_size("rows")
        self.groups = lax.axis_size("batch")
        self.chips = self.rows // 2
        self.place = lax.axis_index("rows")
        self.core = self.place % 2
        self.chip = self.place // 2

    def swap(self, value):
        return lax.ppermute(value, "rows", [(i, i ^ 1) for i in range(self.rows)])

    def chip_hops(self, value):
        return [value] + [
            lax.ppermute(value, "rows", [(i, i ^ (2 * step)) for i in range(self.rows)])
            for step in range(1, self.chips)
        ]

    def plane_hops(self, value):
        return [value] + [
            lax.ppermute(value, "batch", [(i, i ^ step) for i in range(self.groups)])
            for step in range(1, self.groups)
        ]

    def by_core(self, mine, got):
        first = self.core == 0
        return jnp.where(first, mine, got), jnp.where(first, got, mine)

    def split(self, block, axis=0):
        mine = lax.dynamic_index_in_dim(block, self.core, axis, keepdims=False)
        other = lax.dynamic_index_in_dim(block, 1 - self.core, axis, keepdims=False)
        return mine, other

    def pieces(self, mine, other):
        return self.chip_hops(jnp.concatenate([mine, self.swap(other)], axis=0))

    def everywhere(self, pay):
        return self.plane_hops(jnp.concatenate([pay, self.swap(pay)], axis=0))


def rows_loop(total, body, carry=None, step=CHUNK):
    def turn(index, state):
        return body(pl.ds(pl.multiple_of(index * step, step), step), state)

    return lax.fori_loop(0, total // step, turn, carry)


def finish_moments(scal, refs, cols=slice(None)):
    pixels = scal[1]
    center = tree_sum([r[0:1, cols] + r[2:3, cols] for r in refs]) / pixels
    terms = []
    for k, r in enumerate(refs):
        ends = []
        for side in range(2):
            count, over = scal[2 + 4 * k + 2 * side], scal[3 + 4 * k + 2 * side]
            gap = r[2 * side : 2 * side + 1, cols] * over - center
            ends.append(gap * gap * count)
        terms.append((r[1:2, cols] + r[3:4, cols]) + (ends[0] + ends[1]))
    return center, lax.rsqrt(tree_sum(terms) / pixels + EPSILON)


def finish_sums(refs, cols=slice(None)):
    return (
        tree_sum([r[0:1, cols] + r[2:3, cols] for r in refs]),
        tree_sum([r[1:2, cols] + r[3:4, cols] for r in refs]),
    )


def put_moments(values, pay, cols, weight):
    total = jnp.sum(values, axis=0, keepdims=True)
    off = values - total * (1.0 / values.shape[0])
    pay[0:1, cols] = total * weight
    pay[1:2, cols] = jnp.sum(off * off, axis=0, keepdims=True) * weight


def project(left, weights, pre, pay, weight, add=None):
    for start in range(0, pre.shape[1], COLS):
        cols = slice(start, start + COLS)
        out = dot(left[...], weights[:, cols])
        if add is not None:
            out = out + add[:, cols]
        pre[:, cols] = out
        put_moments(out, pay, cols, weight)


def fold(values):
    return jnp.sum(values.reshape(-1, 8, values.shape[-1]), axis=0)


def push(grad_of, pre, center, rstd, gain, offset, pushed, pay):
    def body(rows, sums):
        unit = (pre[rows, :].astype(F32) - center) * rstd
        out = grad_of(rows) * mish_slope(unit * gain + offset)
        pushed[rows, :] = out
        return sums[0] + fold(out), sums[1] + fold(out * unit)

    zero = jnp.zeros((8, pre.shape[1]), F32)
    first, second = rows_loop(pre.shape[0], body, (zero, zero), 16)
    pay[0:1, :] = jnp.sum(first, axis=0, keepdims=True)
    pay[1:2, :] = jnp.sum(second, axis=0, keepdims=True)


def settle(scal, refs, pushed, pre, coef, gain, out, sums):
    first, second = finish_sums(refs)
    sums[0:1, :] = first
    sums[1:2, :] = second
    over = 1.0 / scal[1]
    center, rstd = coef[0:1, :], coef[1:2, :]
    scale = gain * rstd * scal[0]
    level, tilt = first * over, second * over * rstd

    def body(rows, _):
        x = pre[rows, :].astype(F32) - center
        out[rows, :] = (scale * (pushed[rows, :] - level - x * tilt)).astype(BF)

    rows_loop(pre.shape[0], body)


def own_taps(x, w, out):
    slots = x.shape[0]
    for tap in (1, 2):
        blocks = []
        for slot in range(slots):
            both = x[slot, tap - 1]
            blocks.append(shifted_row(both))
        left = jnp.concatenate(blocks, axis=0)
        part = dot(left, w[tap - 1])
        out[...] = part if tap == 1 else out[...] + part


def shifted_row(both):
    half = both.shape[1] // 2
    odd = both[:, half:].astype(F32)
    first = lax.broadcasted_iota(jnp.int32, odd.shape, 0) == 0
    before = jnp.where(first, 0.0, pltpu.roll(odd, 1, 0)).astype(BF)
    return jnp.concatenate([before, both], axis=1)


def borrowed_taps(scal, x, w, part, rows, pay):
    slots, cells = x.shape[0], x.shape[1]
    left = jnp.concatenate([shifted_row(x[slot]) for slot in range(slots)], axis=0)
    out = dot(left, w[...]) + part[...]
    rows[...] = out.astype(BF)
    total = sum(
        jnp.sum(out[slot * cells : (slot + 1) * cells], axis=0, keepdims=True) * scal[slot]
        for slot in range(slots)
    )
    mean = total * scal[slots]
    spread = 0.0
    for slot in range(slots):
        off = out[slot * cells : (slot + 1) * cells] - mean
        spread += jnp.sum(off * off, axis=0, keepdims=True) * scal[slot]
    pay[0:1, :] = total
    pay[1:2, :] = spread


def main_kernel(pieces, scal, spots, got, counts, over, gains, shifts, *rest):
    parts = rest[:pieces]
    w_main, down_pre, sectioned, main_pre, pay, coef = rest[pieces:]
    pixels = scal[1]
    firsts, seconds = got[:, 0, :], got[:, 1, :]
    center = jnp.sum(firsts, axis=0, keepdims=True) / pixels
    gap = firsts * over[...] - center
    total = jnp.sum(seconds + gap * gap * counts[...], axis=0, keepdims=True)
    rstd = lax.rsqrt(total / pixels + EPSILON)
    coef[0:1, :] = center
    coef[1:2, :] = rstd
    scale, offset = rstd * gains[0:1, :], shifts[0:1, :]
    for k, part in enumerate(parts):
        width = part.shape[0] // 2
        for side in range(2):
            start = spots[2 * k + side] * width

            def body(index, _, part=part, side=side, start=start, width=width):
                src = pl.ds(pl.multiple_of(side * width + index * CHUNK, CHUNK), CHUNK)
                dst = pl.ds(pl.multiple_of(start + index * CHUNK, CHUNK), CHUNK)
                x = part[src, :]
                down_pre[dst, :] = x
                value = (x.astype(F32) - center) * scale + offset
                sectioned[dst, :] = mish(value).astype(BF)

            lax.fori_loop(0, width // CHUNK, body, None)
    project(sectioned, w_main, main_pre, pay, scal[0])


def short_kernel(scal, sectioned, w_short, short_pre, pay):
    project(sectioned, w_short, short_pre, pay, scal[0])


def inner_kernel(groups, scal, *rest):
    refs = rest[:groups]
    pre, gains, shifts, w_inner, mainline, inner_pre, pay, coef = rest[groups:]
    center, rstd = finish_moments(scal, refs)
    coef[0:1, :] = center
    coef[1:2, :] = rstd
    scale, offset = rstd * gains[1:2, :], shifts[1:2, :]

    def body(rows, _):
        mainline[rows, :] = mish((pre[rows, :] - center) * scale + offset).astype(BF)

    rows_loop(pre.shape[0], body)
    project(mainline, w_inner, inner_pre, pay, scal[0])


def three_shifts(values, rim, start, forward):
    width, half = values.shape
    place = lax.broadcasted_iota(jnp.int32, values.shape, 0)
    before = jnp.where(place == 0, 0.0, pltpu.roll(values, 1, 0)).astype(BF)
    after = jnp.where(place == width - 1, 0.0, pltpu.roll(values, width - 1, 0)).astype(BF)
    sides = (before, after) if forward else (after, before)
    rows = pl.ds(start, width)
    rim[rows, 0:half] = sides[0]
    rim[rows, half : 2 * half] = values.astype(BF)
    rim[rows, 2 * half : 3 * half] = sides[1]


def spatial_kernel(groups, width, scal, *rest):
    refs = rest[:groups]
    pre, gains, shifts, w_spatial, rim, spatial_pre, pay, coef = rest[groups:]
    cells, half = pre.shape
    center, rstd = finish_moments(scal, refs)
    coef[0:1, :] = center
    coef[1:2, :] = rstd
    scale, offset = rstd * gains[2:3, :], shifts[2:3, :]
    blank = jnp.zeros((width, 3 * half), BF)
    rim[0:width, :] = blank
    rim[width + cells :, :] = blank

    def body(index, _):
        start = pl.multiple_of(index * width, width)
        act = mish((pre[pl.ds(start, width), :] - center) * scale + offset)
        three_shifts(act, rim, pl.multiple_of(start + width, width), True)

    lax.fori_loop(0, cells // width, body, None)
    for begin in range(0, half, COLS):
        cols = slice(begin, begin + COLS)
        out = sum(
            dot(
                rim[i * width : i * width + cells, :],
                w_spatial[i * 3 * half : (i + 1) * 3 * half, cols],
            )
            for i in range(3)
        )
        spatial_pre[:, cols] = out
        put_moments(out, pay, cols, scal[0])


def trans_kernel(groups, scal, *rest):
    refs = rest[:groups]
    pre, mainline, gains, shifts, w_trans, merged, trans_pre, pay, coef = rest[groups:]
    center, rstd = finish_moments(scal, refs)
    coef[0:1, :] = center
    coef[1:2, :] = rstd
    scale, offset = rstd * gains[3:4, :], shifts[3:4, :]

    def body(rows, _):
        act = mish((pre[rows, :] - center) * scale + offset)
        merged[rows, :] = (mainline[rows, :].astype(F32) + act).astype(BF)

    rows_loop(pre.shape[0], body)
    project(merged, w_trans, trans_pre, pay, scal[0])


def shortcut_kernel(groups, scal, *rest):
    refs = rest[:groups]
    pre, gains, shifts, w_unite, shortcut, part, coef = rest[groups:]
    half = pre.shape[1]
    center, rstd = finish_moments(scal, refs)
    coef[0:1, :] = center
    coef[1:2, :] = rstd
    scale, offset = rstd * gains[0:1, :], shifts[0:1, :]

    def body(rows, _):
        shortcut[rows, :] = mish((pre[rows, :] - center) * scale + offset).astype(BF)

    rows_loop(pre.shape[0], body)
    for start in range(0, part.shape[1], COLS):
        cols = slice(start, start + COLS)
        part[:, cols] = dot(shortcut[...], w_unite[0:half, cols])


def unite_kernel(groups, scal, *rest):
    refs = rest[:groups]
    pre, part, gains, shifts, w_unite, transition, unite_pre, pay, coef = rest[groups:]
    half = pre.shape[1]
    center, rstd = finish_moments(scal, refs)
    coef[0:1, :] = center
    coef[1:2, :] = rstd
    scale, offset = rstd * gains[4:5, :], shifts[4:5, :]

    def body(rows, _):
        transition[rows, :] = mish((pre[rows, :] - center) * scale + offset).astype(BF)

    rows_loop(pre.shape[0], body)
    project(transition, w_unite.at[half:, :], unite_pre, pay, scal[0], part)


def turn_kernel(groups, pieces, scal, spots, *rest):
    refs = rest[:groups]
    parts = rest[groups : groups + pieces]
    pre, gains, shifts, pushed, output, pay, coef = rest[groups + pieces :]
    center, rstd = finish_moments(scal, refs)
    coef[0:1, :] = center
    coef[1:2, :] = rstd
    gain, offset, weight = gains[1:2, :], shifts[1:2, :], scal[0]
    sums = (jnp.zeros((8, pre.shape[1]), F32),) * 2
    for k, part in enumerate(parts):
        width = part.shape[0] // 2
        for side in range(2):
            start = spots[2 * k + side] * width

            def body(index, sums, part=part, side=side, start=start, width=width):
                src = pl.ds(pl.multiple_of(side * width + index * 16, 16), 16)
                dst = pl.ds(pl.multiple_of(start + index * 16, 16), 16)
                unit = (pre[dst, :] - center) * rstd
                value = unit * gain + offset
                grown = jnp.exp(jnp.minimum(value, FAR))
                wide = grown * (grown + 2.0)
                share = 1.0 / (wide + 2.0)
                level = wide * share
                output[dst, :] = (value * level * weight).astype(BF)
                slope = level + 4.0 * value * (grown * (grown + 1.0) * share) * share
                out = part[src, :].astype(F32) * weight * slope
                pushed[dst, :] = out
                return sums[0] + fold(out), sums[1] + fold(out * unit)

            sums = lax.fori_loop(0, width // 16, body, sums)
    pay[0:1, :] = jnp.sum(sums[0], axis=0, keepdims=True)
    pay[1:2, :] = jnp.sum(sums[1], axis=0, keepdims=True)


def back_trans_kernel(groups, scal, *rest):
    refs = rest[:groups]
    (
        unite_pushed, unite_pre, unite_coef, gains_wide, w_unite, trans_pre, trans_coef, gains, shifts,
        grad_unite, sums, pushed, pay, scratch,
    ) = rest[groups:]
    half = trans_pre.shape[1]
    settle(scal, refs, unite_pushed, unite_pre, unite_coef, gains_wide[1:2, :], grad_unite, sums)
    for start in range(0, half, COLS):
        scratch[:, start : start + COLS] = dot_back(
            grad_unite[...], w_unite[half + start : half + start + COLS, :]
        )
    push(
        lambda rows: scratch[rows, :],
        trans_pre, trans_coef[0:1, :], trans_coef[1:2, :], gains[4:5, :], shifts[4:5, :],
        pushed, pay,
    )


def back_short_kernel(grad_unite, w_unite, pre, coef, gains, shifts, pushed, pay, scratch):
    half = pre.shape[1]
    for start in range(0, half, COLS):
        scratch[:, start : start + COLS] = dot_back(
            grad_unite[...], w_unite[start : start + COLS, :]
        )
    push(
        lambda rows: scratch[rows, :],
        pre, coef[0:1, :], coef[1:2, :], gains[0:1, :], shifts[0:1, :], pushed, pay,
    )


def back_spatial_kernel(groups, scal, *rest):
    refs = rest[:groups]
    (
        trans_pushed, trans_pre, trans_coef, w_trans, spatial_pre, spatial_coef, gains, shifts,
        grad_trans, sums, grad_merged, pushed, pay,
    ) = rest[groups:]
    half = trans_pre.shape[1]
    settle(scal, refs, trans_pushed, trans_pre, trans_coef, gains[4:5, :], grad_trans, sums)
    for start in range(0, half, COLS):
        grad_merged[:, start : start + COLS] = dot_back(
            grad_trans[...], w_trans[start : start + COLS, :]
        )
    push(
        lambda rows: grad_merged[rows, :],
        spatial_pre, spatial_coef[0:1, :], spatial_coef[1:2, :], gains[3:4, :], shifts[3:4, :],
        pushed, pay,
    )


def back_inner_kernel(groups, width, scal, *rest):
    refs = rest[:groups]
    (
        spatial_pushed, spatial_pre, spatial_coef, w_spatial, inner_pre, inner_coef, gains, shifts,
        grad_spatial, sums, pushed, pay, rim, scratch,
    ) = rest[groups:]
    cells, half = spatial_pre.shape
    settle(scal, refs, spatial_pushed, spatial_pre, spatial_coef, gains[3:4, :], grad_spatial, sums)
    blank = jnp.zeros((width, 3 * half), BF)
    rim[0:width, :] = blank
    rim[width + cells :, :] = blank

    def body(index, _):
        start = pl.multiple_of(index * width, width)
        values = grad_spatial[pl.ds(start, width), :].astype(F32)
        three_shifts(values, rim, pl.multiple_of(start + width, width), False)

    lax.fori_loop(0, cells // width, body, None)
    for start in range(0, half, COLS):
        scratch[:, start : start + COLS] = sum(
            dot_back(
                rim[(2 - i) * width : (2 - i) * width + cells, j * half : (j + 1) * half],
                w_spatial[(3 * i + j) * half + start : (3 * i + j) * half + start + COLS, :],
            )
            for i in range(3)
            for j in range(3)
        )
    push(
        lambda rows: scratch[rows, :],
        inner_pre, inner_coef[0:1, :], inner_coef[1:2, :], gains[2:3, :], shifts[2:3, :],
        pushed, pay,
    )


def back_main_kernel(groups, scal, *rest):
    refs = rest[:groups]
    (
        inner_pushed, inner_pre, inner_coef, w_inner, grad_merged, main_pre, main_coef, gains, shifts,
        grad_inner, sums, pushed, pay, scratch,
    ) = rest[groups:]
    half = inner_pre.shape[1]
    settle(scal, refs, inner_pushed, inner_pre, inner_coef, gains[2:3, :], grad_inner, sums)
    for start in range(0, half, COLS):
        cols = slice(start, start + COLS)
        scratch[:, cols] = grad_merged[:, cols] + dot_back(grad_inner[...], w_inner[cols, :])
    push(
        lambda rows: scratch[rows, :],
        main_pre, main_coef[0:1, :], main_coef[1:2, :], gains[1:2, :], shifts[1:2, :],
        pushed, pay,
    )


def settle_short_kernel(groups, scal, *rest):
    refs = rest[:groups]
    pushed, pre, coef, gains, w_short, grad_short, sums, part = rest[groups:]
    settle(scal, refs, pushed, pre, coef, gains[0:1, :], grad_short, sums)
    for start in range(0, part.shape[1], COLS):
        part[:, start : start + COLS] = dot_back(grad_short[...], w_short[start : start + COLS, :])


def back_down_kernel(groups, scal, *rest):
    refs = rest[:groups]
    (
        main_pushed, main_pre, main_coef, w_main, part, down_pre, down_coef, gains, gains_wide, shifts_wide,
        grad_main, sums, pushed, pay, scratch,
    ) = rest[groups:]
    settle(scal, refs, main_pushed, main_pre, main_coef, gains[1:2, :], grad_main, sums)
    for start in range(0, part.shape[1], COLS):
        cols = slice(start, start + COLS)
        scratch[:, cols] = part[:, cols] + dot_back(grad_main[...], w_main[cols, :])
    push(
        lambda rows: scratch[rows, :],
        down_pre, down_coef[0:1, :], down_coef[1:2, :], gains_wide[0:1, :], shifts_wide[0:1, :],
        pushed, pay,
    )


def settle_down_kernel(groups, scal, *rest):
    refs = rest[:groups]
    pushed, pre, coef, gains_wide, grad_down, sums = rest[groups:]
    settle(scal, refs, pushed, pre, coef, gains_wide[0:1, :], grad_down, sums)


SMEM = pl.BlockSpec(memory_space=pltpu.SMEM)
VMEM = pl.BlockSpec(memory_space=pltpu.VMEM)


def shape(dims, dtype=F32):
    return jax.ShapeDtypeStruct(dims, dtype)


def nbytes(dims, dtype):
    count = 1
    for d in dims:
        count *= d
    return count * jnp.dtype(dtype).itemsize


def call(kernel, name, scalars, arrays, outs, flops, scratch=()):
    moved = sum(nbytes(a.shape, a.dtype) for a in (*arrays, *outs))
    held = moved + sum(nbytes(s.shape, s.dtype) for s in scratch)
    return pl.pallas_call(
        kernel,
        name=name,
        out_shape=tuple(outs),
        in_specs=[SMEM] * len(scalars) + [VMEM] * len(arrays),
        out_specs=tuple([VMEM] * len(outs)),
        scratch_shapes=tuple(pltpu.VMEM(s.shape, s.dtype) for s in scratch),
        compiler_params=pltpu.CompilerParams(vmem_limit_bytes=held + (10 << 20)),
        cost_estimate=pl.CostEstimate(flops=flops, bytes_accessed=moved, transcendentals=0),
    )(*scalars, *arrays)


def first_conv(scal, view, above, w_down):
    slots, _, cells, both = view.shape
    half = both // 2
    full = w_down.shape[-1]
    taps = w_down.reshape(3, 3 * half, full)
    wide = 256
    part = pl.pallas_call(
        own_taps,
        name="own_taps",
        grid=(full // wide,),
        out_shape=shape((slots * cells, full)),
        in_specs=[
            pl.BlockSpec((slots, 2, cells, both), lambda n: (0, 0, 0, 0)),
            pl.BlockSpec((pl.Element(2), pl.Element(3 * half), pl.Element(wide)), lambda n: (1, 0, n * wide)),
        ],
        out_specs=pl.BlockSpec((slots * cells, wide), lambda n: (0, n)),
        compiler_params=pltpu.CompilerParams(vmem_limit_bytes=24 << 20),
        cost_estimate=pl.CostEstimate(
            flops=4 * slots * cells * 3 * half * full, bytes_accessed=2 * 2 * 3 * half * full, transcendentals=0
        ),
    )(view, taps)
    rows, pay = pl.pallas_call(
        borrowed_taps,
        name="borrowed_taps",
        grid=(full // wide,),
        out_shape=(shape((slots * cells, full), BF), shape((2, full))),
        in_specs=[
            SMEM,
            pl.BlockSpec((slots, cells, both), lambda n: (0, 0, 0)),
            pl.BlockSpec((None, 3 * half, wide), lambda n: (0, 0, n)),
            pl.BlockSpec((slots * cells, wide), lambda n: (0, n)),
        ],
        out_specs=(
            pl.BlockSpec((slots * cells, wide), lambda n: (0, n)),
            pl.BlockSpec((2, wide), lambda n: (0, n)),
        ),
        compiler_params=pltpu.CompilerParams(vmem_limit_bytes=24 << 20),
        cost_estimate=pl.CostEstimate(
            flops=2 * slots * cells * 3 * half * full, bytes_accessed=2 * 3 * half * full, transcendentals=0
        ),
    )(scal, above, taps, part)
    return rows.reshape(slots, cells, full), pay


def flipped(kernel):
    return jnp.swapaxes(jnp.flip(kernel, (0, 1)), 2, 3)


def on_device(
    inputs,
    image_counts,
    w_down,
    w_short,
    w_main,
    w_inner,
    w_spatial,
    w_trans,
    w_unite,
    gains_wide,
    gains_narrow,
    shifts_wide,
    shifts_narrow,
    grad_output,
):
    half = w_short.shape[1]
    full = 2 * half
    slots, height_dev, width, _ = grad_output.shape
    here = Plane()
    groups, chips = here.groups, here.chips
    height = here.rows * height_dev
    cells = height * width
    batch = lax.axis_index("batch")
    counts = image_counts.astype(F32)
    own_count = image_counts[batch]
    pixels = jnp.sum(counts) * cells
    weight = (here.core < own_count).astype(F32)

    scal = [weight, pixels]
    for step in range(groups):
        plane = batch ^ step
        for slot in (here.core, 1 - here.core):
            count = (slot < image_counts[plane]).astype(F32) * cells
            scal += [count, 1.0 / jnp.maximum(count, 1.0)]
    scal = jnp.stack(scal)
    spots = jnp.stack(
        [2 * (here.chip ^ step) + (here.core ^ side) for step in range(chips) for side in range(2)]
    ).astype(jnp.int32)
    slot_scal = jnp.concatenate(
        [
            (jnp.arange(slots) < own_count).astype(F32),
            (1.0 / (own_count.astype(F32) * height_dev * width))[None],
        ]
    )
    device_counts = jnp.tile(counts * (height_dev * width), here.rows).reshape(-1, 1)

    view = inputs.reshape(slots, 2, width, 2 * half)
    below = [(i, i + 1) for i in range(here.rows - 1)]
    above = lax.ppermute(view[:, 1], "rows", below)
    down_rows, sums = first_conv(slot_scal, view, above, w_down)
    devices = here.rows * groups
    gathered = lax.all_to_all(
        jnp.broadcast_to(sums[None], (devices,) + sums.shape), ("rows", "batch"), 0, 0, tiled=True
    )
    down_pieces = here.pieces(*here.split(down_rows))
    grad_pieces = here.pieces(*here.split(grad_output.reshape(slots, width, full)))
    down_pre, sectioned, main_pre, main_pay, down_coef = call(
        functools.partial(main_kernel, chips),
        "main",
        [scal, spots],
        [gathered, device_counts, 1.0 / device_counts, gains_wide, shifts_wide, *down_pieces, w_main],
        [
            shape((cells, full), BF), shape((cells, full), BF), shape((cells, half)),
            shape((2, half)), shape((2, full)),
        ],
        2 * cells * full * half,
    )
    narrow = [gains_narrow, shifts_narrow]

    main_all = here.everywhere(main_pay)
    short_pre, short_pay = call(
        short_kernel,
        "short",
        [scal],
        [sectioned, w_short],
        [shape((cells, half)), shape((2, half))],
        2 * cells * full * half,
    )
    mainline, inner_pre, inner_pay, main_coef = call(
        functools.partial(inner_kernel, groups),
        "inner",
        [scal],
        [*main_all, main_pre, *narrow, w_inner],
        [shape((cells, half), BF), shape((cells, half)), shape((2, half)), shape((2, half))],
        2 * cells * half * half,
    )
    inner_all = here.everywhere(inner_pay)
    rim, spatial_pre, spatial_pay, inner_coef = call(
        functools.partial(spatial_kernel, groups, width),
        "spatial",
        [scal],
        [*inner_all, inner_pre, *narrow, w_spatial.reshape(9 * half, half)],
        [
            shape((cells + 2 * width, 3 * half), BF), shape((cells, half)),
            shape((2, half)), shape((2, half)),
        ],
        18 * cells * half * half,
    )
    both_all = here.everywhere(jnp.concatenate([spatial_pay, short_pay], axis=1))
    spatial_all = [b[:, :half] for b in both_all]
    short_all = [b[:, half:] for b in both_all]
    merged, trans_pre, trans_pay, spatial_coef = call(
        functools.partial(trans_kernel, groups),
        "trans",
        [scal],
        [*spatial_all, spatial_pre, mainline, *narrow, w_trans],
        [shape((cells, half), BF), shape((cells, half)), shape((2, half)), shape((2, half))],
        2 * cells * half * half,
    )
    trans_all = here.everywhere(trans_pay)
    shortcut, unite_part, short_coef = call(
        functools.partial(shortcut_kernel, groups),
        "shortcut",
        [scal],
        [*short_all, short_pre, *narrow, w_unite],
        [shape((cells, half), BF), shape((cells, full)), shape((2, half))],
        2 * cells * half * full,
    )
    transition, unite_pre, unite_pay, trans_coef = call(
        functools.partial(unite_kernel, groups),
        "unite",
        [scal],
        [*trans_all, trans_pre, unite_part, *narrow, w_unite],
        [shape((cells, half), BF), shape((cells, full)), shape((2, full)), shape((2, half))],
        2 * cells * half * full,
    )
    unite_all = here.everywhere(unite_pay)
    unite_pushed, out_image, unite_pay, unite_coef = call(
        functools.partial(turn_kernel, groups, chips),
        "turn",
        [scal, spots],
        [*unite_all, *grad_pieces, unite_pre, gains_wide, shifts_wide],
        [shape((cells, full)), shape((cells, full), BF), shape((2, full)), shape((2, full))],
        40 * cells * full,
    )

    def own_rows(image, per_device):
        return [
            lax.dynamic_slice_in_dim(image, place * per_device, per_device, 0)
            for place in (here.place, here.place ^ 1)
        ]

    mine, other = own_rows(out_image, height_dev * width)
    output = jnp.stack(here.by_core(mine, here.swap(other))).reshape(grad_output.shape)

    unite_all = here.everywhere(unite_pay)
    grad_unite_pre, unite_sums, trans_pushed, trans_pay = call(
        functools.partial(back_trans_kernel, groups),
        "back_trans",
        [scal],
        [*unite_all, unite_pushed, unite_pre, unite_coef, gains_wide, w_unite, trans_pre, trans_coef, *narrow],
        [shape((cells, full), BF), shape((2, full)), shape((cells, half)), shape((2, half))],
        2 * cells * half * full,
        [shape((cells, half))],
    )
    trans_all = here.everywhere(trans_pay)
    short_pushed, short_pay = call(
        back_short_kernel,
        "back_short",
        [],
        [grad_unite_pre, w_unite, short_pre, short_coef, *narrow],
        [shape((cells, half)), shape((2, half))],
        2 * cells * half * full,
        [shape((cells, half))],
    )
    grad_trans_pre, trans_sums, grad_merged, spatial_pushed, spatial_pay = call(
        functools.partial(back_spatial_kernel, groups),
        "back_spatial",
        [scal],
        [*trans_all, trans_pushed, trans_pre, trans_coef, w_trans, spatial_pre, spatial_coef, *narrow],
        [
            shape((cells, half), BF), shape((2, half)), shape((cells, half)), shape((cells, half)),
            shape((2, half)),
        ],
        2 * cells * half * half,
    )
    both_all = here.everywhere(jnp.concatenate([spatial_pay, short_pay], axis=1))
    spatial_all = [b[:, :half] for b in both_all]
    short_all = [b[:, half:] for b in both_all]
    grad_spatial_pre, spatial_sums, inner_pushed, inner_pay = call(
        functools.partial(back_inner_kernel, groups, width),
        "back_inner",
        [scal],
        [
            *spatial_all, spatial_pushed, spatial_pre, spatial_coef, w_spatial.reshape(9 * half, half),
            inner_pre, inner_coef, *narrow,
        ],
        [shape((cells, half), BF), shape((2, half)), shape((cells, half)), shape((2, half))],
        18 * cells * half * half,
        [shape((cells + 2 * width, 3 * half), BF), shape((cells, half))],
    )
    inner_all = here.everywhere(inner_pay)
    grad_short_pre, short_sums, sectioned_part = call(
        functools.partial(settle_short_kernel, groups),
        "settle_short",
        [scal],
        [*short_all, short_pushed, short_pre, short_coef, gains_narrow, w_short],
        [shape((cells, half), BF), shape((2, half)), shape((cells, full))],
        2 * cells * half * full,
    )
    grad_inner_pre, inner_sums, main_pushed, main_pay = call(
        functools.partial(back_main_kernel, groups),
        "back_main",
        [scal],
        [*inner_all, inner_pushed, inner_pre, inner_coef, w_inner, grad_merged, main_pre, main_coef, *narrow],
        [shape((cells, half), BF), shape((2, half)), shape((cells, half)), shape((2, half))],
        2 * cells * half * half,
        [shape((cells, half))],
    )
    main_all = here.everywhere(main_pay)
    grad_main_pre, main_sums, down_pushed, down_pay = call(
        functools.partial(back_down_kernel, groups),
        "back_down",
        [scal],
        [
            *main_all, main_pushed, main_pre, main_coef, w_main, sectioned_part, down_pre, down_coef,
            gains_narrow, gains_wide, shifts_wide,
        ],
        [shape((cells, half), BF), shape((2, half)), shape((cells, full)), shape((2, full))],
        2 * cells * half * full,
        [shape((cells, full))],
    )
    down_all = here.everywhere(down_pay)
    grad_down_pre, down_sums = call(
        functools.partial(settle_down_kernel, groups),
        "settle_down",
        [scal],
        [*down_all, down_pushed, down_pre, down_coef, gains_wide],
        [shape((cells, full), BF), shape((2, full))],
        10 * cells * full,
    )

    def share(values, grad):
        columns = grad.shape[1] // chips
        grad = lax.dynamic_slice_in_dim(grad, here.chip * columns, columns, 1)
        part = jnp.concatenate([dot_cells(v, grad) for v in values], axis=0)
        mine, other = here.split(part.reshape(part.shape[0], 2, columns // 2), 1)
        return (mine + here.swap(other.astype(BF)).astype(F32)).astype(BF)

    windows = [rim[i * width : i * width + cells] for i in range(3)]
    early = lax.psum(
        (
            share([sectioned], grad_short_pre),
            share([sectioned], grad_main_pre),
            share([mainline], grad_inner_pre),
            share(windows, grad_spatial_pre),
            share([merged], grad_trans_pre),
            jnp.concatenate([share([shortcut], grad_unite_pre), share([transition], grad_unite_pre)]),
        ),
        "batch",
    )
    early = [e.astype(F32) for e in early]

    mine, other = here.split(view)
    got = here.chip_hops(jnp.stack([mine, here.swap(other)], axis=1))
    source = jnp.zeros((2, here.rows, width, full), BF)
    for step, piece in enumerate(got):
        for side in range(2):
            source = lax.dynamic_update_slice_in_dim(
                source, piece[:, side : side + 1], spots[2 * step + side], 1
            )
    grad_map = grad_down_pre.reshape(height, width, full)
    columns = full // chips
    grad_cut = lax.dynamic_slice_in_dim(grad_map, here.chip * columns, columns, 2)
    ahead = jnp.pad(grad_cut[:, 1:], ((0, 0), (0, 1), (0, 0)))
    upper = jnp.pad(grad_cut[1:], ((0, 1), (0, 0), (0, 0)))
    both_ahead = jnp.pad(ahead[1:], ((0, 1), (0, 0), (0, 0)))
    even_rows = source[0].reshape(cells, full)
    odd_rows = source[1].reshape(cells, full)

    def taps_of(rows, here_grad, ahead_grad):
        plain = dot_cells(rows, here_grad.reshape(cells, columns))
        before = dot_cells(rows[:, half:], ahead_grad.reshape(cells, columns))
        return [before, plain]

    part = jnp.concatenate(
        taps_of(odd_rows, upper, both_ahead)
        + taps_of(even_rows, grad_cut, ahead)
        + taps_of(odd_rows, grad_cut, ahead),
        axis=0,
    )
    mine, other = here.split(part.reshape(9 * half, 2, columns // 2), 1)
    part = (mine + here.swap(other.astype(BF)).astype(F32)).astype(BF)
    grad_w_down = lax.psum(part, "batch").astype(F32)

    pair_rows = 2 * height_dev
    grad_image = jnp.pad(grad_map, ((0, 1), (0, 0), (0, 0)))
    grad_block = lax.dynamic_slice_in_dim(grad_image, here.chip * pair_rows, pair_rows + 1, 0)
    widened = lax.conv_general_dilated(
        grad_block[None],
        flipped(w_down),
        (1, 1),
        ((1, 0), (1, 2)),
        lhs_dilation=(2, 2),
        dimension_numbers=("NHWC", "HWIO", "NHWC"),
        preferred_element_type=F32,
    )[0]
    mine = lax.dynamic_slice_in_dim(widened, here.core * pair_rows, pair_rows, 0)
    other = lax.dynamic_slice_in_dim(widened, (1 - here.core) * pair_rows, pair_rows, 0)
    grad_inputs = jnp.stack(here.by_core(mine, here.swap(other)))

    narrow_sums = [short_sums, main_sums, inner_sums, spatial_sums, trans_sums]
    return (
        output,
        grad_inputs,
        grad_w_down.reshape(3, 3, half, -1),
        early[0],
        early[1],
        early[2],
        early[3].reshape(3, 3, half, -1),
        early[4],
        early[5],
        jnp.stack([down_sums[1], unite_sums[1]]),
        jnp.stack([s[1] for s in narrow_sums]),
        jnp.stack([down_sums[0], unite_sums[0]]),
        jnp.stack([s[0] for s in narrow_sums]),
    )


def solution(mesh):
    placed = (P("batch", "rows", None, None),) + (P(),) * 12 + (P("batch", "rows", None, None),)
    return jax.shard_map(
        on_device,
        mesh=mesh,
        in_specs=placed,
        out_specs=(
            P("batch", "rows", None, None),
            P("batch", "rows", None, None),
            P(None, None, None, "rows"),
            P(None, "rows"),
            P(None, "rows"),
            P(None, "rows"),
            P(None, None, None, "rows"),
            P(None, "rows"),
            P(None, "rows"),
            P(),
            P(),
            P(),
            P(),
        ),
        check_vma=False,
    )
```

```python
import functools

import jax
import jax.numpy as jnp
from jax import lax
from jax.experimental import pallas as pl
from jax.experimental.pallas import tpu as pltpu
from jax.sharding import PartitionSpec as P

EPSILON = 1e-05
FAR = 20.0
CHUNK = 32
COLS = 256
BF = jnp.bfloat16
F32 = jnp.float32


def mish(values):
    grown = jnp.exp(jnp.minimum(values, FAR))
    wide = grown * (grown + 2.0)
    return values * (wide / (wide + 2.0))


def mish_slope(values):
    grown = jnp.exp(jnp.minimum(values, FAR))
    wide = grown * (grown + 2.0)
    share = 1.0 / (wide + 2.0)
    return wide * share + 4.0 * values * (grown * (grown + 1.0) * share) * share


def after(value, *others):
    return lax.optimization_barrier((value,) + others)[0]


def tree_sum(parts):
    while len(parts) > 1:
        parts = [parts[i] + parts[i + 1] for i in range(0, len(parts), 2)]
    return parts[0]


def dot(a, b):
    return jnp.dot(a, b, preferred_element_type=F32)


def dot_back(a, b):
    return lax.dot_general(a, b, (((1,), (1,)), ((), ())), preferred_element_type=F32)


def dot_cells(a, b):
    return lax.dot_general(a, b, (((0,), (0,)), ((), ())), preferred_element_type=F32)


class Plane:
    def __init__(self):
        self.rows = lax.axis_size("rows")
        self.groups = lax.axis_size("batch")
        self.chips = self.rows // 2
        self.place = lax.axis_index("rows")
        self.core = self.place % 2
        self.chip = self.place // 2

    def swap(self, value):
        return lax.ppermute(value, "rows", [(i, i ^ 1) for i in range(self.rows)])

    def chip_hops(self, value):
        return [value] + [
            lax.ppermute(value, "rows", [(i, i ^ (2 * step)) for i in range(self.rows)])
            for step in range(1, self.chips)
        ]

    def two_ways(self, first, second):
        hop = lambda value, step: lax.ppermute(
            value, "rows", [(i, i ^ (2 * step)) for i in range(self.rows)]
        )
        first_near, second_near = hop(first, 1), hop(second, 2)
        return first_near, second_near, lambda: (
            [first, first_near, hop(first, 2), hop(first_near, 2)],
            [second, hop(second, 1), second_near, hop(second_near, 1)],
        )

    def plane_hops(self, value):
        return [value] + [
            lax.ppermute(value, "batch", [(i, i ^ step) for i in range(self.groups)])
            for step in range(1, self.groups)
        ]

    def by_core(self, mine, got):
        first = self.core == 0
        return jnp.where(first, mine, got), jnp.where(first, got, mine)

    def split(self, block, axis=0):
        mine = lax.dynamic_index_in_dim(block, self.core, axis, keepdims=False)
        other = lax.dynamic_index_in_dim(block, 1 - self.core, axis, keepdims=False)
        return mine, other

    def row_pieces(self, mine, other):
        got = self.swap(other)
        if self.chips == 4:
            firsts, seconds = self.two_ways(mine, got)[2]()
        else:
            firsts, seconds = self.chip_hops(mine), self.chip_hops(got)
        return [piece for pair in zip(firsts, seconds) for piece in pair]

    def everywhere(self, pay):
        return self.plane_hops(jnp.concatenate([pay, self.swap(pay)], axis=0))


class Far:
    def __init__(self, source, target, semaphore):
        self.copy = pltpu.make_async_copy(source, target, semaphore)
        self.copy.start()
        self.target, self.waits = target, True

    def ready(self):
        if self.waits:
            self.copy.wait()
            self.waits = False
        return self.target


def rows_loop(total, body, carry=None, step=CHUNK):
    def turn(index, state):
        return body(pl.ds(pl.multiple_of(index * step, step), step), state)

    return lax.fori_loop(0, total // step, turn, carry)


GAIN_WIDE, SHIFT_WIDE, GAIN, SHIFT = 0, 2, 4, 9


def row_of(params, first, index, half=None):
    return params[first + index : first + index + 1, 0 : (half or params.shape[1])]


def finish_moments(scal, refs, cols=slice(None)):
    pixels = scal[1]
    center = tree_sum([r[0:1, cols] + r[2:3, cols] for r in refs]) / pixels
    terms = []
    for k, r in enumerate(refs):
        ends = []
        for side in range(2):
            count, over = scal[2 + 4 * k + 2 * side], scal[3 + 4 * k + 2 * side]
            gap = r[2 * side : 2 * side + 1, cols] * over - center
            ends.append(gap * gap * count)
        terms.append((r[1:2, cols] + r[3:4, cols]) + (ends[0] + ends[1]))
    return center, lax.rsqrt(tree_sum(terms) / pixels + EPSILON)


def finish_sums(refs, cols=slice(None)):
    return (
        tree_sum([r[0:1, cols] + r[2:3, cols] for r in refs]),
        tree_sum([r[1:2, cols] + r[3:4, cols] for r in refs]),
    )


def put_moments(values, pay, cols, weight):
    total = jnp.sum(values, axis=0, keepdims=True)
    off = values - total * (1.0 / values.shape[0])
    pay[0:1, cols] = total * weight
    pay[1:2, cols] = jnp.sum(off * off, axis=0, keepdims=True) * weight


def project(left, weights, pre, pay, weight, add=None):
    weights = weights.ready() if isinstance(weights, Far) else weights
    for start in range(0, pre.shape[1], COLS):
        cols = slice(start, start + COLS)
        out = dot(left[...], weights[:, cols])
        if add is not None:
            out = out + add[:, cols]
        pre[:, cols] = out
        put_moments(out, pay, cols, weight)


def fold(values):
    return jnp.sum(values.reshape(-1, 8, values.shape[-1]), axis=0)


def push(grad_of, pre, center, rstd, gain, offset, pushed, pay):
    def body(rows, sums):
        unit = (pre[rows, :].astype(F32) - center) * rstd
        out = grad_of(rows) * mish_slope(unit * gain + offset)
        pushed[rows, :] = out
        return sums[0] + fold(out), sums[1] + fold(out * unit)

    zero = jnp.zeros((8, pre.shape[1]), F32)
    first, second = rows_loop(pre.shape[0], body, (zero, zero), 16)
    pay[0:1, :] = jnp.sum(first, axis=0, keepdims=True)
    pay[1:2, :] = jnp.sum(second, axis=0, keepdims=True)


def settle(scal, refs, pushed, pre, coef, gain, out, sums):
    first, second = finish_sums(refs)
    sums[0:1, :] = first
    sums[1:2, :] = second
    over = 1.0 / scal[1]
    center, rstd = coef[0:1, :], coef[1:2, :]
    scale = gain * rstd * scal[0]
    level, tilt = first * over, second * over * rstd

    def body(rows, _):
        x = pre[rows, :].astype(F32) - center
        out[rows, :] = (scale * (pushed[rows, :] - level - x * tilt)).astype(BF)

    rows_loop(pre.shape[0], body)


def shifted_row(both):
    half = both.shape[1] // 2
    odd = both[:, half:].astype(F32)
    first = lax.broadcasted_iota(jnp.int32, odd.shape, 0) == 0
    before = jnp.where(first, 0.0, pltpu.roll(odd, 1, 0)).astype(BF)
    return jnp.concatenate([before, both], axis=1)


def first_kernel(scal, x, above, w, rows, pay, held, semaphores):
    slots, cells = above.shape[0], above.shape[1]
    count, _, _, wide = held.shape
    copies = [
        pltpu.make_async_copy(w.at[:, :, n * wide : (n + 1) * wide], held.at[n], semaphores.at[n])
        for n in range(count)
    ]
    for copy in copies:
        copy.start()
    sources = [above[...]] + [x[:, row] for row in range(2)]
    lefts = [
        jnp.concatenate([shifted_row(source[slot]) for slot in range(slots)], axis=0)
        for source in sources
    ]
    for n, copy in enumerate(copies):
        cols = slice(n * wide, (n + 1) * wide)
        copy.wait()
        out = sum(dot(left, held[n, tap]) for tap, left in enumerate(lefts))
        for slot in range(slots):
            rows[slot, :, cols] = out[slot * cells : (slot + 1) * cells].astype(BF)
        total = sum(
            jnp.sum(out[slot * cells : (slot + 1) * cells], axis=0, keepdims=True) * scal[slot]
            for slot in range(slots)
        )
        mean = total * scal[slots]
        spread = 0.0
        for slot in range(slots):
            off = out[slot * cells : (slot + 1) * cells] - mean
            spread += jnp.sum(off * off, axis=0, keepdims=True) * scal[slot]
        both = jnp.concatenate([total, spread], axis=0)
        pay[:, :, cols] = jnp.broadcast_to(both[None], (pay.shape[0],) + both.shape)


def main_kernel(pieces, scal, spots, got, counts, over, params, *rest):
    parts = rest[:pieces]
    w_main, down_pre, sectioned, main_pre, pay, coef = rest[pieces:]
    pixels = scal[1]
    firsts, seconds = got[:, 0, :], got[:, 1, :]
    center = jnp.sum(firsts, axis=0, keepdims=True) / pixels
    gap = firsts * over[...] - center
    total = jnp.sum(seconds + gap * gap * counts[...], axis=0, keepdims=True)
    rstd = lax.rsqrt(total / pixels + EPSILON)
    coef[0:1, :] = center
    coef[1:2, :] = rstd
    scale, offset = rstd * row_of(params, GAIN_WIDE, 0), row_of(params, SHIFT_WIDE, 0)
    for k, part in enumerate(parts):
        part = part.ready()
        width = part.shape[0]
        start = spots[k] * width

        def body(index, _, part=part, start=start):
            src = pl.ds(pl.multiple_of(index * CHUNK, CHUNK), CHUNK)
            dst = pl.ds(pl.multiple_of(start + index * CHUNK, CHUNK), CHUNK)
            x = part[src, :]
            down_pre[dst, :] = x
            value = (x.astype(F32) - center) * scale + offset
            sectioned[dst, :] = mish(value).astype(BF)

        lax.fori_loop(0, width // CHUNK, body, None)
    project(sectioned, w_main, main_pre, pay, scal[0])


def short_kernel(scal, sectioned, w_short, short_pre, pay):
    project(sectioned, w_short, short_pre, pay, scal[0])


def inner_kernel(groups, scal, *rest):
    refs = rest[:groups]
    pre, params, w_inner, mainline, inner_pre, pay, coef = rest[groups:]
    half = pre.shape[1]
    center, rstd = finish_moments(scal, refs)
    coef[0:1, :] = center
    coef[1:2, :] = rstd
    scale, offset = rstd * row_of(params, GAIN, 1, half), row_of(params, SHIFT, 1, half)

    def body(rows, _):
        mainline[rows, :] = mish((pre[rows, :] - center) * scale + offset).astype(BF)

    rows_loop(pre.shape[0], body)
    project(mainline, w_inner, inner_pre, pay, scal[0])


def three_shifts(values, rim, start, forward):
    width, half = values.shape
    place = lax.broadcasted_iota(jnp.int32, values.shape, 0)
    before = jnp.where(place == 0, 0.0, pltpu.roll(values, 1, 0)).astype(BF)
    after = jnp.where(place == width - 1, 0.0, pltpu.roll(values, width - 1, 0)).astype(BF)
    sides = (before, after) if forward else (after, before)
    rows = pl.ds(start, width)
    rim[rows, 0:half] = sides[0]
    rim[rows, half : 2 * half] = values.astype(BF)
    rim[rows, 2 * half : 3 * half] = sides[1]


def spatial_kernel(groups, width, scal, *rest):
    refs = rest[:groups]
    pre, params, w_spatial, rim, spatial_pre, pay, coef = rest[groups:]
    cells, half = pre.shape
    center, rstd = finish_moments(scal, refs)
    coef[0:1, :] = center
    coef[1:2, :] = rstd
    scale, offset = rstd * row_of(params, GAIN, 2, half), row_of(params, SHIFT, 2, half)
    blank = jnp.zeros((width, 3 * half), BF)
    rim[0:width, :] = blank
    rim[width + cells :, :] = blank

    def body(index, _):
        start = pl.multiple_of(index * width, width)
        act = mish((pre[pl.ds(start, width), :] - center) * scale + offset)
        three_shifts(act, rim, pl.multiple_of(start + width, width), True)

    lax.fori_loop(0, cells // width, body, None)
    w_spatial = w_spatial.ready()
    for begin in range(0, half, COLS):
        cols = slice(begin, begin + COLS)
        out = sum(
            dot(
                rim[i * width : i * width + cells, :],
                w_spatial[i * 3 * half : (i + 1) * 3 * half, cols],
            )
            for i in range(3)
        )
        spatial_pre[:, cols] = out
        put_moments(out, pay, cols, scal[0])


def trans_kernel(groups, scal, *rest):
    refs = rest[:groups]
    pre, mainline, params, w_trans, merged, trans_pre, pay, coef = rest[groups:]
    half = pre.shape[1]
    center, rstd = finish_moments(scal, refs)
    coef[0:1, :] = center
    coef[1:2, :] = rstd
    scale, offset = rstd * row_of(params, GAIN, 3, half), row_of(params, SHIFT, 3, half)

    def body(rows, _):
        act = mish((pre[rows, :] - center) * scale + offset)
        merged[rows, :] = (mainline[rows, :].astype(F32) + act).astype(BF)

    rows_loop(pre.shape[0], body)
    project(merged, w_trans, trans_pre, pay, scal[0])


def shortcut_kernel(groups, scal, *rest):
    refs = rest[:groups]
    pre, params, w_unite, shortcut, part, coef = rest[groups:]
    half = pre.shape[1]
    center, rstd = finish_moments(scal, refs)
    coef[0:1, :] = center
    coef[1:2, :] = rstd
    scale, offset = rstd * row_of(params, GAIN, 0, half), row_of(params, SHIFT, 0, half)

    def body(rows, _):
        shortcut[rows, :] = mish((pre[rows, :] - center) * scale + offset).astype(BF)

    rows_loop(pre.shape[0], body)
    w_unite = w_unite.ready()
    for start in range(0, part.shape[1], COLS):
        cols = slice(start, start + COLS)
        part[:, cols] = dot(shortcut[...], w_unite[0:half, cols])


def unite_kernel(groups, scal, *rest):
    refs = rest[:groups]
    pre, part, params, w_unite, transition, unite_pre, pay, coef = rest[groups:]
    half = pre.shape[1]
    center, rstd = finish_moments(scal, refs)
    coef[0:1, :] = center
    coef[1:2, :] = rstd
    scale, offset = rstd * row_of(params, GAIN, 4, half), row_of(params, SHIFT, 4, half)

    def body(rows, _):
        transition[rows, :] = mish((pre[rows, :] - center) * scale + offset).astype(BF)

    rows_loop(pre.shape[0], body)
    project(transition, w_unite.ready().at[half:, :], unite_pre, pay, scal[0], part)


def turn_kernel(groups, pieces, scal, spots, *rest):
    refs = rest[:groups]
    pre, params = rest[groups : groups + 2]
    parts = rest[groups + 2 : groups + 2 + pieces]
    pushed, *outputs, pay, coef = rest[groups + 2 + pieces :]
    center, rstd = finish_moments(scal, refs)
    coef[0:1, :] = center
    coef[1:2, :] = rstd
    gain, offset, weight = row_of(params, GAIN_WIDE, 1), row_of(params, SHIFT_WIDE, 1), scal[0]
    sums = (jnp.zeros((8, pre.shape[1]), F32),) * 2
    for k, part in enumerate(parts):
        part = part.ready()
        width = part.shape[0]
        start = spots[k] * width

        def body(index, sums, k=k, part=part, start=start):
            src = pl.ds(pl.multiple_of(index * 16, 16), 16)
            dst = pl.ds(pl.multiple_of(start + index * 16, 16), 16)
            unit = (pre[dst, :] - center) * rstd
            value = unit * gain + offset
            grown = jnp.exp(jnp.minimum(value, FAR))
            wide = grown * (grown + 2.0)
            share = 1.0 / (wide + 2.0)
            level = wide * share
            if k < 2:
                outputs[k][src, :] = (value * level * weight).astype(BF)
            slope = level + 4.0 * value * (grown * (grown + 1.0) * share) * share
            out = part[src, :].astype(F32) * weight * slope
            pushed[dst, :] = out
            return sums[0] + fold(out), sums[1] + fold(out * unit)

        sums = lax.fori_loop(0, width // 16, body, sums)
    pay[0:1, :] = jnp.sum(sums[0], axis=0, keepdims=True)
    pay[1:2, :] = jnp.sum(sums[1], axis=0, keepdims=True)


def back_trans_kernel(groups, scal, *rest):
    refs = rest[:groups]
    (
        unite_pushed, unite_pre, unite_coef, params, trans_pre, trans_coef, w_unite,
        grad_unite, sums, pushed, pay, scratch,
    ) = rest[groups:]
    half = trans_pre.shape[1]
    settle(scal, refs, unite_pushed, unite_pre, unite_coef, row_of(params, GAIN_WIDE, 1), grad_unite, sums)
    w_unite = w_unite.ready()
    for start in range(0, half, COLS):
        scratch[:, start : start + COLS] = dot_back(
            grad_unite[...], w_unite[half + start : half + start + COLS, :]
        )
    push(
        lambda rows: scratch[rows, :],
        trans_pre, trans_coef[0:1, :], trans_coef[1:2, :], row_of(params, GAIN, 4, half), row_of(params, SHIFT, 4, half),
        pushed, pay,
    )


def back_short_kernel(grad_unite, pre, coef, params, w_unite, pushed, pay, scratch):
    half = pre.shape[1]
    w_unite = w_unite.ready()
    for start in range(0, half, COLS):
        scratch[:, start : start + COLS] = dot_back(
            grad_unite[...], w_unite[start : start + COLS, :]
        )
    push(
        lambda rows: scratch[rows, :],
        pre, coef[0:1, :], coef[1:2, :], row_of(params, GAIN, 0, half), row_of(params, SHIFT, 0, half), pushed, pay,
    )


def back_spatial_kernel(groups, scal, *rest):
    refs = rest[:groups]
    (
        trans_pushed, trans_pre, trans_coef, spatial_pre, spatial_coef, params, w_trans,
        grad_trans, sums, grad_merged, pushed, pay,
    ) = rest[groups:]
    half = trans_pre.shape[1]
    settle(scal, refs, trans_pushed, trans_pre, trans_coef, row_of(params, GAIN, 4, half), grad_trans, sums)
    w_trans = w_trans.ready()
    for start in range(0, half, COLS):
        grad_merged[:, start : start + COLS] = dot_back(
            grad_trans[...], w_trans[start : start + COLS, :]
        )
    push(
        lambda rows: grad_merged[rows, :],
        spatial_pre, spatial_coef[0:1, :], spatial_coef[1:2, :], row_of(params, GAIN, 3, half), row_of(params, SHIFT, 3, half),
        pushed, pay,
    )


def back_inner_kernel(groups, width, scal, *rest):
    refs = rest[:groups]
    (
        spatial_pushed, spatial_pre, spatial_coef, inner_pre, inner_coef, params, w_spatial,
        grad_spatial, sums, pushed, pay, rim, scratch,
    ) = rest[groups:]
    cells, half = spatial_pre.shape
    settle(scal, refs, spatial_pushed, spatial_pre, spatial_coef, row_of(params, GAIN, 3, half), grad_spatial, sums)
    blank = jnp.zeros((width, 3 * half), BF)
    rim[0:width, :] = blank
    rim[width + cells :, :] = blank

    def body(index, _):
        start = pl.multiple_of(index * width, width)
        values = grad_spatial[pl.ds(start, width), :].astype(F32)
        three_shifts(values, rim, pl.multiple_of(start + width, width), False)

    lax.fori_loop(0, cells // width, body, None)
    w_spatial = w_spatial.ready()
    for start in range(0, half, COLS):
        scratch[:, start : start + COLS] = sum(
            dot_back(
                rim[(2 - i) * width : (2 - i) * width + cells, j * half : (j + 1) * half],
                w_spatial[(3 * i + j) * half + start : (3 * i + j) * half + start + COLS, :],
            )
            for i in range(3)
            for j in range(3)
        )
    push(
        lambda rows: scratch[rows, :],
        inner_pre, inner_coef[0:1, :], inner_coef[1:2, :], row_of(params, GAIN, 2, half), row_of(params, SHIFT, 2, half),
        pushed, pay,
    )


def back_main_kernel(groups, scal, *rest):
    refs = rest[:groups]
    (
        inner_pushed, inner_pre, inner_coef, grad_merged, main_pre, main_coef, params, w_inner,
        grad_inner, sums, pushed, pay, scratch,
    ) = rest[groups:]
    half = inner_pre.shape[1]
    settle(scal, refs, inner_pushed, inner_pre, inner_coef, row_of(params, GAIN, 2, half), grad_inner, sums)
    w_inner = w_inner.ready()
    for start in range(0, half, COLS):
        cols = slice(start, start + COLS)
        scratch[:, cols] = grad_merged[:, cols] + dot_back(grad_inner[...], w_inner[cols, :])
    push(
        lambda rows: scratch[rows, :],
        main_pre, main_coef[0:1, :], main_coef[1:2, :], row_of(params, GAIN, 1, half), row_of(params, SHIFT, 1, half),
        pushed, pay,
    )


def settle_short_kernel(groups, scal, *rest):
    refs = rest[:groups]
    pushed, pre, coef, params, w_short, grad_short, sums, part = rest[groups:]
    half = pre.shape[1]
    settle(scal, refs, pushed, pre, coef, row_of(params, GAIN, 0, half), grad_short, sums)
    w_short = w_short.ready()
    for start in range(0, part.shape[1], COLS):
        part[:, start : start + COLS] = dot_back(grad_short[...], w_short[start : start + COLS, :])


def back_down_kernel(groups, scal, *rest):
    refs = rest[:groups]
    (
        main_pushed, main_pre, main_coef, part, down_pre, down_coef, params, w_main,
        grad_main, sums, pushed, pay, scratch,
    ) = rest[groups:]
    half = main_pre.shape[1]
    settle(scal, refs, main_pushed, main_pre, main_coef, row_of(params, GAIN, 1, half), grad_main, sums)
    w_main = w_main.ready()
    for start in range(0, part.shape[1], COLS):
        cols = slice(start, start + COLS)
        scratch[:, cols] = part[:, cols] + dot_back(grad_main[...], w_main[cols, :])
    push(
        lambda rows: scratch[rows, :],
        down_pre, down_coef[0:1, :], down_coef[1:2, :], row_of(params, GAIN_WIDE, 0), row_of(params, SHIFT_WIDE, 0),
        pushed, pay,
    )


def settle_down_kernel(groups, scal, *rest):
    refs = rest[:groups]
    pushed, pre, coef, params, grad_down, sums = rest[groups:]
    settle(scal, refs, pushed, pre, coef, row_of(params, GAIN_WIDE, 0), grad_down, sums)
    cells = pre.shape[0]
    grad_down[cells:, :] = jnp.zeros((grad_down.shape[0] - cells, pre.shape[1]), BF)


def cut_down_kernel(groups, scal, spots, *rest):
    refs = rest[:groups]
    pushed, pre, coef, params, cut = rest[groups:]
    width = cut.shape[1]
    cols = pl.ds(pl.multiple_of(spots[1] * width, width), width)
    first, second = finish_sums(refs, cols)
    over = 1.0 / scal[1]
    center, rstd = coef[0:1, cols], coef[1:2, cols]
    scale = params[GAIN_WIDE : GAIN_WIDE + 1, cols] * rstd * scal[0]
    level, tilt = first * over, second * over * rstd

    def body(rows, _):
        x = pre[rows, cols].astype(F32) - center
        cut[rows, :] = (scale * (pushed[rows, cols] - level - x * tilt)).astype(BF)

    rows_loop(pre.shape[0], body)


def by_place(spots, first, second):
    low = spots[0] == 0
    return jnp.where(low, first, second), jnp.where(low, second, first)


def share_unite_kernel(spots, shortcut, transition, grad, mine, other):
    width = 2 * mine.shape[1]
    cut = grad[:, pl.ds(pl.multiple_of(spots[1] * width, width), width)]
    half = shortcut.shape[1]
    for k, values in enumerate((shortcut, transition)):
        out = dot_cells(values[...], cut)
        near, far = by_place(spots, out[:, : width // 2], out[:, width // 2 :])
        mine[k * half : (k + 1) * half, :] = near.astype(BF)
        other[k * half : (k + 1) * half, :] = far.astype(BF)


def put_halves(spots, cut, values, start, mine, other):
    out = dot_cells(cut, values)
    rows, cols = mine.shape[0], slice(start, start + out.shape[1])
    near, far = by_place(spots, out[:rows], out[rows:])
    mine[:, cols] = near.astype(BF)
    other[:, cols] = far.astype(BF)


def chip_columns(spots, mine):
    width = 2 * mine.shape[0]
    return pl.ds(pl.multiple_of(spots[1] * width, width), width)


def share_pack_kernel(spots, sectioned, grad_short, merged, grad_trans, mainline, grad_inner, mine, other):
    cols = chip_columns(spots, mine)
    start = 0
    for values, grad in ((sectioned, grad_short), (merged, grad_trans), (mainline, grad_inner)):
        put_halves(spots, grad[:, cols], values[...], start, mine, other)
        start += values.shape[1]


def share_spatial_kernel(cells, spots, rim, grad, mine, other):
    cut = grad[:, chip_columns(spots, mine)]
    line, side = (rim.shape[0] - cells) // 2, rim.shape[1]
    for row in range(3):
        put_halves(spots, cut, rim[row * line : row * line + cells, :], row * side, mine, other)


def share_main_kernel(spots, sectioned, grad, mine, other):
    put_halves(spots, grad[:, chip_columns(spots, mine)], sectioned[...], 0, mine, other)


def finish_kernel(unite, pack, taps, main, w_unite, w_short, w_trans, w_inner, w_spatial, w_main):
    w_unite[...] = unite[...].astype(F32)
    w_main[...] = main[...].astype(F32)
    start = 0
    for out in (w_short, w_trans, w_inner):
        out[...] = pack[:, start : start + out.shape[1]].astype(F32)
        start += out.shape[1]
    half = w_trans.shape[1]
    for tap in range(w_spatial.shape[0]):
        w_spatial[tap] = taps[:, tap * half : (tap + 1) * half].astype(F32)


def norm_sums_kernel(wide_count, *refs):
    sums, outs = refs[:-4], refs[-4:]
    for k, pair in enumerate(sums):
        index = k if k < wide_count else k - wide_count
        for row, out in ((1, outs[0 if k < wide_count else 1]), (0, outs[2 if k < wide_count else 3])):
            out[index : index + 1, :] = pair[row : row + 1, :]


def share_down_kernel(steps, chips, width, last_call, spots, *rest):
    grads = rest[: len(steps)]
    earlier = rest[len(steps) : len(steps) + 2 * last_call]
    rest = rest[len(steps) + 2 * last_call :]
    source, outs, rest = rest[0], rest[1:3], rest[3:]
    if last_call:
        odd_acc, even_acc = rest[:2]
        rest = rest[2:]
    else:
        odd_acc, even_acc = outs
    padded, sides, held, semaphores = rest
    cells, columns = grads[0].shape
    half = source.shape[-1] // 2
    planes = source.shape[0] // (2 * chips)
    copies = []
    for k, step in enumerate(steps):
        plane = spots[2 + step]
        copies.append(
            [
                pltpu.make_async_copy(
                    source.at[row * planes + plane, spots[0]], held.at[k, row], semaphores.at[k, row]
                )
                for row in range(2 * chips)
            ]
        )
        for copy in copies[-1]:
            copy.start()
    padded[cells:, :] = jnp.zeros((padded.shape[0] - cells, columns), BF)
    last = lax.broadcasted_iota(jnp.int32, (width, columns), 0) == width - 1

    def ahead(values):
        return jnp.where(last, 0.0, pltpu.roll(values.astype(F32), width - 1, 0)).astype(BF)

    for k in range(len(steps)):
        padded[0:cells, :] = grads[k][...]
        for block in range(2 * chips):
            rows = slice(block * width, (block + 1) * width)
            here = padded[rows, :]
            upper = padded[(block + 1) * width : (block + 2) * width, :]
            sides[rows, 0:columns] = upper
            sides[rows, columns : 2 * columns] = here
            sides[rows, 2 * columns : 3 * columns] = ahead(here)
            sides[rows, 3 * columns : 4 * columns] = ahead(upper)
        for copy in copies[k]:
            copy.wait()

        def add(which, side, start, values, k=k):
            rows, cols = slice(side * half, (side + 1) * half), slice(start, start + columns)
            acc = (even_acc, odd_acc)[which]
            if k > 0:
                values = values + acc[rows, cols]
            elif last_call:
                values = values + earlier[1 - which][rows, cols]
            acc[rows, cols] = values

        for which in range(2):
            for side in range(2):
                left = held[k, :, which, :, side * half : (side + 1) * half].reshape(cells, half)
                for block in range(4):
                    if (which == 0 and block in (0, 3)) or (side == 0 and block in (2, 3)):
                        continue
                    start = block * columns
                    add(which, side, start, dot_cells(left, sides[:, start : start + columns]))
    if not last_call:
        return
    mine, other = outs
    places = (
        (odd_acc, 1, 3), (odd_acc, 0, 0), (odd_acc, 1, 0),
        (even_acc, 1, 2), (even_acc, 0, 1), (even_acc, 1, 1),
        (odd_acc, 1, 2), (odd_acc, 0, 1), (odd_acc, 1, 1),
    )
    for tap, (acc, side, block) in enumerate(places):
        values = acc[side * half : (side + 1) * half, block * columns : (block + 1) * columns]
        near, far = by_place(spots, values[:, : columns // 2], values[:, columns // 2 :])
        mine[tap * half : (tap + 1) * half, :] = near.astype(BF)
        other[tap * half : (tap + 1) * half, :] = far.astype(BF)


def back_input_kernel(width, spots, grad, w, out, near, far):
    cells = 2 * width
    full = grad.shape[1]

    @pl.when(pl.program_id(0) == 0)
    def _():
        last = lax.broadcasted_iota(jnp.int32, (width, full), 0) == width - 1
        for block in range(3):
            start = pl.multiple_of(spots[1] * cells + block * width, width)
            values = grad[pl.ds(start, width), :]
            rows = slice(block * width, (block + 1) * width)
            near[rows, :] = values
            far[rows, :] = jnp.where(
                last, 0.0, pltpu.roll(values.astype(F32), width - 1, 0)
            ).astype(BF)

    low, high = slice(0, cells), slice(width, width + cells)

    def term(values, rows, i, j):
        return dot_back(values[rows, :], w[3 * i + j])

    def put(parity, column, values):
        for row in range(2):
            out[2 * row + parity, pl.ds(column, width, stride=2), :] = values[
                row * width : (row + 1) * width
            ]

    put(0, 0, term(near, low, 1, 1))
    put(0, 1, term(near, low, 1, 2) + term(far, low, 1, 0))
    put(1, 0, term(near, high, 0, 1) + term(near, low, 2, 1))
    put(
        1,
        1,
        term(near, high, 0, 2) + term(far, high, 0, 0) + term(near, low, 2, 2) + term(far, low, 2, 0),
    )


SMEM = pl.BlockSpec(memory_space=pltpu.SMEM)
VMEM = pl.BlockSpec(memory_space=pltpu.VMEM)
ANY = pl.BlockSpec(memory_space=pl.ANY)


def shape(dims, dtype=F32):
    return jax.ShapeDtypeStruct(dims, dtype)


def nbytes(dims, dtype):
    count = 1
    for d in dims:
        count *= d
    return count * jnp.dtype(dtype).itemsize


def in_vmem(value):
    return pltpu.with_memory_space_constraint(value, pltpu.VMEM)


def in_hbm(value):
    return pltpu.with_memory_space_constraint(value, pltpu.HBM)


def call(kernel, name, scalars, near, outs, flops, scratch=(), far=(), pin=False, spill=()):
    moved = sum(nbytes(a.shape, a.dtype) for a in (*near, *far, *outs))
    held = moved + sum(nbytes(s.shape, s.dtype) for s in scratch)
    if pin:
        held -= moved - sum(nbytes(a.shape, a.dtype) for a in far)
        held += sum(nbytes(outs[k].shape, outs[k].dtype) for k in spill)
        near, far = [in_vmem(a) for a in near], [in_hbm(a) for a in far]
        outs = [
            o if k in spill else pltpu.VMEM(o.shape, o.dtype) for k, o in enumerate(outs)
        ]
    before, after_far, last = len(scalars) + len(near), len(far), len(outs) + len(scratch)

    def body(*refs):
        sources, rest = refs[before : before + after_far], refs[before + after_far :]
        targets = rest[last : last + after_far]
        fars = [Far(a, b, rest[-1].at[k]) for k, (a, b) in enumerate(zip(sources, targets))]
        kernel(*refs[:before], *fars, *rest[:last])
        for one in fars:
            one.ready()

    return pl.pallas_call(
        body if far else kernel,
        name=name,
        out_shape=tuple(outs),
        in_specs=[SMEM] * len(scalars) + [VMEM] * len(near) + [ANY] * len(far),
        out_specs=tuple([VMEM] * len(outs)),
        scratch_shapes=[pltpu.VMEM(s.shape, s.dtype) for s in scratch]
        + [pltpu.VMEM(a.shape, a.dtype) for a in far]
        + ([pltpu.SemaphoreType.DMA((len(far),))] if far else []),
        compiler_params=pltpu.CompilerParams(vmem_limit_bytes=held + (8 << 20)),
        cost_estimate=pl.CostEstimate(flops=flops, bytes_accessed=moved, transcendentals=0),
    )(*scalars, *near, *far)


def first_conv(scal, view, above, w_down, devices, pin):
    slots, _, cells, both = view.shape
    half = both // 2
    full = w_down.shape[-1]
    taps = w_down.reshape(3, 3 * half, full)
    if pin:
        view, above, taps = in_vmem(view), in_vmem(above), in_hbm(taps)
    wide = 256
    count = full // wide
    return pl.pallas_call(
        first_kernel,
        name="first",
        out_shape=(shape((slots, cells, full), BF), shape((devices, 2, full))),
        in_specs=[SMEM, VMEM, VMEM, ANY],
        out_specs=(VMEM, VMEM),
        scratch_shapes=[
            pltpu.VMEM((count, 3, 3 * half, wide), BF), pltpu.SemaphoreType.DMA((count,))
        ],
        compiler_params=pltpu.CompilerParams(vmem_limit_bytes=32 << 20),
        cost_estimate=pl.CostEstimate(
            flops=18 * slots * cells * half * full, bytes_accessed=18 * half * full, transcendentals=0
        ),
    )(scal, view, above, taps)


def flipped(kernel):
    return jnp.swapaxes(jnp.flip(kernel, (0, 1)), 2, 3)


def on_device(
    inputs,
    image_counts,
    w_down,
    w_short,
    w_main,
    w_inner,
    w_spatial,
    w_trans,
    w_unite,
    gains_wide,
    gains_narrow,
    shifts_wide,
    shifts_narrow,
    grad_output,
):
    half = w_short.shape[1]
    full = 2 * half
    slots, height_dev, width, _ = grad_output.shape
    here = Plane()
    wide = here.chips == 4 and half % (128 * here.chips) == 0
    stage = functools.partial(call, pin=wide)
    groups, chips = here.groups, here.chips
    height = here.rows * height_dev
    cells = height * width
    batch = lax.axis_index("batch")
    counts = image_counts.astype(F32)
    own_count = image_counts[batch]
    pixels = jnp.sum(counts) * cells
    weight = (here.core < own_count).astype(F32)

    scal = [weight, pixels]
    for step in range(groups):
        plane = batch ^ step
        for slot in (here.core, 1 - here.core):
            count = (slot < image_counts[plane]).astype(F32) * cells
            scal += [count, 1.0 / jnp.maximum(count, 1.0)]
    scal = jnp.stack(scal)
    spots = jnp.stack(
        [2 * (here.chip ^ step) + (here.core ^ side) for step in range(chips) for side in range(2)]
    ).astype(jnp.int32)
    slot_scal = jnp.concatenate(
        [
            (jnp.arange(slots) < own_count).astype(F32),
            (1.0 / (own_count.astype(F32) * height_dev * width))[None],
        ]
    )
    device_counts = jnp.tile(counts * (height_dev * width), here.rows).reshape(-1, 1)

    view = inputs.reshape(slots, 2, width, 2 * half)
    below = [(i, i + 1) for i in range(here.rows - 1)]
    above = lax.ppermute(view[:, 1], "rows", below)
    params = jnp.concatenate(
        [gains_wide, shifts_wide]
        + [jnp.pad(p, ((0, 0), (0, half))) for p in (gains_narrow, shifts_narrow)]
    )
    down_rows, sums = first_conv(slot_scal, view, above, w_down, here.rows * groups, wide)
    gathered = lax.all_to_all(sums, ("rows", "batch"), 0, 0, tiled=True)
    down_pieces = here.row_pieces(*here.split(down_rows))
    grad_mine, grad_other = here.split(grad_output.reshape(slots, width, full))
    spot_pair = jnp.stack([here.core, here.chip]).astype(jnp.int32)
    planes = jnp.stack([here.core, here.chip] + [batch ^ step for step in range(groups)]).astype(jnp.int32)
    over_counts = 1.0 / device_counts
    gathered, scal, spots, spot_pair, planes, device_counts, over_counts, params, grad_mine, grad_other = (
        lax.optimization_barrier(
            (gathered, scal, spots, spot_pair, planes, device_counts, over_counts, params, grad_mine, grad_other)
        )
    )
    if wide:
        source = lax.all_gather(view, ("rows", "batch"))
    down_pre, sectioned, main_pre, main_pay, down_coef = stage(
        functools.partial(main_kernel, 2 * chips),
        "main",
        [scal, spots],
        [gathered, device_counts, over_counts, params],
        [
            shape((cells, full), BF), shape((cells, full), BF), shape((cells, half)),
            shape((2, half)), shape((2, full)),
        ],
        2 * cells * full * half,
        far=[*down_pieces, w_main],
    )

    grad_pieces = here.row_pieces(after(grad_mine, main_pay), after(grad_other, main_pay))

    main_all = here.everywhere(main_pay)
    short_pre, short_pay = stage(
        short_kernel,
        "short",
        [scal],
        [sectioned],
        [shape((cells, half)), shape((2, half))],
        2 * cells * full * half,
        far=[w_short],
    )
    mainline, inner_pre, inner_pay, main_coef = stage(
        functools.partial(inner_kernel, groups),
        "inner",
        [scal],
        [*main_all, main_pre, params],
        [shape((cells, half), BF), shape((cells, half)), shape((2, half)), shape((2, half))],
        2 * cells * half * half,
        far=[w_inner],
    )
    inner_all = here.everywhere(inner_pay)
    rim, spatial_pre, spatial_pay, inner_coef = stage(
        functools.partial(spatial_kernel, groups, width),
        "spatial",
        [scal],
        [*inner_all, inner_pre, params],
        [
            shape((cells + 2 * width, 3 * half), BF), shape((cells, half)),
            shape((2, half)), shape((2, half)),
        ],
        18 * cells * half * half,
        far=[w_spatial.reshape(9 * half, half)],
    )
    if wide:
        spatial_pay = after(spatial_pay, *grad_pieces)
    both_all = here.everywhere(jnp.concatenate([spatial_pay, short_pay], axis=1))
    spatial_all = [b[:, :half] for b in both_all]
    short_all = [b[:, half:] for b in both_all]
    merged, trans_pre, trans_pay, spatial_coef = stage(
        functools.partial(trans_kernel, groups),
        "trans",
        [scal],
        [*spatial_all, spatial_pre, mainline, params],
        [shape((cells, half), BF), shape((cells, half)), shape((2, half)), shape((2, half))],
        2 * cells * half * half,
        far=[w_trans],
    )
    trans_all = here.everywhere(trans_pay)
    shortcut, unite_part, short_coef = stage(
        functools.partial(shortcut_kernel, groups),
        "shortcut",
        [scal],
        [*short_all, short_pre, params],
        [shape((cells, half), BF), shape((cells, full)), shape((2, half))],
        2 * cells * half * full,
        far=[w_unite],
    )
    transition, unite_pre, unite_pay, trans_coef = stage(
        functools.partial(unite_kernel, groups),
        "unite",
        [scal],
        [*trans_all, trans_pre, unite_part, params],
        [shape((cells, half), BF), shape((cells, full)), shape((2, full)), shape((2, half))],
        2 * cells * half * full,
        far=[w_unite],
    )
    unite_all = here.everywhere(unite_pay)
    unite_pushed, mine, other, unite_pay, unite_coef = stage(
        functools.partial(turn_kernel, groups, 2 * chips),
        "turn",
        [scal, spots],
        [*unite_all, unite_pre, params],
        [
            shape((cells, full)), shape((width, full), BF), shape((width, full), BF),
            shape((2, full)), shape((2, full)),
        ],
        40 * cells * full,
        far=grad_pieces,
        spill=(1, 2),
    )
    output_rows = (mine, here.swap(other))

    unite_all = here.everywhere(unite_pay)
    grad_unite_pre, unite_sums, trans_pushed, trans_pay = stage(
        functools.partial(back_trans_kernel, groups),
        "back_trans",
        [scal],
        [*unite_all, unite_pushed, unite_pre, unite_coef, params, trans_pre, trans_coef],
        [shape((cells, full), BF), shape((2, full)), shape((cells, half)), shape((2, half))],
        2 * cells * half * full,
        [shape((cells, half))],
        far=[w_unite],
    )
    trans_all = here.everywhere(trans_pay)
    if wide:

        def of_pair(pair):
            mine, other = pair
            return (mine.astype(F32) + here.swap(other).astype(F32)).astype(BF)

        share_unite = of_pair(
            stage(
                share_unite_kernel,
                "share_unite",
                [spot_pair],
                [shortcut, transition, grad_unite_pre],
                [shape((full, full // chips // 2), BF)] * 2,
                2 * cells * full * full // chips,
            )
        )
    short_pushed, short_pay = stage(
        back_short_kernel,
        "back_short",
        [],
        [grad_unite_pre, short_pre, short_coef, params],
        [shape((cells, half)), shape((2, half))],
        2 * cells * half * full,
        [shape((cells, half))],
        far=[w_unite],
    )
    grad_trans_pre, trans_sums, grad_merged, spatial_pushed, spatial_pay = stage(
        functools.partial(back_spatial_kernel, groups),
        "back_spatial",
        [scal],
        [*trans_all, trans_pushed, trans_pre, trans_coef, spatial_pre, spatial_coef, params],
        [
            shape((cells, half), BF), shape((2, half)), shape((cells, half)), shape((cells, half)),
            shape((2, half)),
        ],
        2 * cells * half * half,
        far=[w_trans],
    )
    both_all = here.everywhere(jnp.concatenate([spatial_pay, short_pay], axis=1))
    spatial_all = [b[:, :half] for b in both_all]
    short_all = [b[:, half:] for b in both_all]
    grad_spatial_pre, spatial_sums, inner_pushed, inner_pay = stage(
        functools.partial(back_inner_kernel, groups, width),
        "back_inner",
        [scal],
        [
            *spatial_all, spatial_pushed, spatial_pre, spatial_coef, inner_pre, inner_coef, params,
        ],
        [shape((cells, half), BF), shape((2, half)), shape((cells, half)), shape((2, half))],
        18 * cells * half * half,
        [shape((cells + 2 * width, 3 * half), BF), shape((cells, half))],
        far=[w_spatial.reshape(9 * half, half)],
    )
    inner_all = here.everywhere(inner_pay)
    grad_short_pre, short_sums, sectioned_part = stage(
        functools.partial(settle_short_kernel, groups),
        "settle_short",
        [scal],
        [*short_all, short_pushed, short_pre, short_coef, params],
        [shape((cells, half), BF), shape((2, half)), shape((cells, full))],
        2 * cells * half * full,
        far=[w_short],
    )
    grad_inner_pre, inner_sums, main_pushed, main_pay = stage(
        functools.partial(back_main_kernel, groups),
        "back_main",
        [scal],
        [*inner_all, inner_pushed, inner_pre, inner_coef, grad_merged, main_pre, main_coef, params],
        [shape((cells, half), BF), shape((2, half)), shape((cells, half)), shape((2, half))],
        2 * cells * half * half,
        [shape((cells, half))],
        far=[w_inner],
    )
    if wide:
        lean = half // chips // 2
        share_spatial = of_pair(
            stage(
                functools.partial(share_spatial_kernel, cells),
                "share_spatial",
                [spot_pair],
                [rim, grad_spatial_pre],
                [shape((lean, 9 * half), BF)] * 2,
                18 * cells * half * half // chips,
            )
        )
        share_pack = of_pair(
            stage(
                share_pack_kernel,
                "share_pack",
                [spot_pair],
                [sectioned, grad_short_pre, merged, grad_trans_pre, mainline, grad_inner_pre],
                [shape((lean, 2 * full), BF)] * 2,
                8 * cells * half * half // chips,
            )
        )
    main_all = here.everywhere(main_pay)
    grad_main_pre, main_sums, down_pushed, down_pay = stage(
        functools.partial(back_down_kernel, groups),
        "back_down",
        [scal],
        [
            *main_all, main_pushed, main_pre, main_coef, sectioned_part, down_pre, down_coef, params,
        ],
        [shape((cells, half), BF), shape((2, half)), shape((cells, full)), shape((2, full))],
        2 * cells * half * full,
        [shape((cells, full))],
        far=[w_main],
    )
    down_all = here.everywhere(down_pay)
    spare = width
    if wide:
        grad_cut = stage(
            functools.partial(cut_down_kernel, groups),
            "cut_down",
            [scal, spot_pair],
            [*down_all, down_pushed, down_pre, down_coef, params],
            [shape((cells, full // chips), BF)],
            10 * cells * full // chips,
        )[0]
        cuts = here.plane_hops(grad_cut)
    grad_down_pre, down_sums = stage(
        functools.partial(settle_down_kernel, groups),
        "settle_down",
        [scal],
        [*down_all, down_pushed, down_pre, down_coef, params],
        [shape((cells + spare, full), BF), shape((2, full))],
        10 * cells * full,
    )
    if wide:
        near = pl.pallas_call(
            functools.partial(back_input_kernel, width),
            name="back_input",
            grid=(half // 128,),
            out_shape=shape((4, 2 * width, half)),
            in_specs=[
                SMEM,
                pl.BlockSpec((cells + spare, full), lambda n: (0, 0)),
                pl.BlockSpec((9, 128, full), lambda n: (0, n, 0)),
            ],
            out_specs=pl.BlockSpec((4, 2 * width, 128), lambda n: (0, 0, n)),
            scratch_shapes=[pltpu.VMEM((3 * width, full), BF)] * 2,
            compiler_params=pltpu.CompilerParams(vmem_limit_bytes=16 << 20),
            cost_estimate=pl.CostEstimate(
                flops=36 * width * full * half, bytes_accessed=18 * full * half, transcendentals=0
            ),
        )(spot_pair, grad_down_pre, w_down.reshape(9, half, full))
        share_main = of_pair(
            stage(
                share_main_kernel,
                "share_main",
                [spot_pair],
                [sectioned, grad_main_pre],
                [shape((lean, full), BF)] * 2,
                4 * cells * half * half // chips,
            )
        )
        shares = lax.psum((share_unite, share_pack, share_spatial, share_main), "batch")
        mine, other = here.split(near.reshape(2, 2, 2 * width, half))
        grad_inputs = jnp.stack(here.by_core(mine, here.swap(other)))
        columns = full // chips
        sums_here = [shape((full, 4 * columns)), shape((full, 4 * columns))]
        halves = [shape((9 * half, columns // 2), BF)] * 2

        def share_down(steps, earlier):
            outs = halves if earlier else sums_here
            near = [*(cuts[step] for step in steps), *earlier]
            scratch = [
                pltpu.VMEM((cells + spare, columns), BF),
                pltpu.VMEM((cells, 4 * columns), BF),
                pltpu.VMEM((len(steps), 2 * chips, 2, width, full), BF),
                pltpu.SemaphoreType.DMA((len(steps), 2 * chips)),
            ]
            if earlier:
                scratch = [pltpu.VMEM(a.shape, F32) for a in sums_here] + scratch
            return pl.pallas_call(
                functools.partial(share_down_kernel, steps, chips, width, int(bool(earlier))),
                name="share_down",
                out_shape=tuple(pltpu.VMEM(o.shape, o.dtype) for o in outs),
                in_specs=[SMEM] + [VMEM] * len(near) + [ANY],
                out_specs=(VMEM, VMEM),
                scratch_shapes=scratch,
                compiler_params=pltpu.CompilerParams(vmem_limit_bytes=30 << 20),
                cost_estimate=pl.CostEstimate(
                    flops=18 * len(steps) * cells * half * columns,
                    bytes_accessed=len(steps) * 4 * cells * full,
                    transcendentals=0,
                ),
            )(planes, *map(in_vmem, near), in_hbm(source))

        middle = (groups + 1) // 2
        cuts[:middle] = lax.optimization_barrier((*cuts[:middle], near))[:middle]
        first_sums = share_down(range(middle), ())
        cuts[middle:] = lax.optimization_barrier((*cuts[middle:], *first_sums))[: groups - middle]
        mine, other = share_down(range(middle, groups), first_sums)
        grad_w_down = mine.astype(F32) + here.swap(other).astype(F32)
        early = stage(
            finish_kernel,
            "finish",
            [],
            shares,
            [
                shape((full, 2 * lean)), shape((lean, full)), shape((lean, half)), shape((lean, half)),
                shape((9, lean, half)), shape((lean, full)),
            ],
            0,
            spill=range(6),
        )
        early = [
            early[1].T, early[5].T, early[3].T, jnp.swapaxes(early[4], 1, 2), early[2].T, early[0],
        ]
    else:
        grad_down_pre = grad_down_pre[:cells]
        def share(values, grad):
            columns = grad.shape[1] // chips
            grad = lax.dynamic_slice_in_dim(grad, here.chip * columns, columns, 1)
            part = jnp.concatenate([dot_cells(v, grad) for v in values], axis=0)
            mine, other = here.split(part.reshape(part.shape[0], 2, columns // 2), 1)
            return (mine + here.swap(other.astype(BF)).astype(F32)).astype(BF)

        windows = [rim[i * width : i * width + cells] for i in range(3)]
        early = lax.psum(
            (
                share([sectioned], grad_short_pre),
                share([sectioned], grad_main_pre),
                share([mainline], grad_inner_pre),
                share(windows, grad_spatial_pre),
                share([merged], grad_trans_pre),
                jnp.concatenate([share([shortcut], grad_unite_pre), share([transition], grad_unite_pre)]),
            ),
            "batch",
        )
        early = [e.astype(F32) for e in early]

        mine, other = here.split(view)
        got = here.chip_hops(jnp.stack([mine, here.swap(other)], axis=1))
        source = jnp.zeros((2, here.rows, width, full), BF)
        for step, piece in enumerate(got):
            for side in range(2):
                source = lax.dynamic_update_slice_in_dim(
                    source, piece[:, side : side + 1], spots[2 * step + side], 1
                )
        grad_map = grad_down_pre.reshape(height, width, full)
        columns = full // chips
        grad_cut = lax.dynamic_slice_in_dim(grad_map, here.chip * columns, columns, 2)
        ahead = jnp.pad(grad_cut[:, 1:], ((0, 0), (0, 1), (0, 0)))
        upper = jnp.pad(grad_cut[1:], ((0, 1), (0, 0), (0, 0)))
        both_ahead = jnp.pad(ahead[1:], ((0, 1), (0, 0), (0, 0)))
        even_rows = source[0].reshape(cells, full)
        odd_rows = source[1].reshape(cells, full)

        def taps_of(rows, here_grad, ahead_grad):
            plain = dot_cells(rows, here_grad.reshape(cells, columns))
            before = dot_cells(rows[:, half:], ahead_grad.reshape(cells, columns))
            return [before, plain]

        part = jnp.concatenate(
            taps_of(odd_rows, upper, both_ahead)
            + taps_of(even_rows, grad_cut, ahead)
            + taps_of(odd_rows, grad_cut, ahead),
            axis=0,
        )
        mine, other = here.split(part.reshape(9 * half, 2, columns // 2), 1)
        part = (mine + here.swap(other.astype(BF)).astype(F32)).astype(BF)
        grad_w_down = lax.psum(part, "batch").astype(F32)

        pair_rows = 2 * height_dev
        grad_image = jnp.pad(grad_map, ((0, 1), (0, 0), (0, 0)))
        grad_block = lax.dynamic_slice_in_dim(grad_image, here.chip * pair_rows, pair_rows + 1, 0)
        widened = lax.conv_general_dilated(
            grad_block[None],
            flipped(w_down),
            (1, 1),
            ((1, 0), (1, 2)),
            lhs_dilation=(2, 2),
            dimension_numbers=("NHWC", "HWIO", "NHWC"),
            preferred_element_type=F32,
        )[0]
        mine = lax.dynamic_slice_in_dim(widened, here.core * pair_rows, pair_rows, 0)
        other = lax.dynamic_slice_in_dim(widened, (1 - here.core) * pair_rows, pair_rows, 0)
        grad_inputs = jnp.stack(here.by_core(mine, here.swap(other)))

    output = jnp.stack(here.by_core(*after(output_rows, down_pay))).reshape(grad_output.shape)
    norm_grads = stage(
        functools.partial(norm_sums_kernel, 2),
        "norm_sums",
        [],
        [down_sums, unite_sums, short_sums, main_sums, inner_sums, spatial_sums, trans_sums],
        [shape((2, full)), shape((5, half))] * 2,
        0,
        spill=range(4),
    )
    return (
        output,
        grad_inputs,
        grad_w_down.reshape(3, 3, half, -1),
        early[0],
        early[1],
        early[2],
        early[3].reshape(3, 3, half, -1),
        early[4],
        early[5],
        *norm_grads,
    )


def solution(mesh):
    placed = (P("batch", "rows", None, None),) + (P(),) * 12 + (P("batch", "rows", None, None),)
    return jax.shard_map(
        on_device,
        mesh=mesh,
        in_specs=placed,
        out_specs=(
            P("batch", "rows", None, None),
            P("batch", "rows", None, None),
            P(None, None, None, "rows"),
            P(None, "rows"),
            P(None, "rows"),
            P(None, "rows"),
            P(None, None, None, "rows"),
            P(None, "rows"),
            P(None, "rows"),
            P(),
            P(),
            P(),
            P(),
        ),
        check_vma=False,
    )
```

```python
import functools

import jax
import jax.numpy as jnp
from jax import lax
from jax.experimental import pallas as pl
from jax.experimental.pallas import tpu as pltpu
from jax.sharding import PartitionSpec as P

EPSILON = 1e-05
FAR = 20.0
CHUNK = 32
COLS = 256
BF = jnp.bfloat16
F32 = jnp.float32


def mish(values):
    grown = jnp.exp(jnp.minimum(values, FAR))
    wide = grown * (grown + 2.0)
    return values * (wide / (wide + 2.0))


def mish_slope(values):
    grown = jnp.exp(jnp.minimum(values, FAR))
    wide = grown * (grown + 2.0)
    share = 1.0 / (wide + 2.0)
    return wide * share + 4.0 * values * (grown * (grown + 1.0) * share) * share


def after(value, *others):
    return lax.optimization_barrier((value,) + others)[0]


def tree_sum(parts):
    while len(parts) > 1:
        parts = [parts[i] + parts[i + 1] for i in range(0, len(parts), 2)]
    return parts[0]


def dot(a, b):
    return jnp.dot(a, b, preferred_element_type=F32)


def dot_back(a, b):
    return lax.dot_general(a, b, (((1,), (1,)), ((), ())), preferred_element_type=F32)


def dot_cells(a, b):
    return lax.dot_general(a, b, (((0,), (0,)), ((), ())), preferred_element_type=F32)


class Plane:
    def __init__(self):
        self.rows = lax.axis_size("rows")
        self.groups = lax.axis_size("batch")
        self.chips = self.rows // 2
        self.place = lax.axis_index("rows")
        self.core = self.place % 2
        self.chip = self.place // 2

    def swap(self, value):
        return lax.ppermute(value, "rows", [(i, i ^ 1) for i in range(self.rows)])

    def chip_hops(self, value):
        return [value] + [
            lax.ppermute(value, "rows", [(i, i ^ (2 * step)) for i in range(self.rows)])
            for step in range(1, self.chips)
        ]

    def chip_hop(self, value, step):
        return lax.ppermute(value, "rows", [(i, i ^ (2 * step)) for i in range(self.rows)])

    def plane_hops(self, value):
        return [value] + [
            lax.ppermute(value, "batch", [(i, i ^ step) for i in range(self.groups)])
            for step in range(1, self.groups)
        ]

    def by_core(self, mine, got):
        first = self.core == 0
        return jnp.where(first, mine, got), jnp.where(first, got, mine)

    def split(self, block, axis=0):
        mine = lax.dynamic_index_in_dim(block, self.core, axis, keepdims=False)
        other = lax.dynamic_index_in_dim(block, 1 - self.core, axis, keepdims=False)
        return mine, other

    def pieces(self, mine, other):
        return self.chip_hops(jnp.concatenate([mine, self.swap(other)], axis=0))

    def plane_steps(self, value):
        found = {0: value}
        step = self.groups // 2
        while step:
            found |= {far + step: self.plane_hop(v, step) for far, v in found.items()}
            step //= 2
        return [found[k] for k in range(self.groups)]

    def plane_hop(self, value, step):
        return lax.ppermute(value, "batch", [(i, i ^ step) for i in range(self.groups)])

    def everywhere(self, pay):
        return self.plane_hops(jnp.concatenate([pay, self.swap(pay)], axis=0))


class Far:
    def __init__(self, source, target, semaphore):
        self.copy = pltpu.make_async_copy(source, target, semaphore)
        self.copy.start()
        self.target, self.waits = target, True

    def ready(self):
        if self.waits:
            self.copy.wait()
            self.waits = False
        return self.target


def rows_loop(total, body, carry=None, step=CHUNK):
    def turn(index, state):
        return body(pl.ds(pl.multiple_of(index * step, step), step), state)

    return lax.fori_loop(0, total // step, turn, carry)


GAIN_WIDE, SHIFT_WIDE, GAIN, SHIFT = 0, 2, 4, 9


def row_of(params, first, index, half=None):
    return params[first + index : first + index + 1, 0 : (half or params.shape[1])]


def finish_moments(scal, refs, cols=slice(None)):
    scal = [scal[k : k + 1, 0 : refs[0].shape[1]] for k in range(2 + 4 * len(refs))]
    pixels = scal[1]
    center = tree_sum([r[0:1, cols] + r[2:3, cols] for r in refs]) / pixels
    terms = []
    for k, r in enumerate(refs):
        ends = []
        for side in range(2):
            count, over = scal[2 + 4 * k + 2 * side], scal[3 + 4 * k + 2 * side]
            gap = r[2 * side : 2 * side + 1, cols] * over - center
            ends.append(gap * gap * count)
        terms.append((r[1:2, cols] + r[3:4, cols]) + (ends[0] + ends[1]))
    return center, lax.rsqrt(tree_sum(terms) / pixels + EPSILON)


def finish_sums(refs, cols=slice(None)):
    return (
        tree_sum([r[0:1, cols] + r[2:3, cols] for r in refs]),
        tree_sum([r[1:2, cols] + r[3:4, cols] for r in refs]),
    )


def put_moments(values, pay, cols, scal):
    weight = scal[0:1, cols]
    total = jnp.sum(values, axis=0, keepdims=True)
    off = values - total * (1.0 / values.shape[0])
    pay[0:1, cols] = total * weight
    pay[1:2, cols] = jnp.sum(off * off, axis=0, keepdims=True) * weight


def project(left, weights, pre, pay, scal, add=None):
    weights = weights.ready() if isinstance(weights, Far) else weights
    for start in range(0, pre.shape[1], COLS):
        cols = slice(start, start + COLS)
        out = dot(left[...], weights[:, cols])
        if add is not None:
            out = out + add[:, cols]
        pre[:, cols] = out
        put_moments(out, pay, cols, scal)


def fold(values):
    return jnp.sum(values.reshape(-1, 8, values.shape[-1]), axis=0)


def push(grad_of, pre, center, rstd, gain, offset, pushed, pay):
    def body(rows, sums):
        unit = (pre[rows, :].astype(F32) - center) * rstd
        out = grad_of(rows) * mish_slope(unit * gain + offset)
        pushed[rows, :] = out
        return sums[0] + fold(out), sums[1] + fold(out * unit)

    zero = jnp.zeros((8, pre.shape[1]), F32)
    first, second = rows_loop(pre.shape[0], body, (zero, zero), 16)
    pay[0:1, :] = jnp.sum(first, axis=0, keepdims=True)
    pay[1:2, :] = jnp.sum(second, axis=0, keepdims=True)


def settle(scal, refs, pushed, pre, coef, gain, out, sums):
    first, second = finish_sums(refs)
    sums[0:1, :] = first
    sums[1:2, :] = second
    width = pre.shape[1]
    over = 1.0 / scal[1:2, 0:width]
    center, rstd = coef[0:1, :], coef[1:2, :]
    scale = gain * rstd * scal[0:1, 0:width]
    level, tilt = first * over, second * over * rstd

    def body(rows, _):
        x = pre[rows, :].astype(F32) - center
        out[rows, :] = (scale * (pushed[rows, :] - level - x * tilt)).astype(BF)

    rows_loop(pre.shape[0], body)


def own_core():
    return lax.rem(lax.axis_index("rows"), 2)


def own_chip():
    return lax.div(lax.axis_index("rows"), 2)


def image_row(step, side):
    return 2 * (own_chip() ^ step) + (own_core() ^ side)


def put_scalars(cells, counts, scal):
    groups = counts.shape[0]
    core, batch = own_core(), lax.axis_index("batch")
    total = counts[0]
    for k in range(1, groups):
        total = total + counts[k]

    def put(k, value):
        scal[k : k + 1, :] = jnp.full((1, scal.shape[1]), value, F32)

    put(0, (core < counts[batch]).astype(F32))
    put(1, total.astype(F32) * cells)
    for step in range(groups):
        own = counts[batch ^ step]
        for side, slot in enumerate((core, 1 - core)):
            valid = (slot < own).astype(F32)
            put(2 + 4 * step + 2 * side, valid * cells)
            put(3 + 4 * step + 2 * side, valid * (1.0 / cells) + (1.0 - valid))


def shifted_row(both):
    half = both.shape[1] // 2
    odd = both[:, half:].astype(F32)
    first = lax.broadcasted_iota(jnp.int32, odd.shape, 0) == 0
    before = jnp.where(first, 0.0, pltpu.roll(odd, 1, 0)).astype(BF)
    return jnp.concatenate([before, both], axis=1)


def row_of_slots(values):
    return jnp.concatenate([shifted_row(values[slot]) for slot in range(values.shape[0])], axis=0)


def streamed(w, rows, held, semaphores):
    count, wide = held.shape[0], held.shape[-1]
    copies = [
        pltpu.make_async_copy(w.at[rows, :, n * wide : (n + 1) * wide], held.at[n], semaphores.at[n])
        for n in range(count)
    ]
    for copy in copies[:2]:
        copy.start()
    for n in range(count):
        copies[n].wait()
        if n + 2 < count:
            copies[n + 2].start()
        yield slice(n * wide, (n + 1) * wide), held.at[n]


def own_kernel(x, w, part, held, semaphores):
    blocks = streamed(w, slice(1, 3), held, semaphores)
    cols, block = next(blocks)
    lefts = [row_of_slots(x[:, row]) for row in range(2)]
    while cols is not None:
        part[:, cols] = dot(lefts[0], block[0]) + dot(lefts[1], block[1])
        cols, block = next(blocks, (None, None))


def above_kernel(above, part, w, rows, held, semaphores):
    cells = above.shape[1]
    blocks = streamed(w, slice(0, 1), held, semaphores)
    cols, block = next(blocks)
    left = row_of_slots(above[...])
    while cols is not None:
        out = part[:, cols] + dot(left, block[0])
        for slot in range(above.shape[0]):
            rows[slot, :, cols] = out[slot * cells : (slot + 1) * cells].astype(BF)
        cols, block = next(blocks, (None, None))


def whole_kernel(counts, *rest):
    parts, (down_pre, keep, pay, scal, semaphore) = rest[:-5], rest[-5:]
    put_scalars(down_pre.shape[0], counts, scal)
    total = jnp.zeros((8, down_pre.shape[1]), F32)
    for k, part in enumerate(parts):
        width = part.shape[0] // 2
        for side in range(2):
            start = image_row(k, side) * width

            def body(index, total, part=part, side=side, start=start, width=width):
                src = pl.ds(pl.multiple_of(side * width + index * CHUNK, CHUNK), CHUNK)
                dst = pl.ds(pl.multiple_of(start + index * CHUNK, CHUNK), CHUNK)
                down_pre[dst, :] = part[src, :]
                return total + fold(part[src, :].astype(F32))

            total = lax.fori_loop(0, width // CHUNK, body, total)
    copy = pltpu.make_async_copy(down_pre, keep, semaphore)
    copy.start()
    total = jnp.sum(total, axis=0, keepdims=True)
    mean = total * (1.0 / down_pre.shape[0])

    def spread(rows, squares):
        off = down_pre[rows, :].astype(F32) - mean
        return squares + fold(off * off)

    squares = rows_loop(down_pre.shape[0], spread, jnp.zeros((8, down_pre.shape[1]), F32))
    pay[0:1, :] = total * scal[0:1, :]
    pay[1:2, :] = jnp.sum(squares, axis=0, keepdims=True) * scal[0:1, :]
    copy.wait()


def main_kernel(groups, scal, *rest):
    refs = rest[:groups]
    down_pre, params, w_main, sectioned, main_pre, main_keep, pay, coef, semaphore = rest[groups:]
    center, rstd = finish_moments(scal, refs)
    coef[0:1, :] = center
    coef[1:2, :] = rstd
    scale, offset = rstd * row_of(params, GAIN_WIDE, 0), row_of(params, SHIFT_WIDE, 0)

    def body(rows, _):
        value = (down_pre[rows, :].astype(F32) - center) * scale + offset
        sectioned[rows, :] = mish(value).astype(BF)

    rows_loop(down_pre.shape[0], body)
    project(sectioned, w_main, main_pre, pay, scal)
    copy = pltpu.make_async_copy(main_pre, main_keep, semaphore)
    copy.start()
    copy.wait()


def short_kernel(scal, sectioned, w_short, short_pre, pay):
    project(sectioned, w_short, short_pre, pay, scal)


def inner_kernel(groups, scal, *rest):
    refs = rest[:groups]
    pre, params, w_inner, mainline, inner_pre, pay, coef = rest[groups:]
    half = pre.shape[1]
    center, rstd = finish_moments(scal, refs)
    coef[0:1, :] = center
    coef[1:2, :] = rstd
    scale, offset = rstd * row_of(params, GAIN, 1, half), row_of(params, SHIFT, 1, half)

    def body(rows, _):
        mainline[rows, :] = mish((pre[rows, :] - center) * scale + offset).astype(BF)

    rows_loop(pre.shape[0], body)
    project(mainline, w_inner, inner_pre, pay, scal)


def three_shifts(values, rim, start, forward):
    width, half = values.shape
    place = lax.broadcasted_iota(jnp.int32, values.shape, 0)
    before = jnp.where(place == 0, 0.0, pltpu.roll(values, 1, 0)).astype(BF)
    after = jnp.where(place == width - 1, 0.0, pltpu.roll(values, width - 1, 0)).astype(BF)
    sides = (before, after) if forward else (after, before)
    rows = pl.ds(start, width)
    rim[rows, 0:half] = sides[0]
    rim[rows, half : 2 * half] = values.astype(BF)
    rim[rows, 2 * half : 3 * half] = sides[1]


def spatial_kernel(groups, width, scal, *rest):
    refs = rest[:groups]
    pre, params, w_spatial, rim, spatial_pre, pay, coef = rest[groups:]
    cells, half = pre.shape
    center, rstd = finish_moments(scal, refs)
    coef[0:1, :] = center
    coef[1:2, :] = rstd
    scale, offset = rstd * row_of(params, GAIN, 2, half), row_of(params, SHIFT, 2, half)
    blank = jnp.zeros((width, 3 * half), BF)
    rim[0:width, :] = blank
    rim[width + cells :, :] = blank

    def body(index, _):
        start = pl.multiple_of(index * width, width)
        act = mish((pre[pl.ds(start, width), :] - center) * scale + offset)
        three_shifts(act, rim, pl.multiple_of(start + width, width), True)

    lax.fori_loop(0, cells // width, body, None)
    w_spatial = w_spatial.ready()
    for begin in range(0, half, COLS):
        cols = slice(begin, begin + COLS)
        out = sum(
            dot(
                rim[i * width : i * width + cells, :],
                w_spatial[i * 3 * half : (i + 1) * 3 * half, cols],
            )
            for i in range(3)
        )
        spatial_pre[:, cols] = out
        put_moments(out, pay, cols, scal)


def trans_kernel(groups, scal, *rest):
    refs = rest[:groups]
    pre, mainline, params, w_trans, merged, trans_pre, pay, coef = rest[groups:]
    half = pre.shape[1]
    center, rstd = finish_moments(scal, refs)
    coef[0:1, :] = center
    coef[1:2, :] = rstd
    scale, offset = rstd * row_of(params, GAIN, 3, half), row_of(params, SHIFT, 3, half)

    def body(rows, _):
        act = mish((pre[rows, :] - center) * scale + offset)
        merged[rows, :] = (mainline[rows, :].astype(F32) + act).astype(BF)

    rows_loop(pre.shape[0], body)
    project(merged, w_trans, trans_pre, pay, scal)


def shortcut_kernel(groups, scal, *rest):
    refs = rest[:groups]
    pre, params, w_unite, shortcut, part, coef = rest[groups:]
    half = pre.shape[1]
    center, rstd = finish_moments(scal, refs)
    coef[0:1, :] = center
    coef[1:2, :] = rstd
    scale, offset = rstd * row_of(params, GAIN, 0, half), row_of(params, SHIFT, 0, half)

    def body(rows, _):
        shortcut[rows, :] = mish((pre[rows, :] - center) * scale + offset).astype(BF)

    rows_loop(pre.shape[0], body)
    w_unite = w_unite.ready()
    for start in range(0, part.shape[1], COLS):
        cols = slice(start, start + COLS)
        part[:, cols] = dot(shortcut[...], w_unite[0:half, cols])


def unite_kernel(groups, scal, *rest):
    refs = rest[:groups]
    pre, part, params, w_unite, transition, unite_pre, pay, coef = rest[groups:]
    half = pre.shape[1]
    center, rstd = finish_moments(scal, refs)
    coef[0:1, :] = center
    coef[1:2, :] = rstd
    scale, offset = rstd * row_of(params, GAIN, 4, half), row_of(params, SHIFT, 4, half)

    def body(rows, _):
        transition[rows, :] = mish((pre[rows, :] - center) * scale + offset).astype(BF)

    rows_loop(pre.shape[0], body)
    project(transition, w_unite.ready().at[half:, :], unite_pre, pay, scal, part)


def turn_kernel(groups, pieces, scal, *rest):
    refs = rest[:groups]
    pre, params = rest[groups : groups + 2]
    parts = rest[groups + 2 : groups + 2 + pieces]
    pushed, *outputs, pay, coef = rest[groups + 2 + pieces :]
    center, rstd = finish_moments(scal, refs)
    coef[0:1, :] = center
    coef[1:2, :] = rstd
    gain, offset, weight = row_of(params, GAIN_WIDE, 1), row_of(params, SHIFT_WIDE, 1), scal[0:1, 0 : pre.shape[1]]
    sums = (jnp.zeros((8, pre.shape[1]), F32),) * 2
    for k, part in enumerate(parts):
        part = part.ready()
        width = part.shape[0] // 2
        for side in range(2):
            start = image_row(k, side) * width

            def body(index, sums, k=k, part=part, side=side, start=start, width=width):
                src = pl.ds(pl.multiple_of(side * width + index * 16, 16), 16)
                dst = pl.ds(pl.multiple_of(start + index * 16, 16), 16)
                unit = (pre[dst, :] - center) * rstd
                value = unit * gain + offset
                grown = jnp.exp(jnp.minimum(value, FAR))
                wide = grown * (grown + 2.0)
                share = 1.0 / (wide + 2.0)
                level = wide * share
                if k == 0:
                    rows = pl.ds(pl.multiple_of(index * 16, 16), 16)
                    outputs[side][rows, :] = (value * level * weight).astype(BF)
                slope = level + 4.0 * value * (grown * (grown + 1.0) * share) * share
                out = part[src, :].astype(F32) * weight * slope
                pushed[dst, :] = out
                return sums[0] + fold(out), sums[1] + fold(out * unit)

            sums = lax.fori_loop(0, width // 16, body, sums)
    pay[0:1, :] = jnp.sum(sums[0], axis=0, keepdims=True)
    pay[1:2, :] = jnp.sum(sums[1], axis=0, keepdims=True)


def back_trans_kernel(groups, scal, *rest):
    refs = rest[:groups]
    (
        unite_pushed, unite_pre, unite_coef, params, trans_pre, trans_coef, w_unite,
        grad_unite, sums, pushed, pay, scratch,
    ) = rest[groups:]
    half = trans_pre.shape[1]
    settle(scal, refs, unite_pushed, unite_pre, unite_coef, row_of(params, GAIN_WIDE, 1), grad_unite, sums)
    w_unite = w_unite.ready()
    for start in range(0, half, COLS):
        scratch[:, start : start + COLS] = dot_back(
            grad_unite[...], w_unite[half + start : half + start + COLS, :]
        )
    push(
        lambda rows: scratch[rows, :],
        trans_pre, trans_coef[0:1, :], trans_coef[1:2, :], row_of(params, GAIN, 4, half), row_of(params, SHIFT, 4, half),
        pushed, pay,
    )


def back_short_kernel(grad_unite, pre, coef, params, w_unite, pushed, pay, scratch):
    half = pre.shape[1]
    w_unite = w_unite.ready()
    for start in range(0, half, COLS):
        scratch[:, start : start + COLS] = dot_back(
            grad_unite[...], w_unite[start : start + COLS, :]
        )
    push(
        lambda rows: scratch[rows, :],
        pre, coef[0:1, :], coef[1:2, :], row_of(params, GAIN, 0, half), row_of(params, SHIFT, 0, half), pushed, pay,
    )


def back_spatial_kernel(groups, scal, *rest):
    refs = rest[:groups]
    (
        trans_pushed, trans_pre, trans_coef, spatial_pre, spatial_coef, params, w_trans,
        grad_trans, sums, grad_merged, pushed, pay,
    ) = rest[groups:]
    half = trans_pre.shape[1]
    settle(scal, refs, trans_pushed, trans_pre, trans_coef, row_of(params, GAIN, 4, half), grad_trans, sums)
    w_trans = w_trans.ready()
    for start in range(0, half, COLS):
        grad_merged[:, start : start + COLS] = dot_back(
            grad_trans[...], w_trans[start : start + COLS, :]
        )
    push(
        lambda rows: grad_merged[rows, :],
        spatial_pre, spatial_coef[0:1, :], spatial_coef[1:2, :], row_of(params, GAIN, 3, half), row_of(params, SHIFT, 3, half),
        pushed, pay,
    )


def back_inner_kernel(groups, width, scal, *rest):
    refs = rest[:groups]
    (
        spatial_pushed, spatial_pre, spatial_coef, inner_pre, inner_coef, params, w_spatial,
        grad_spatial, sums, pushed, pay, rim, scratch,
    ) = rest[groups:]
    cells, half = spatial_pre.shape
    settle(scal, refs, spatial_pushed, spatial_pre, spatial_coef, row_of(params, GAIN, 3, half), grad_spatial, sums)
    blank = jnp.zeros((width, 3 * half), BF)
    rim[0:width, :] = blank
    rim[width + cells :, :] = blank

    def body(index, _):
        start = pl.multiple_of(index * width, width)
        values = grad_spatial[pl.ds(start, width), :].astype(F32)
        three_shifts(values, rim, pl.multiple_of(start + width, width), False)

    lax.fori_loop(0, cells // width, body, None)
    w_spatial = w_spatial.ready()
    for start in range(0, half, COLS):
        scratch[:, start : start + COLS] = sum(
            dot_back(
                rim[(2 - i) * width : (2 - i) * width + cells, j * half : (j + 1) * half],
                w_spatial[(3 * i + j) * half + start : (3 * i + j) * half + start + COLS, :],
            )
            for i in range(3)
            for j in range(3)
        )
    push(
        lambda rows: scratch[rows, :],
        inner_pre, inner_coef[0:1, :], inner_coef[1:2, :], row_of(params, GAIN, 2, half), row_of(params, SHIFT, 2, half),
        pushed, pay,
    )


def back_main_kernel(groups, scal, *rest):
    refs = rest[:groups]
    (
        inner_pushed, inner_pre, inner_coef, grad_merged, main_pre, main_coef, params, w_inner,
        grad_inner, sums, pushed, pay, scratch,
    ) = rest[groups:]
    half = inner_pre.shape[1]
    settle(scal, refs, inner_pushed, inner_pre, inner_coef, row_of(params, GAIN, 2, half), grad_inner, sums)
    w_inner = w_inner.ready()
    for start in range(0, half, COLS):
        cols = slice(start, start + COLS)
        scratch[:, cols] = grad_merged[:, cols] + dot_back(grad_inner[...], w_inner[cols, :])
    push(
        lambda rows: scratch[rows, :],
        main_pre, main_coef[0:1, :], main_coef[1:2, :], row_of(params, GAIN, 1, half), row_of(params, SHIFT, 1, half),
        pushed, pay,
    )


def settle_short_kernel(groups, scal, *rest):
    refs = rest[:groups]
    pushed, pre, coef, params, grad_short, sums = rest[groups:]
    half = pre.shape[1]
    settle(scal, refs, pushed, pre, coef, row_of(params, GAIN, 0, half), grad_short, sums)


def back_down_kernel(groups, scal, *rest):
    refs = rest[:groups]
    (
        main_coef, down_coef, params, main_pushed, main_pre, w_main, grad_short, w_short, down_pre,
        grad_main, sums, pushed, pay, scratch,
    ) = rest[groups:]
    main_pushed, main_pre = main_pushed.ready(), main_pre.ready()
    half = main_pre.shape[1]
    settle(scal, refs, main_pushed, main_pre, main_coef, row_of(params, GAIN, 1, half), grad_main, sums)
    w_main, grad_short, w_short = w_main.ready(), grad_short.ready(), w_short.ready()
    for start in range(0, pushed.shape[1], COLS):
        cols = slice(start, start + COLS)
        scratch[:, cols] = dot_back(grad_short[...], w_short[cols, :]) + dot_back(
            grad_main[...], w_main[cols, :]
        )
    push(
        lambda rows: scratch[rows, :],
        down_pre.ready(), down_coef[0:1, :], down_coef[1:2, :],
        row_of(params, GAIN_WIDE, 0), row_of(params, SHIFT_WIDE, 0),
        pushed, pay,
    )


def settle_down_kernel(groups, scal, *rest):
    refs = rest[:groups]
    pushed, pre, coef, params, grad_down, sums = rest[groups:]
    settle(scal, refs, pushed, pre, coef, row_of(params, GAIN_WIDE, 0), grad_down, sums)
    cells = pre.shape[0]
    grad_down[cells:, :] = jnp.zeros((grad_down.shape[0] - cells, pre.shape[1]), BF)


def cut_down_kernel(groups, scal, *rest):
    refs = rest[:groups]
    pushed, pre, coef, params, cut = rest[groups:]
    width = cut.shape[1]
    cols = pl.ds(pl.multiple_of(own_chip() * width, width), width)
    first, second = finish_sums(refs, cols)
    over = 1.0 / scal[1:2, 0:width]
    center, rstd = coef[0:1, cols], coef[1:2, cols]
    scale = params[GAIN_WIDE : GAIN_WIDE + 1, cols] * rstd * scal[0:1, 0:width]
    level, tilt = first * over, second * over * rstd

    def body(rows, _):
        x = pre[rows, cols].astype(F32) - center
        cut[rows, :] = (scale * (pushed[rows, cols] - level - x * tilt)).astype(BF)

    rows_loop(pre.shape[0], body)


def by_place(first, second):
    low = own_core() == 0
    return jnp.where(low, first, second), jnp.where(low, second, first)


def share_unite_kernel(shortcut, transition, grad, mine, other):
    width = 2 * mine.shape[1]
    cut = grad[:, pl.ds(pl.multiple_of(own_chip() * width, width), width)]
    half = shortcut.shape[1]
    for k, values in enumerate((shortcut, transition)):
        out = dot_cells(values[...], cut)
        near, far = by_place(out[:, : width // 2], out[:, width // 2 :])
        mine[k * half : (k + 1) * half, :] = near.astype(BF)
        other[k * half : (k + 1) * half, :] = far.astype(BF)


def put_halves(cut, values, start, mine, other):
    out = dot_cells(cut, values)
    rows, cols = mine.shape[0], slice(start, start + out.shape[1])
    near, far = by_place(out[:rows], out[rows:])
    mine[:, cols] = near.astype(BF)
    other[:, cols] = far.astype(BF)


def chip_columns(mine):
    width = 2 * mine.shape[0]
    return pl.ds(pl.multiple_of(own_chip() * width, width), width)


def share_pack_kernel(*rest):
    pairs, (mine, other) = rest[:-2], rest[-2:]
    cols = chip_columns(mine)
    start = 0
    for values, grad in zip(pairs[::2], pairs[1::2]):
        put_halves(grad[:, cols], values[...], start, mine, other)
        start += values.shape[1]


def share_spatial_kernel(cells, rim, grad, mine, other):
    cut = grad[:, chip_columns(mine)]
    line, side = (rim.shape[0] - cells) // 2, rim.shape[1]
    for row in range(3):
        put_halves(cut, rim[row * line : row * line + cells, :], row * side, mine, other)


def share_main_kernel(grad, grad_inner, sectioned, mainline, mine, other):
    cols = chip_columns(mine)
    sectioned, mainline = sectioned.ready(), mainline.ready()
    put_halves(grad[:, cols], sectioned[...], 0, mine, other)
    put_halves(grad_inner[:, cols], mainline[...], sectioned.shape[1], mine, other)


def finish_kernel(unite, pack, taps, *rest):
    mains, (w_unite, w_short, w_trans, w_inner, w_spatial, w_main) = rest[:-6], rest[-6:]
    w_unite[...] = unite[...].astype(F32)
    for outs, values in (
        ((w_short, w_trans), pack[...].astype(F32)),
        ((w_main, w_inner), tree_sum([main[...].astype(F32) for main in mains])),
    ):
        start = 0
        for out in outs:
            out[...] = values[:, start : start + out.shape[1]]
            start += out.shape[1]
    half = w_trans.shape[1]
    for tap in range(w_spatial.shape[0]):
        w_spatial[tap] = taps[:, tap * half : (tap + 1) * half].astype(F32)


def norm_sums_kernel(wide_count, *refs):
    sums, outs = refs[:-4], refs[-4:]
    for k, pair in enumerate(sums):
        index = k if k < wide_count else k - wide_count
        for row, out in ((1, outs[0 if k < wide_count else 1]), (0, outs[2 if k < wide_count else 3])):
            out[index : index + 1, :] = pair[row : row + 1, :]


def share_down_kernel(steps, chips, width, last_call, *rest):
    grads = rest[: len(steps)]
    earlier = rest[len(steps) : len(steps) + 2 * last_call]
    rest = rest[len(steps) + 2 * last_call :]
    source, outs, rest = rest[0], rest[1:3], rest[3:]
    if last_call:
        odd_acc, even_acc = rest[:2]
        rest = rest[2:]
    else:
        odd_acc, even_acc = outs
    padded, sides, held, semaphores = rest
    cells, columns = grads[0].shape
    half = source.shape[-1] // 2
    planes = source.shape[0] // (2 * chips)
    copies = []
    for k, step in enumerate(steps):
        plane = lax.axis_index("batch") ^ step
        copies.append(
            [
                pltpu.make_async_copy(
                    source.at[row * planes + plane, own_core()], held.at[k, row], semaphores.at[k, row]
                )
                for row in range(2 * chips)
            ]
        )
        for copy in copies[-1]:
            copy.start()
    padded[cells:, :] = jnp.zeros((padded.shape[0] - cells, columns), BF)
    last = lax.broadcasted_iota(jnp.int32, (width, columns), 0) == width - 1

    def ahead(values):
        return jnp.where(last, 0.0, pltpu.roll(values.astype(F32), width - 1, 0)).astype(BF)

    for k in range(len(steps)):
        padded[0:cells, :] = grads[k][...]
        for block in range(2 * chips):
            rows = slice(block * width, (block + 1) * width)
            here = padded[rows, :]
            upper = padded[(block + 1) * width : (block + 2) * width, :]
            sides[rows, 0:columns] = upper
            sides[rows, columns : 2 * columns] = here
            sides[rows, 2 * columns : 3 * columns] = ahead(here)
            sides[rows, 3 * columns : 4 * columns] = ahead(upper)
        for copy in copies[k]:
            copy.wait()

        def add(which, side, start, values, k=k):
            rows, cols = slice(side * half, (side + 1) * half), slice(start, start + columns)
            acc = (even_acc, odd_acc)[which]
            if k > 0:
                values = values + acc[rows, cols]
            elif last_call:
                values = values + earlier[1 - which][rows, cols]
            acc[rows, cols] = values

        for which in range(2):
            for side in range(2):
                left = held[k, :, which, :, side * half : (side + 1) * half].reshape(cells, half)
                for block in range(4):
                    if (which == 0 and block in (0, 3)) or (side == 0 and block in (2, 3)):
                        continue
                    start = block * columns
                    add(which, side, start, dot_cells(left, sides[:, start : start + columns]))
    if not last_call:
        return
    mine, other = outs
    places = (
        (odd_acc, 1, 3), (odd_acc, 0, 0), (odd_acc, 1, 0),
        (even_acc, 1, 2), (even_acc, 0, 1), (even_acc, 1, 1),
        (odd_acc, 1, 2), (odd_acc, 0, 1), (odd_acc, 1, 1),
    )
    for tap, (acc, side, block) in enumerate(places):
        values = acc[side * half : (side + 1) * half, block * columns : (block + 1) * columns]
        near, far = by_place(values[:, : columns // 2], values[:, columns // 2 :])
        mine[tap * half : (tap + 1) * half, :] = near.astype(BF)
        other[tap * half : (tap + 1) * half, :] = far.astype(BF)


def back_input_kernel(width, grad, w, out, near, far):
    cells = 2 * width
    full = grad.shape[1]

    @pl.when(pl.program_id(0) == 0)
    def _():
        last = lax.broadcasted_iota(jnp.int32, (width, full), 0) == width - 1
        for block in range(3):
            start = pl.multiple_of(own_chip() * cells + block * width, width)
            values = grad[pl.ds(start, width), :]
            rows = slice(block * width, (block + 1) * width)
            near[rows, :] = values
            far[rows, :] = jnp.where(
                last, 0.0, pltpu.roll(values.astype(F32), width - 1, 0)
            ).astype(BF)

    low, high = slice(0, cells), slice(width, width + cells)

    def term(values, rows, i, j):
        return dot_back(values[rows, :], w[3 * i + j])

    def put(parity, column, values):
        for row in range(2):
            out[2 * row + parity, pl.ds(column, width, stride=2), :] = values[
                row * width : (row + 1) * width
            ]

    put(0, 0, term(near, low, 1, 1))
    put(0, 1, term(near, low, 1, 2) + term(far, low, 1, 0))
    put(1, 0, term(near, high, 0, 1) + term(near, low, 2, 1))
    put(
        1,
        1,
        term(near, high, 0, 2) + term(far, high, 0, 0) + term(near, low, 2, 2) + term(far, low, 2, 0),
    )


SMEM = pl.BlockSpec(memory_space=pltpu.SMEM)
VMEM = pl.BlockSpec(memory_space=pltpu.VMEM)
ANY = pl.BlockSpec(memory_space=pl.ANY)


def shape(dims, dtype=F32):
    return jax.ShapeDtypeStruct(dims, dtype)


def nbytes(dims, dtype):
    count = 1
    for d in dims:
        count *= d
    return count * jnp.dtype(dtype).itemsize


def in_vmem(value):
    return pltpu.with_memory_space_constraint(value, pltpu.VMEM)


def in_hbm(value):
    return pltpu.with_memory_space_constraint(value, pltpu.HBM)


LIGHT = pl.CostEstimate(flops=0, bytes_accessed=0, transcendentals=0)


def call(kernel, name, scalars, near, outs, flops, scratch=(), far=(), pin=False, spill=(), light=False, out=(), late=False):
    moved = sum(nbytes(a.shape, a.dtype) for a in (*near, *far, *outs))
    scratch = [s if hasattr(s, "memory_space") or not hasattr(s, "shape") else pltpu.VMEM(s.shape, s.dtype) for s in scratch]
    held = moved + sum(nbytes(s.shape, s.dtype) for s in scratch if hasattr(s, "shape"))
    if pin:
        held -= moved - sum(nbytes(a.shape, a.dtype) for a in far)
        held += sum(nbytes(outs[k].shape, outs[k].dtype) for k in spill)
        near, far = [in_vmem(a) for a in near], [in_hbm(a) for a in far]
        outs = [
            o if k in spill else (pltpu.HBM if k in out else pltpu.VMEM)(o.shape, o.dtype)
            for k, o in enumerate(outs)
        ]
    before, after_far, last = len(scalars) + len(near), len(far), len(outs) + len(scratch)

    def body(*refs):
        sources, rest = refs[before : before + after_far], refs[before + after_far :]
        targets = rest[last : last + after_far]
        fars = [Far(a, b, rest[-1].at[k]) for k, (a, b) in enumerate(zip(sources, targets))]
        kernel(*refs[:before], *fars, *rest[:last])
        for one in fars:
            one.ready()

    return pl.pallas_call(
        body if far else kernel,
        name=name,
        out_shape=tuple(outs),
        in_specs=[SMEM] * len(scalars) + [VMEM] * len(near) + [ANY] * len(far),
        out_specs=tuple(ANY if k in out and not late else VMEM for k in range(len(outs))),
        scratch_shapes=scratch
        + [pltpu.VMEM(a.shape, a.dtype) for a in far]
        + ([pltpu.SemaphoreType.DMA((len(far),))] if far else []),
        compiler_params=pltpu.CompilerParams(vmem_limit_bytes=held + (8 << 20)),
        cost_estimate=LIGHT if light else pl.CostEstimate(flops=flops, bytes_accessed=moved, transcendentals=0),
    )(*scalars, *near, *far)


def first_conv(view, above, w_down, pin):
    slots, _, cells, both = view.shape
    half = both // 2
    full = w_down.shape[-1]
    taps = w_down.reshape(3, 3 * half, full)
    if pin:
        view, above, taps = in_vmem(view), in_vmem(above), in_hbm(taps)
    wide = 256
    count = full // wide

    def run(kernel, name, rows, values, out):
        return pl.pallas_call(
            kernel,
            name=name,
            out_shape=(pltpu.VMEM if pin else shape)(out.shape, out.dtype),
            in_specs=[VMEM] * len(values) + [ANY],
            out_specs=VMEM,
            scratch_shapes=[
                pltpu.VMEM((count, rows, 3 * half, wide), BF), pltpu.SemaphoreType.DMA((count,))
            ],
            compiler_params=pltpu.CompilerParams(vmem_limit_bytes=24 << 20),
            cost_estimate=pl.CostEstimate(
                flops=6 * rows * slots * cells * half * full,
                bytes_accessed=6 * rows * half * full,
                transcendentals=0,
            ),
        )(*values, taps)

    part = run(own_kernel, "own", 2, [view], shape((slots * cells, full)))
    part = in_vmem(part) if pin else part
    return run(above_kernel, "above", 1, [above, part], shape((slots, cells, full), BF))


def flipped(kernel):
    return jnp.swapaxes(jnp.flip(kernel, (0, 1)), 2, 3)


def on_device(
    inputs,
    image_counts,
    w_down,
    w_short,
    w_main,
    w_inner,
    w_spatial,
    w_trans,
    w_unite,
    gains_wide,
    gains_narrow,
    shifts_wide,
    shifts_narrow,
    grad_output,
):
    half = w_short.shape[1]
    full = 2 * half
    slots, height_dev, width, _ = grad_output.shape
    here = Plane()
    wide = here.chips == 4 and half % (128 * here.chips) == 0
    stage = functools.partial(call, pin=wide)
    groups, chips = here.groups, here.chips
    height = here.rows * height_dev
    cells = height * width
    batch = lax.axis_index("batch")
    view = inputs.reshape(slots, 2, width, 2 * half)
    below = [(i, i + 1) for i in range(here.rows - 1)]
    above = lax.ppermute(view[:, 1], "rows", below)
    params = jnp.concatenate(
        [gains_wide, shifts_wide]
        + [jnp.pad(p, ((0, 0), (0, half))) for p in (gains_narrow, shifts_narrow)]
    )
    down_rows = first_conv(view, above, w_down, wide)
    down_pieces = here.pieces(*here.split(down_rows))
    grad_mine, grad_other = here.split(grad_output.reshape(slots, width, full))
    down_pieces[1], params, grad_mine, grad_other = lax.optimization_barrier(
        (down_pieces[1], params, grad_mine, grad_other)
    )
    down_pre, down_keep, down_pay, scal = stage(
        whole_kernel,
        "whole",
        [image_counts],
        down_pieces,
        [
            shape((cells, full), BF), shape((cells, full), BF), shape((2, full)),
            shape((2 + 4 * groups, full)),
        ],
        10 * cells * full,
        out=(1,),
        scratch=[pltpu.SemaphoreType.DMA],
    )
    if wide:
        flat = after(view, down_pay).reshape(slots * 2 * width, 2 * half)
        source = lax.all_gather(flat, ("rows", "batch")).reshape(-1, *view.shape)
        grad_piece = jnp.concatenate([grad_mine, here.swap(after(grad_other, down_pay))], axis=0)
        grad_pieces = [grad_piece, here.chip_hop(grad_piece, 1), here.chip_hop(grad_piece, 2)]
        grad_pieces.append(here.chip_hop(grad_pieces[1], 2))
    else:
        grad_pieces = here.pieces(grad_mine, grad_other)
    sectioned, main_pre, main_keep, main_pay, down_coef = stage(
        functools.partial(main_kernel, groups),
        "main",
        [],
        [scal, *here.everywhere(down_pay), down_pre, params],
        [
            shape((cells, full), BF), shape((cells, half)), shape((cells, half)),
            shape((2, half)), shape((2, full)),
        ],
        2 * cells * full * half,
        far=[w_main],
        out=(2,),
        scratch=[pltpu.SemaphoreType.DMA],
    )

    if wide:
        main_pay = after(main_pay, *grad_pieces[:3])
    main_all = here.everywhere(main_pay)
    short_pre, short_pay = stage(
        short_kernel,
        "short",
        [],
        [scal, sectioned],
        [shape((cells, half)), shape((2, half))],
        2 * cells * full * half,
        far=[w_short],
    )
    mainline, inner_pre, inner_pay, main_coef = stage(
        functools.partial(inner_kernel, groups),
        "inner",
        [],
        [scal, *main_all, main_pre, params],
        [shape((cells, half), BF), shape((cells, half)), shape((2, half)), shape((2, half))],
        2 * cells * half * half,
        far=[w_inner],
    )
    inner_all = here.everywhere(inner_pay)
    rim, spatial_pre, spatial_pay, inner_coef = stage(
        functools.partial(spatial_kernel, groups, width),
        "spatial",
        [],
        [scal, *inner_all, inner_pre, params],
        [
            shape((cells + 2 * width, 3 * half), BF), shape((cells, half)),
            shape((2, half)), shape((2, half)),
        ],
        18 * cells * half * half,
        far=[w_spatial.reshape(9 * half, half)],
    )
    if wide:
        spatial_pay = after(spatial_pay, grad_pieces[3])
    both_all = here.everywhere(jnp.concatenate([spatial_pay, short_pay], axis=1))
    spatial_all = [b[:, :half] for b in both_all]
    short_all = [b[:, half:] for b in both_all]
    merged, trans_pre, trans_pay, spatial_coef = stage(
        functools.partial(trans_kernel, groups),
        "trans",
        [],
        [scal, *spatial_all, spatial_pre, mainline, params],
        [shape((cells, half), BF), shape((cells, half)), shape((2, half)), shape((2, half))],
        2 * cells * half * half,
        far=[w_trans],
    )
    trans_all = here.everywhere(trans_pay)
    shortcut, unite_part, short_coef = stage(
        functools.partial(shortcut_kernel, groups),
        "shortcut",
        [],
        [scal, *short_all, short_pre, params],
        [shape((cells, half), BF), shape((cells, full)), shape((2, half))],
        2 * cells * half * full,
        far=[w_unite],
    )
    transition, unite_pre, unite_pay, trans_coef = stage(
        functools.partial(unite_kernel, groups),
        "unite",
        [],
        [scal, *trans_all, trans_pre, unite_part, params],
        [shape((cells, half), BF), shape((cells, full)), shape((2, full)), shape((2, half))],
        2 * cells * half * full,
        far=[w_unite],
    )
    unite_all = here.everywhere(unite_pay)
    unite_pushed, mine, other, unite_pay, unite_coef = stage(
        functools.partial(turn_kernel, groups, chips),
        "turn",
        [],
        [scal, *unite_all, unite_pre, params],
        [
            shape((cells, full)), shape((width, full), BF), shape((width, full), BF),
            shape((2, full)), shape((2, full)),
        ],
        40 * cells * full,
        far=grad_pieces,
        spill=(1, 2),
    )
    output_rows = (mine, here.swap(other))

    unite_all = here.everywhere(unite_pay)
    grad_unite_pre, unite_sums, trans_pushed, trans_pay = stage(
        functools.partial(back_trans_kernel, groups),
        "back_trans",
        [],
        [scal, *unite_all, unite_pushed, unite_pre, unite_coef, params, trans_pre, trans_coef],
        [shape((cells, full), BF), shape((2, full)), shape((cells, half)), shape((2, half))],
        2 * cells * half * full,
        [shape((cells, half))],
        far=[w_unite],
    )
    trans_all = here.everywhere(trans_pay)
    if wide:

        def of_pair(pair):
            mine, other = pair
            return (mine.astype(F32) + here.swap(other).astype(F32)).astype(BF)

        share_unite = of_pair(
            stage(
                share_unite_kernel,
                "share_unite",
                [],
                [shortcut, transition, grad_unite_pre],
                [shape((full, full // chips // 2), BF)] * 2,
                2 * cells * full * full // chips,
            )
        )
    short_pushed, short_pay = stage(
        back_short_kernel,
        "back_short",
        [],
        [grad_unite_pre, short_pre, short_coef, params],
        [shape((cells, half)), shape((2, half))],
        2 * cells * half * full,
        [shape((cells, half))],
        far=[w_unite],
    )
    grad_trans_pre, trans_sums, grad_merged, spatial_pushed, spatial_pay = stage(
        functools.partial(back_spatial_kernel, groups),
        "back_spatial",
        [],
        [scal, *trans_all, trans_pushed, trans_pre, trans_coef, spatial_pre, spatial_coef, params],
        [
            shape((cells, half), BF), shape((2, half)), shape((cells, half)), shape((cells, half)),
            shape((2, half)),
        ],
        2 * cells * half * half,
        far=[w_trans],
    )
    both_all = here.everywhere(jnp.concatenate([spatial_pay, short_pay], axis=1))
    spatial_all = [b[:, :half] for b in both_all]
    short_all = [b[:, half:] for b in both_all]
    grad_spatial_pre, spatial_sums, inner_pushed, inner_pay = stage(
        functools.partial(back_inner_kernel, groups, width),
        "back_inner",
        [],
        [scal,
            *spatial_all, spatial_pushed, spatial_pre, spatial_coef, inner_pre, inner_coef, params,
        ],
        [shape((cells, half), BF), shape((2, half)), shape((cells, half)), shape((2, half))],
        18 * cells * half * half,
        [shape((cells + 2 * width, 3 * half), BF), shape((cells, half))],
        far=[w_spatial.reshape(9 * half, half)],
    )
    inner_all = here.everywhere(inner_pay)
    grad_short_pre, short_sums = stage(
        functools.partial(settle_short_kernel, groups),
        "settle_short",
        [],
        [scal, *short_all, short_pushed, short_pre, short_coef, params],
        [shape((cells, half), BF), shape((2, half))],
        10 * cells * half,
    )
    if wide:
        lean = half // chips // 2
        share_spatial = of_pair(
            stage(
                functools.partial(share_spatial_kernel, cells),
                "share_spatial",
                [],
                [rim, grad_spatial_pre],
                [shape((lean, 9 * half), BF)] * 2,
                18 * cells * half * half // chips,
            )
        )
        share_pack = of_pair(
            stage(
                share_pack_kernel,
                "share_pack",
                [],
                [sectioned, grad_short_pre, merged, grad_trans_pre],
                [shape((lean, full + half), BF)] * 2,
                6 * cells * half * half // chips,
            )
        )
        inner_all[0], source, *shares = lax.optimization_barrier(
            (inner_all[0], source, share_unite, share_pack, share_spatial)
        )
        shares = lax.psum(tuple(shares), "batch")
    grad_inner_pre, inner_sums, main_pushed, main_pay = stage(
        functools.partial(back_main_kernel, groups),
        "back_main",
        [],
        [scal, *inner_all, inner_pushed, inner_pre, inner_coef, grad_merged, main_pre, main_coef, params],
        [shape((cells, half), BF), shape((2, half)), shape((cells, half)), shape((2, half))],
        2 * cells * half * half,
        [shape((cells, half))],
        far=[w_inner],
        out=(2,),
        late=True,
    )
    main_all = here.everywhere(main_pay)
    grad_main_pre, main_sums, down_pushed, down_pay = stage(
        functools.partial(back_down_kernel, groups),
        "back_down",
        [],
        [scal, *main_all, main_coef, down_coef, params],
        [shape((cells, half), BF), shape((2, half)), shape((cells, full)), shape((2, full))],
        4 * cells * half * full,
        [shape((cells, full))],
        far=[main_pushed, main_keep, w_main, grad_short_pre, w_short, down_keep], light=True)
    down_all = here.everywhere(down_pay)
    spare = width
    if wide:
        grad_cut = stage(
            functools.partial(cut_down_kernel, groups),
            "cut_down",
            [],
            [scal, *down_all, down_pushed, down_pre, down_coef, params],
            [shape((cells, full // chips), BF)],
            10 * cells * full // chips, light=True)[0]
        cuts = here.plane_hops(grad_cut)
    grad_down_pre, down_sums = stage(
        functools.partial(settle_down_kernel, groups),
        "settle_down",
        [],
        [scal, *down_all, down_pushed, down_pre, down_coef, params],
        [shape((cells + spare, full), BF), shape((2, full))],
        10 * cells * full, light=True)
    output = jnp.stack(here.by_core(*after(output_rows, down_pay))).reshape(grad_output.shape)
    norm_grads = stage(
        functools.partial(norm_sums_kernel, 2),
        "norm_sums",
        [],
        [down_sums, unite_sums, short_sums, main_sums, inner_sums, spatial_sums, trans_sums],
        [shape((2, full)), shape((5, half))] * 2,
        0,
        spill=range(4), light=True)
    if wide:
        near = pl.pallas_call(
            functools.partial(back_input_kernel, width),
            name="back_input",
            grid=(half // 128,),
            out_shape=shape((4, 2 * width, half)),
            in_specs=[
                pl.BlockSpec((cells + spare, full), lambda n: (0, 0)),
                pl.BlockSpec((9, 128, full), lambda n: (0, n, 0)),
            ],
            out_specs=pl.BlockSpec((4, 2 * width, 128), lambda n: (0, 0, n)),
            scratch_shapes=[pltpu.VMEM((3 * width, full), BF)] * 2,
            compiler_params=pltpu.CompilerParams(vmem_limit_bytes=16 << 20),
            cost_estimate=LIGHT,
        )(grad_down_pre, in_hbm(w_down.reshape(9, half, full)))
        share_main = of_pair(
            stage(
                share_main_kernel,
                "share_main",
                [],
                [grad_main_pre, grad_inner_pre],
                [shape((lean, full + half), BF)] * 2,
                6 * cells * half * half // chips,
                far=[sectioned, mainline],
                light=True,
            )
        )
        mine, other = here.split(near.reshape(2, 2, 2 * width, half))
        grad_inputs = jnp.stack(here.by_core(mine, here.swap(other)))
        columns = full // chips
        sums_here = [shape((full, 4 * columns)), shape((full, 4 * columns))]
        halves = [shape((9 * half, columns // 2), BF)] * 2

        def share_down(steps, earlier):
            outs = halves if earlier else sums_here
            near = [*(cuts[step] for step in steps), *earlier]
            scratch = [
                pltpu.VMEM((cells + spare, columns), BF),
                pltpu.VMEM((cells, 4 * columns), BF),
                pltpu.VMEM((len(steps), 2 * chips, 2, width, full), BF),
                pltpu.SemaphoreType.DMA((len(steps), 2 * chips)),
            ]
            if earlier:
                scratch = [pltpu.VMEM(a.shape, F32) for a in sums_here] + scratch
            return pl.pallas_call(
                functools.partial(share_down_kernel, steps, chips, width, int(bool(earlier))),
                name="share_down",
                out_shape=tuple(pltpu.VMEM(o.shape, o.dtype) for o in outs),
                in_specs=[VMEM] * len(near) + [ANY],
                out_specs=(VMEM,) * len(outs),
                scratch_shapes=scratch,
                compiler_params=pltpu.CompilerParams(vmem_limit_bytes=30 << 20),
                cost_estimate=LIGHT,
            )(*map(in_vmem, near), in_hbm(source))

        middle = (groups + 1) // 2
        cuts[:middle], near = lax.optimization_barrier((cuts[:middle], near))
        first_sums = share_down(range(middle), ())
        mains = here.plane_hops(after(share_main, grad_cut))
        cuts[middle:], first_sums = lax.optimization_barrier((cuts[middle:], first_sums))
        mine, other = share_down(range(middle, groups), first_sums)
        other, *tied = lax.optimization_barrier((other, *shares, *mains))
        shares, mains = tied[: len(shares)], tied[len(shares) :]
        grad_w_down = mine.astype(F32) + here.swap(other).astype(F32)
        early = stage(
            finish_kernel,
            "finish",
            [],
            [*shares, *mains],
            [
                shape((full, 2 * lean)), shape((lean, full)), shape((lean, half)), shape((lean, half)),
                shape((9, lean, half)), shape((lean, full)),
            ],
            0,
            spill=range(6), light=True)
        early = [
            early[1].T, early[5].T, early[3].T, jnp.swapaxes(early[4], 1, 2), early[2].T, early[0],
        ]
    else:
        grad_down_pre = grad_down_pre[:cells]
        def share(values, grad):
            columns = grad.shape[1] // chips
            grad = lax.dynamic_slice_in_dim(grad, here.chip * columns, columns, 1)
            part = jnp.concatenate([dot_cells(v, grad) for v in values], axis=0)
            mine, other = here.split(part.reshape(part.shape[0], 2, columns // 2), 1)
            return (mine + here.swap(other.astype(BF)).astype(F32)).astype(BF)

        windows = [rim[i * width : i * width + cells] for i in range(3)]
        early = lax.psum(
            (
                share([sectioned], grad_short_pre),
                share([sectioned], grad_main_pre),
                share([mainline], grad_inner_pre),
                share(windows, grad_spatial_pre),
                share([merged], grad_trans_pre),
                jnp.concatenate([share([shortcut], grad_unite_pre), share([transition], grad_unite_pre)]),
            ),
            "batch",
        )
        early = [e.astype(F32) for e in early]

        mine, other = here.split(view)
        got = here.chip_hops(jnp.stack([mine, here.swap(other)], axis=1))
        source = jnp.zeros((2, here.rows, width, full), BF)
        for step, piece in enumerate(got):
            for side in range(2):
                source = lax.dynamic_update_slice_in_dim(
                    source, piece[:, side : side + 1], 2 * (here.chip ^ step) + (here.core ^ side), 1
                )
        grad_map = grad_down_pre.reshape(height, width, full)
        columns = full // chips
        grad_cut = lax.dynamic_slice_in_dim(grad_map, here.chip * columns, columns, 2)
        ahead = jnp.pad(grad_cut[:, 1:], ((0, 0), (0, 1), (0, 0)))
        upper = jnp.pad(grad_cut[1:], ((0, 1), (0, 0), (0, 0)))
        both_ahead = jnp.pad(ahead[1:], ((0, 1), (0, 0), (0, 0)))
        even_rows = source[0].reshape(cells, full)
        odd_rows = source[1].reshape(cells, full)

        def taps_of(rows, here_grad, ahead_grad):
            plain = dot_cells(rows, here_grad.reshape(cells, columns))
            before = dot_cells(rows[:, half:], ahead_grad.reshape(cells, columns))
            return [before, plain]

        part = jnp.concatenate(
            taps_of(odd_rows, upper, both_ahead)
            + taps_of(even_rows, grad_cut, ahead)
            + taps_of(odd_rows, grad_cut, ahead),
            axis=0,
        )
        mine, other = here.split(part.reshape(9 * half, 2, columns // 2), 1)
        part = (mine + here.swap(other.astype(BF)).astype(F32)).astype(BF)
        grad_w_down = lax.psum(part, "batch").astype(F32)

        pair_rows = 2 * height_dev
        grad_image = jnp.pad(grad_map, ((0, 1), (0, 0), (0, 0)))
        grad_block = lax.dynamic_slice_in_dim(grad_image, here.chip * pair_rows, pair_rows + 1, 0)
        widened = lax.conv_general_dilated(
            grad_block[None],
            flipped(w_down),
            (1, 1),
            ((1, 0), (1, 2)),
            lhs_dilation=(2, 2),
            dimension_numbers=("NHWC", "HWIO", "NHWC"),
            preferred_element_type=F32,
        )[0]
        mine = lax.dynamic_slice_in_dim(widened, here.core * pair_rows, pair_rows, 0)
        other = lax.dynamic_slice_in_dim(widened, (1 - here.core) * pair_rows, pair_rows, 0)
        grad_inputs = jnp.stack(here.by_core(mine, here.swap(other)))

    return (
        output,
        grad_inputs,
        grad_w_down.reshape(3, 3, half, -1),
        early[0],
        early[1],
        early[2],
        early[3].reshape(3, 3, half, -1),
        early[4],
        early[5],
        *norm_grads,
    )


def solution(mesh):
    placed = (P("batch", "rows", None, None),) + (P(),) * 12 + (P("batch", "rows", None, None),)
    return jax.shard_map(
        on_device,
        mesh=mesh,
        in_specs=placed,
        out_specs=(
            P("batch", "rows", None, None),
            P("batch", "rows", None, None),
            P(None, None, None, "rows"),
            P(None, "rows"),
            P(None, "rows"),
            P(None, "rows"),
            P(None, None, None, "rows"),
            P(None, "rows"),
            P(None, "rows"),
            P(),
            P(),
            P(),
            P(),
        ),
        check_vma=False,
    )
```

```python
import functools

import jax
import jax.numpy as jnp
from jax import lax
from jax.experimental import pallas as pl
from jax.experimental.pallas import tpu as pltpu
from jax.sharding import PartitionSpec as P

EPSILON = 1e-05
FAR = 20.0
CHUNK = 64
COLS = 256
BF = jnp.bfloat16
F32 = jnp.float32


def mish(values):
    grown = jnp.exp(jnp.minimum(values, FAR))
    wide = grown * (grown + 2.0)
    return values * (wide / (wide + 2.0))


def mish_slope(values):
    grown = jnp.exp(jnp.minimum(values, FAR))
    wide = grown * (grown + 2.0)
    share = 1.0 / (wide + 2.0)
    return wide * share + 4.0 * values * (grown * (grown + 1.0) * share) * share


def after(value, *others):
    return lax.optimization_barrier((value,) + others)[0]


def tree_sum(parts):
    while len(parts) > 1:
        parts = [parts[i] + parts[i + 1] for i in range(0, len(parts), 2)]
    return parts[0]


def dot(a, b):
    return jnp.dot(a, b, preferred_element_type=F32)


def dot_back(a, b):
    return lax.dot_general(a, b, (((1,), (1,)), ((), ())), preferred_element_type=F32)


def dot_cells(a, b):
    return lax.dot_general(a, b, (((0,), (0,)), ((), ())), preferred_element_type=F32)


class Plane:
    def __init__(self):
        self.rows = lax.axis_size("rows")
        self.groups = lax.axis_size("batch")
        self.chips = self.rows // 2
        self.place = lax.axis_index("rows")
        self.core = self.place % 2
        self.chip = self.place // 2

    def swap(self, value):
        return lax.ppermute(value, "rows", [(i, i ^ 1) for i in range(self.rows)])

    def chip_hops(self, value):
        return [value] + [
            lax.ppermute(value, "rows", [(i, i ^ (2 * step)) for i in range(self.rows)])
            for step in range(1, self.chips)
        ]

    def chip_hop(self, value, step):
        return lax.ppermute(value, "rows", [(i, i ^ (2 * step)) for i in range(self.rows)])

    def plane_hops(self, value):
        return [value] + [
            lax.ppermute(value, "batch", [(i, i ^ step) for i in range(self.groups)])
            for step in range(1, self.groups)
        ]

    def by_core(self, mine, got):
        first = self.core == 0
        return jnp.where(first, mine, got), jnp.where(first, got, mine)

    def split(self, block, axis=0):
        mine = lax.dynamic_index_in_dim(block, self.core, axis, keepdims=False)
        other = lax.dynamic_index_in_dim(block, 1 - self.core, axis, keepdims=False)
        return mine, other

    def pieces(self, mine, other):
        return self.chip_hops(jnp.concatenate([mine, self.swap(other)], axis=0))

    def plane_steps(self, value):
        found = {0: value}
        step = self.groups // 2
        while step:
            found |= {far + step: self.plane_hop(v, step) for far, v in found.items()}
            step //= 2
        return [found[k] for k in range(self.groups)]

    def plane_hop(self, value, step):
        return lax.ppermute(value, "batch", [(i, i ^ step) for i in range(self.groups)])

    def everywhere(self, pay):
        return self.plane_hops(jnp.concatenate([pay, self.swap(pay)], axis=0))


class Far:
    def __init__(self, source, target, semaphore):
        self.copy = pltpu.make_async_copy(source, target, semaphore)
        self.copy.start()
        self.target, self.waits = target, True

    def ready(self):
        if self.waits:
            self.copy.wait()
            self.waits = False
        return self.target


def rows_loop(total, body, carry=None, step=CHUNK):
    def turn(index, state):
        return body(pl.ds(pl.multiple_of(index * step, step), step), state)

    return lax.fori_loop(0, total // step, turn, carry, unroll=2)


GAIN_WIDE, SHIFT_WIDE, GAIN, SHIFT = 0, 2, 4, 9


def row_of(params, first, index, half=None):
    return params[first + index : first + index + 1, 0 : (half or params.shape[1])]


def finish_moments(scal, refs, cols=slice(None)):
    scal = [scal[k : k + 1, 0 : refs[0].shape[1]] for k in range(2 + 4 * len(refs))]
    pixels = scal[1]
    center = tree_sum([r[0:1, cols] + r[2:3, cols] for r in refs]) / pixels
    terms = []
    for k, r in enumerate(refs):
        ends = []
        for side in range(2):
            count, over = scal[2 + 4 * k + 2 * side], scal[3 + 4 * k + 2 * side]
            gap = r[2 * side : 2 * side + 1, cols] * over - center
            ends.append(gap * gap * count)
        terms.append((r[1:2, cols] + r[3:4, cols]) + (ends[0] + ends[1]))
    return center, lax.rsqrt(tree_sum(terms) / pixels + EPSILON)


def finish_sums(refs, cols=slice(None)):
    return (
        tree_sum([r[0:1, cols] + r[2:3, cols] for r in refs]),
        tree_sum([r[1:2, cols] + r[3:4, cols] for r in refs]),
    )


def put_moments(values, pay, cols, scal):
    weight = scal[0:1, cols]
    total = jnp.sum(values, axis=0, keepdims=True)
    off = values - total * (1.0 / values.shape[0])
    pay[0:1, cols] = total * weight
    pay[1:2, cols] = jnp.sum(off * off, axis=0, keepdims=True) * weight


def project(left, weights, pre, pay, scal, add=None):
    weights = weights.ready() if isinstance(weights, Far) else weights
    for start in range(0, pre.shape[1], COLS):
        cols = slice(start, start + COLS)
        out = dot(left[...], weights[:, cols])
        if add is not None:
            out = out + add[:, cols]
        pre[:, cols] = out
        put_moments(out, pay, cols, scal)


def fold(values):
    return jnp.sum(values.reshape(-1, 8, values.shape[-1]), axis=0)


def push(grad_of, pre, center, rstd, gain, offset, pushed, pay):
    def body(rows, sums):
        unit = (pre[rows, :].astype(F32) - center) * rstd
        out = grad_of(rows) * mish_slope(unit * gain + offset)
        pushed[rows, :] = out
        return sums[0] + fold(out), sums[1] + fold(out * unit)

    zero = jnp.zeros((8, pre.shape[1]), F32)
    first, second = rows_loop(pre.shape[0], body, (zero, zero), 32)
    pay[0:1, :] = jnp.sum(first, axis=0, keepdims=True)
    pay[1:2, :] = jnp.sum(second, axis=0, keepdims=True)


def settle(scal, refs, pushed, pre, coef, gain, out, sums):
    first, second = finish_sums(refs)
    sums[0:1, :] = first
    sums[1:2, :] = second
    width = pre.shape[1]
    over = 1.0 / scal[1:2, 0:width]
    center, rstd = coef[0:1, :], coef[1:2, :]
    scale = gain * rstd * scal[0:1, 0:width]
    level, tilt = first * over, second * over * rstd

    def body(rows, _):
        x = pre[rows, :].astype(F32) - center
        out[rows, :] = (scale * (pushed[rows, :] - level - x * tilt)).astype(BF)

    rows_loop(pre.shape[0], body)


def own_core():
    return lax.rem(lax.axis_index("rows"), 2)


def own_chip():
    return lax.div(lax.axis_index("rows"), 2)


def image_row(step, side):
    return 2 * (own_chip() ^ step) + (own_core() ^ side)


def put_scalars(cells, counts, scal):
    groups = counts.shape[0]
    core, batch = own_core(), lax.axis_index("batch")
    total = counts[0]
    for k in range(1, groups):
        total = total + counts[k]

    def put(k, value):
        scal[k : k + 1, :] = jnp.full((1, scal.shape[1]), value, F32)

    put(0, (core < counts[batch]).astype(F32))
    put(1, total.astype(F32) * cells)
    for step in range(groups):
        own = counts[batch ^ step]
        for side, slot in enumerate((core, 1 - core)):
            valid = (slot < own).astype(F32)
            put(2 + 4 * step + 2 * side, valid * cells)
            put(3 + 4 * step + 2 * side, valid * (1.0 / cells) + (1.0 - valid))


def shifted_row(both):
    half = both.shape[1] // 2
    odd = both[:, half:].astype(F32)
    first = lax.broadcasted_iota(jnp.int32, odd.shape, 0) == 0
    before = jnp.where(first, 0.0, pltpu.roll(odd, 1, 0)).astype(BF)
    return jnp.concatenate([before, both], axis=1)


def row_of_slots(values):
    return jnp.concatenate([shifted_row(values[slot]) for slot in range(values.shape[0])], axis=0)


def streamed(w, rows, held, semaphores):
    count, wide = held.shape[0], held.shape[-1]
    copies = [
        pltpu.make_async_copy(w.at[rows, :, n * wide : (n + 1) * wide], held.at[n], semaphores.at[n])
        for n in range(count)
    ]
    for copy in copies[:2]:
        copy.start()
    for n in range(count):
        copies[n].wait()
        if n + 2 < count:
            copies[n + 2].start()
        yield slice(n * wide, (n + 1) * wide), held.at[n]


def own_kernel(x, w, part, held, semaphores):
    blocks = streamed(w, slice(1, 3), held, semaphores)
    cols, block = next(blocks)
    lefts = [row_of_slots(x[:, row]) for row in range(2)]
    while cols is not None:
        part[:, cols] = dot(lefts[0], block[0]) + dot(lefts[1], block[1])
        cols, block = next(blocks, (None, None))


def above_kernel(above, part, w, rows, held, semaphores):
    cells = above.shape[1]
    blocks = streamed(w, slice(0, 1), held, semaphores)
    cols, block = next(blocks)
    left = row_of_slots(above[...])
    while cols is not None:
        out = part[:, cols] + dot(left, block[0])
        for slot in range(above.shape[0]):
            rows[slot, :, cols] = out[slot * cells : (slot + 1) * cells].astype(BF)
        cols, block = next(blocks, (None, None))


def whole_kernel(counts, *rest):
    parts, (down_pre, keep, pay, scal, semaphore) = rest[:-5], rest[-5:]
    put_scalars(down_pre.shape[0], counts, scal)
    total = jnp.zeros((8, down_pre.shape[1]), F32)
    for k, part in enumerate(parts):
        width = part.shape[0] // 2
        for side in range(2):
            start = image_row(k, side) * width

            def body(index, total, part=part, side=side, start=start, width=width):
                src = pl.ds(pl.multiple_of(side * width + index * CHUNK, CHUNK), CHUNK)
                dst = pl.ds(pl.multiple_of(start + index * CHUNK, CHUNK), CHUNK)
                down_pre[dst, :] = part[src, :]
                return total + fold(part[src, :].astype(F32))

            total = lax.fori_loop(0, width // CHUNK, body, total)
    copy = pltpu.make_async_copy(down_pre, keep, semaphore)
    copy.start()
    total = jnp.sum(total, axis=0, keepdims=True)
    mean = total * (1.0 / down_pre.shape[0])

    def spread(rows, squares):
        off = down_pre[rows, :].astype(F32) - mean
        return squares + fold(off * off)

    squares = rows_loop(down_pre.shape[0], spread, jnp.zeros((8, down_pre.shape[1]), F32))
    pay[0:1, :] = total * scal[0:1, :]
    pay[1:2, :] = jnp.sum(squares, axis=0, keepdims=True) * scal[0:1, :]
    copy.wait()


def main_kernel(groups, scal, *rest):
    refs = rest[:groups]
    down_pre, params, w_main, sectioned, main_pre, main_keep, pay, coef, semaphore = rest[groups:]
    center, rstd = finish_moments(scal, refs)
    coef[0:1, :] = center
    coef[1:2, :] = rstd
    scale, offset = rstd * row_of(params, GAIN_WIDE, 0), row_of(params, SHIFT_WIDE, 0)

    def body(rows, _):
        value = (down_pre[rows, :].astype(F32) - center) * scale + offset
        sectioned[rows, :] = mish(value).astype(BF)

    rows_loop(down_pre.shape[0], body)
    project(sectioned, w_main, main_pre, pay, scal)
    copy = pltpu.make_async_copy(main_pre, main_keep, semaphore)
    copy.start()
    copy.wait()


def short_kernel(scal, sectioned, w_short, short_pre, pay):
    project(sectioned, w_short, short_pre, pay, scal)


def inner_kernel(groups, scal, *rest):
    refs = rest[:groups]
    pre, params, w_inner, mainline, inner_pre, pay, coef = rest[groups:]
    half = pre.shape[1]
    center, rstd = finish_moments(scal, refs)
    coef[0:1, :] = center
    coef[1:2, :] = rstd
    scale, offset = rstd * row_of(params, GAIN, 1, half), row_of(params, SHIFT, 1, half)

    def body(rows, _):
        mainline[rows, :] = mish((pre[rows, :] - center) * scale + offset).astype(BF)

    rows_loop(pre.shape[0], body)
    project(mainline, w_inner, inner_pre, pay, scal)


def three_shifts(values, rim, start, forward):
    width, half = values.shape
    place = lax.broadcasted_iota(jnp.int32, values.shape, 0)
    before = jnp.where(place == 0, 0.0, pltpu.roll(values, 1, 0)).astype(BF)
    after = jnp.where(place == width - 1, 0.0, pltpu.roll(values, width - 1, 0)).astype(BF)
    sides = (before, after) if forward else (after, before)
    rows = pl.ds(start, width)
    rim[rows, 0:half] = sides[0]
    rim[rows, half : 2 * half] = values.astype(BF)
    rim[rows, 2 * half : 3 * half] = sides[1]


def spatial_kernel(groups, width, scal, *rest):
    refs = rest[:groups]
    pre, params, w_spatial, rim, spatial_pre, pay, coef = rest[groups:]
    cells, half = pre.shape
    center, rstd = finish_moments(scal, refs)
    coef[0:1, :] = center
    coef[1:2, :] = rstd
    scale, offset = rstd * row_of(params, GAIN, 2, half), row_of(params, SHIFT, 2, half)
    blank = jnp.zeros((width, 3 * half), BF)
    rim[0:width, :] = blank
    rim[width + cells :, :] = blank

    def body(index, _):
        start = pl.multiple_of(index * width, width)
        act = mish((pre[pl.ds(start, width), :] - center) * scale + offset)
        three_shifts(act, rim, pl.multiple_of(start + width, width), True)

    lax.fori_loop(0, cells // width, body, None)
    w_spatial = w_spatial.ready()
    for begin in range(0, half, COLS):
        cols = slice(begin, begin + COLS)
        out = sum(
            dot(
                rim[i * width : i * width + cells, :],
                w_spatial[i * 3 * half : (i + 1) * 3 * half, cols],
            )
            for i in range(3)
        )
        spatial_pre[:, cols] = out
        put_moments(out, pay, cols, scal)


def trans_kernel(groups, scal, *rest):
    refs = rest[:groups]
    pre, mainline, params, w_trans, merged, trans_pre, pay, coef = rest[groups:]
    half = pre.shape[1]
    center, rstd = finish_moments(scal, refs)
    coef[0:1, :] = center
    coef[1:2, :] = rstd
    scale, offset = rstd * row_of(params, GAIN, 3, half), row_of(params, SHIFT, 3, half)

    def body(rows, _):
        act = mish((pre[rows, :] - center) * scale + offset)
        merged[rows, :] = (mainline[rows, :].astype(F32) + act).astype(BF)

    rows_loop(pre.shape[0], body)
    project(merged, w_trans, trans_pre, pay, scal)


def shortcut_kernel(groups, scal, *rest):
    refs = rest[:groups]
    pre, params, w_unite, shortcut, part, coef = rest[groups:]
    half = pre.shape[1]
    center, rstd = finish_moments(scal, refs)
    coef[0:1, :] = center
    coef[1:2, :] = rstd
    scale, offset = rstd * row_of(params, GAIN, 0, half), row_of(params, SHIFT, 0, half)

    def body(rows, _):
        shortcut[rows, :] = mish((pre[rows, :] - center) * scale + offset).astype(BF)

    rows_loop(pre.shape[0], body)
    w_unite = w_unite.ready()
    for start in range(0, part.shape[1], COLS):
        cols = slice(start, start + COLS)
        part[:, cols] = dot(shortcut[...], w_unite[:, cols])


def unite_kernel(groups, scal, *rest):
    refs = rest[:groups]
    pre, part, params, w_unite, transition, unite_pre, pay, coef = rest[groups:]
    half = pre.shape[1]
    center, rstd = finish_moments(scal, refs)
    coef[0:1, :] = center
    coef[1:2, :] = rstd
    scale, offset = rstd * row_of(params, GAIN, 4, half), row_of(params, SHIFT, 4, half)

    def body(rows, _):
        transition[rows, :] = mish((pre[rows, :] - center) * scale + offset).astype(BF)

    rows_loop(pre.shape[0], body)
    project(transition, w_unite.ready(), unite_pre, pay, scal, part)


def turn_kernel(groups, pieces, scal, *rest):
    refs = rest[:groups]
    pre, params = rest[groups : groups + 2]
    parts = rest[groups + 2 : groups + 2 + pieces]
    pushed, *outputs, pay, coef = rest[groups + 2 + pieces :]
    center, rstd = finish_moments(scal, refs)
    coef[0:1, :] = center
    coef[1:2, :] = rstd
    gain, offset, weight = row_of(params, GAIN_WIDE, 1), row_of(params, SHIFT_WIDE, 1), scal[0:1, 0 : pre.shape[1]]
    sums = (jnp.zeros((8, pre.shape[1]), F32),) * 2
    for k, part in enumerate(parts):
        part = part.ready()
        width = part.shape[0] // 2
        for side in range(2):
            start = image_row(k, side) * width

            def body(index, sums, k=k, part=part, side=side, start=start, width=width):
                src = pl.ds(pl.multiple_of(side * width + index * 16, 16), 16)
                dst = pl.ds(pl.multiple_of(start + index * 16, 16), 16)
                unit = (pre[dst, :] - center) * rstd
                value = unit * gain + offset
                grown = jnp.exp(jnp.minimum(value, FAR))
                wide = grown * (grown + 2.0)
                share = 1.0 / (wide + 2.0)
                level = wide * share
                if k == 0:
                    rows = pl.ds(pl.multiple_of(index * 16, 16), 16)
                    outputs[side][rows, :] = (value * level * weight).astype(BF)
                slope = level + 4.0 * value * (grown * (grown + 1.0) * share) * share
                out = part[src, :].astype(F32) * weight * slope
                pushed[dst, :] = out
                return sums[0] + fold(out), sums[1] + fold(out * unit)

            sums = lax.fori_loop(0, width // 16, body, sums)
    pay[0:1, :] = jnp.sum(sums[0], axis=0, keepdims=True)
    pay[1:2, :] = jnp.sum(sums[1], axis=0, keepdims=True)


def back_trans_kernel(groups, scal, *rest):
    refs = rest[:groups]
    (
        unite_pushed, unite_pre, unite_coef, params, trans_pre, trans_coef, w_unite,
        grad_unite, sums, pushed, pay, scratch,
    ) = rest[groups:]
    half = trans_pre.shape[1]
    settle(scal, refs, unite_pushed, unite_pre, unite_coef, row_of(params, GAIN_WIDE, 1), grad_unite, sums)
    w_unite = w_unite.ready()
    for start in range(0, half, COLS):
        scratch[:, start : start + COLS] = dot_back(
            grad_unite[...], w_unite[start : start + COLS, :]
        )
    push(
        lambda rows: scratch[rows, :],
        trans_pre, trans_coef[0:1, :], trans_coef[1:2, :], row_of(params, GAIN, 4, half), row_of(params, SHIFT, 4, half),
        pushed, pay,
    )


def back_short_kernel(grad_unite, pre, coef, params, w_unite, pushed, pay, scratch):
    half = pre.shape[1]
    w_unite = w_unite.ready()
    for start in range(0, half, COLS):
        scratch[:, start : start + COLS] = dot_back(
            grad_unite[...], w_unite[start : start + COLS, :]
        )
    push(
        lambda rows: scratch[rows, :],
        pre, coef[0:1, :], coef[1:2, :], row_of(params, GAIN, 0, half), row_of(params, SHIFT, 0, half), pushed, pay,
    )


def back_spatial_kernel(groups, scal, *rest):
    refs = rest[:groups]
    (
        trans_pushed, trans_pre, trans_coef, spatial_pre, spatial_coef, params, w_trans,
        grad_trans, sums, grad_merged, pushed, pay,
    ) = rest[groups:]
    half = trans_pre.shape[1]
    settle(scal, refs, trans_pushed, trans_pre, trans_coef, row_of(params, GAIN, 4, half), grad_trans, sums)
    w_trans = w_trans.ready()
    for start in range(0, half, COLS):
        grad_merged[:, start : start + COLS] = dot_back(
            grad_trans[...], w_trans[start : start + COLS, :]
        )
    push(
        lambda rows: grad_merged[rows, :],
        spatial_pre, spatial_coef[0:1, :], spatial_coef[1:2, :], row_of(params, GAIN, 3, half), row_of(params, SHIFT, 3, half),
        pushed, pay,
    )


def back_inner_kernel(groups, width, scal, *rest):
    refs = rest[:groups]
    (
        spatial_pushed, spatial_pre, spatial_coef, inner_pre, inner_coef, params, w_spatial,
        grad_spatial, sums, pushed, pay, rim, scratch,
    ) = rest[groups:]
    cells, half = spatial_pre.shape
    settle(scal, refs, spatial_pushed, spatial_pre, spatial_coef, row_of(params, GAIN, 3, half), grad_spatial, sums)
    blank = jnp.zeros((width, 3 * half), BF)
    rim[0:width, :] = blank
    rim[width + cells :, :] = blank

    def body(index, _):
        start = pl.multiple_of(index * width, width)
        values = grad_spatial[pl.ds(start, width), :].astype(F32)
        three_shifts(values, rim, pl.multiple_of(start + width, width), False)

    lax.fori_loop(0, cells // width, body, None)
    w_spatial = w_spatial.ready()
    for start in range(0, half, COLS):
        scratch[:, start : start + COLS] = sum(
            dot_back(
                rim[(2 - i) * width : (2 - i) * width + cells, j * half : (j + 1) * half],
                w_spatial[(3 * i + j) * half + start : (3 * i + j) * half + start + COLS, :],
            )
            for i in range(3)
            for j in range(3)
        )
    push(
        lambda rows: scratch[rows, :],
        inner_pre, inner_coef[0:1, :], inner_coef[1:2, :], row_of(params, GAIN, 2, half), row_of(params, SHIFT, 2, half),
        pushed, pay,
    )


def back_main_kernel(groups, scal, *rest):
    refs = rest[:groups]
    (
        inner_pushed, inner_pre, inner_coef, grad_merged, main_pre, main_coef, params, w_inner,
        grad_inner, sums, pushed, pay, scratch,
    ) = rest[groups:]
    half = inner_pre.shape[1]
    settle(scal, refs, inner_pushed, inner_pre, inner_coef, row_of(params, GAIN, 2, half), grad_inner, sums)
    w_inner = w_inner.ready()
    for start in range(0, half, COLS):
        cols = slice(start, start + COLS)
        scratch[:, cols] = grad_merged[:, cols] + dot_back(grad_inner[...], w_inner[cols, :])
    push(
        lambda rows: scratch[rows, :],
        main_pre, main_coef[0:1, :], main_coef[1:2, :], row_of(params, GAIN, 1, half), row_of(params, SHIFT, 1, half),
        pushed, pay,
    )


def settle_short_kernel(groups, scal, *rest):
    refs = rest[:groups]
    pushed, pre, coef, params, grad_short, sums = rest[groups:]
    half = pre.shape[1]
    settle(scal, refs, pushed, pre, coef, row_of(params, GAIN, 0, half), grad_short, sums)


def back_down_kernel(groups, scal, *rest):
    refs = rest[:groups]
    (
        main_pushed, main_coef, down_coef, params, main_pre, w_main, grad_short, w_short, down_pre,
        grad_main, sums, pushed, pay, scratch,
    ) = rest[groups:]
    main_pre = main_pre.ready()
    half = main_pre.shape[1]
    settle(scal, refs, main_pushed, main_pre, main_coef, row_of(params, GAIN, 1, half), grad_main, sums)
    w_main, grad_short, w_short = w_main.ready(), grad_short.ready(), w_short.ready()
    for start in range(0, pushed.shape[1], COLS):
        cols = slice(start, start + COLS)
        scratch[:, cols] = dot_back(grad_short[...], w_short[cols, :]) + dot_back(
            grad_main[...], w_main[cols, :]
        )
    push(
        lambda rows: scratch[rows, :],
        down_pre.ready(), down_coef[0:1, :], down_coef[1:2, :],
        row_of(params, GAIN_WIDE, 0), row_of(params, SHIFT_WIDE, 0),
        pushed, pay,
    )


def settle_down_kernel(groups, scal, *rest):
    refs = rest[:groups]
    pushed, pre, coef, params, grad_down, sums = rest[groups:]
    settle(scal, refs, pushed, pre, coef, row_of(params, GAIN_WIDE, 0), grad_down, sums)
    cells = pre.shape[0]
    grad_down[cells:, :] = jnp.zeros((grad_down.shape[0] - cells, pre.shape[1]), BF)


def cut_down_kernel(groups, scal, *rest):
    refs = rest[:groups]
    pushed, pre, coef, params, cut = rest[groups:]
    width = cut.shape[1]
    cols = pl.ds(pl.multiple_of(own_chip() * width, width), width)
    first, second = finish_sums(refs, cols)
    over = 1.0 / scal[1:2, 0:width]
    center, rstd = coef[0:1, cols], coef[1:2, cols]
    scale = params[GAIN_WIDE : GAIN_WIDE + 1, cols] * rstd * scal[0:1, 0:width]
    level, tilt = first * over, second * over * rstd

    def body(rows, _):
        x = pre[rows, cols].astype(F32) - center
        cut[rows, :] = (scale * (pushed[rows, cols] - level - x * tilt)).astype(BF)

    rows_loop(pre.shape[0], body)


def by_place(first, second):
    low = own_core() == 0
    return jnp.where(low, first, second), jnp.where(low, second, first)


def share_unite_kernel(shortcut, transition, grad, mine, other):
    width = 2 * mine.shape[1]
    cut = grad[:, pl.ds(pl.multiple_of(own_chip() * width, width), width)]
    half = shortcut.shape[1]
    for k, values in enumerate((shortcut, transition)):
        out = dot_cells(values[...], cut)
        near, far = by_place(out[:, : width // 2], out[:, width // 2 :])
        mine[k * half : (k + 1) * half, :] = near.astype(BF)
        other[k * half : (k + 1) * half, :] = far.astype(BF)


def put_halves(cut, values, start, mine, other):
    out = dot_cells(cut, values)
    rows, cols = mine.shape[0], slice(start, start + out.shape[1])
    near, far = by_place(out[:rows], out[rows:])
    mine[:, cols] = near.astype(BF)
    other[:, cols] = far.astype(BF)


def chip_columns(mine):
    width = 2 * mine.shape[0]
    return pl.ds(pl.multiple_of(own_chip() * width, width), width)


def share_pack_kernel(*rest):
    pairs, (mine, other) = rest[:-2], rest[-2:]
    cols = chip_columns(mine)
    start = 0
    for values, grad in zip(pairs[::2], pairs[1::2]):
        put_halves(grad[:, cols], values[...], start, mine, other)
        start += values.shape[1]


def share_spatial_kernel(cells, rim, grad, mine, other):
    cut = grad[:, chip_columns(mine)]
    line, side = (rim.shape[0] - cells) // 2, rim.shape[1]
    for row in range(3):
        put_halves(cut, rim[row * line : row * line + cells, :], row * side, mine, other)


def share_main_kernel(grad, grad_inner, sectioned, mainline, mine, other):
    cols = chip_columns(mine)
    sectioned, mainline = sectioned.ready(), mainline.ready()
    put_halves(grad[:, cols], sectioned[...], 0, mine, other)
    put_halves(grad_inner[:, cols], mainline[...], sectioned.shape[1], mine, other)


def finish_kernel(planes, unite, pack, taps, *rest):
    mains, (mine, got, near, far) = rest[:planes], rest[planes : planes + 4]
    w_unite, w_short, w_trans, w_inner, w_spatial, w_main, output, grad_inputs, semaphores = rest[planes + 4 :]
    core = own_core()
    copies = [
        pltpu.make_async_copy(mine, output.at[core, 0], semaphores.at[0]),
        pltpu.make_async_copy(got, output.at[1 - core, 0], semaphores.at[1]),
        pltpu.make_async_copy(near.at[0], grad_inputs.at[core], semaphores.at[2]),
        pltpu.make_async_copy(far.at[1], grad_inputs.at[1 - core], semaphores.at[3]),
    ]
    for copy in copies:
        copy.start()
    w_unite[...] = unite[...].astype(F32)
    for outs, values in (
        ((w_short, w_trans), pack[...].astype(F32)),
        ((w_main, w_inner), tree_sum([main[...].astype(F32) for main in mains])),
    ):
        start = 0
        for out in outs:
            out[...] = values[:, start : start + out.shape[1]]
            start += out.shape[1]
    half = w_trans.shape[1]
    for tap in range(w_spatial.shape[0]):
        w_spatial[tap] = taps[:, tap * half : (tap + 1) * half].astype(F32)
    for copy in copies:
        copy.wait()


def norm_sums_kernel(wide_count, *refs):
    sums, outs = refs[:-4], refs[-4:]
    for k, pair in enumerate(sums):
        index = k if k < wide_count else k - wide_count
        for row, out in ((1, outs[0 if k < wide_count else 1]), (0, outs[2 if k < wide_count else 3])):
            out[index : index + 1, :] = pair[row : row + 1, :]


def share_down_kernel(steps, chips, width, last_call, *rest):
    grads = rest[: len(steps)]
    earlier = rest[len(steps) : len(steps) + 2 * last_call]
    rest = rest[len(steps) + 2 * last_call :]
    source, outs, rest = rest[0], rest[1:3], rest[3:]
    if last_call:
        odd_acc, even_acc = rest[:2]
        rest = rest[2:]
    else:
        odd_acc, even_acc = outs
    padded, sides, held, semaphores = rest
    cells, columns = grads[0].shape
    half = source.shape[-1] // 2
    planes = source.shape[0] // (2 * chips)
    copies = []
    for k, step in enumerate(steps):
        plane = lax.axis_index("batch") ^ step
        copies.append(
            [
                pltpu.make_async_copy(
                    source.at[row * planes + plane, own_core()], held.at[k, row], semaphores.at[k, row]
                )
                for row in range(2 * chips)
            ]
        )
        for copy in copies[-1]:
            copy.start()
    padded[cells:, :] = jnp.zeros((padded.shape[0] - cells, columns), BF)
    last = lax.broadcasted_iota(jnp.int32, (width, columns), 0) == width - 1

    def ahead(values):
        return jnp.where(last, 0.0, pltpu.roll(values.astype(F32), width - 1, 0)).astype(BF)

    for k in range(len(steps)):
        padded[0:cells, :] = grads[k][...]
        for block in range(2 * chips):
            rows = slice(block * width, (block + 1) * width)
            here = padded[rows, :]
            upper = padded[(block + 1) * width : (block + 2) * width, :]
            sides[rows, 0:columns] = upper
            sides[rows, columns : 2 * columns] = here
            sides[rows, 2 * columns : 3 * columns] = ahead(here)
            sides[rows, 3 * columns : 4 * columns] = ahead(upper)
        for copy in copies[k]:
            copy.wait()

        def add(which, side, start, values, k=k):
            rows, cols = slice(side * half, (side + 1) * half), slice(start, start + columns)
            acc = (even_acc, odd_acc)[which]
            if k > 0:
                values = values + acc[rows, cols]
            elif last_call:
                values = values + earlier[1 - which][rows, cols]
            acc[rows, cols] = values

        for which in range(2):
            for side in range(2):
                left = held[k, :, which, :, side * half : (side + 1) * half].reshape(cells, half)
                for block in range(4):
                    if (which == 0 and block in (0, 3)) or (side == 0 and block in (2, 3)):
                        continue
                    start = block * columns
                    add(which, side, start, dot_cells(left, sides[:, start : start + columns]))
    if not last_call:
        return
    mine, other = outs
    places = (
        (odd_acc, 1, 3), (odd_acc, 0, 0), (odd_acc, 1, 0),
        (even_acc, 1, 2), (even_acc, 0, 1), (even_acc, 1, 1),
        (odd_acc, 1, 2), (odd_acc, 0, 1), (odd_acc, 1, 1),
    )
    for tap, (acc, side, block) in enumerate(places):
        values = acc[side * half : (side + 1) * half, block * columns : (block + 1) * columns]
        near, far = by_place(values[:, : columns // 2], values[:, columns // 2 :])
        mine[tap * half : (tap + 1) * half, :] = near.astype(BF)
        other[tap * half : (tap + 1) * half, :] = far.astype(BF)


def back_input_kernel(width, grad, w, out, near, far):
    cells = 2 * width
    full = grad.shape[1]

    @pl.when(pl.program_id(0) == 0)
    def _():
        last = lax.broadcasted_iota(jnp.int32, (width, full), 0) == width - 1
        for block in range(3):
            start = pl.multiple_of(own_chip() * cells + block * width, width)
            values = grad[pl.ds(start, width), :]
            rows = slice(block * width, (block + 1) * width)
            near[rows, :] = values
            far[rows, :] = jnp.where(
                last, 0.0, pltpu.roll(values.astype(F32), width - 1, 0)
            ).astype(BF)

    low, high = slice(0, cells), slice(width, width + cells)

    def term(values, rows, i, j):
        return dot_back(values[rows, :], w[3 * i + j])

    def put(parity, column, values):
        for row in range(2):
            out[row ^ own_core(), parity, pl.ds(column, width, stride=2), :] = values[
                row * width : (row + 1) * width
            ]

    put(0, 0, term(near, low, 1, 1))
    put(0, 1, term(near, low, 1, 2) + term(far, low, 1, 0))
    put(1, 0, term(near, high, 0, 1) + term(near, low, 2, 1))
    put(
        1,
        1,
        term(near, high, 0, 2) + term(far, high, 0, 0) + term(near, low, 2, 2) + term(far, low, 2, 0),
    )


SMEM = pl.BlockSpec(memory_space=pltpu.SMEM)
VMEM = pl.BlockSpec(memory_space=pltpu.VMEM)
ANY = pl.BlockSpec(memory_space=pl.ANY)


def shape(dims, dtype=F32):
    return jax.ShapeDtypeStruct(dims, dtype)


def nbytes(dims, dtype):
    count = 1
    for d in dims:
        count *= d
    return count * jnp.dtype(dtype).itemsize


def in_vmem(value):
    return pltpu.with_memory_space_constraint(value, pltpu.VMEM)


def in_hbm(value):
    return pltpu.with_memory_space_constraint(value, pltpu.HBM)


LIGHT = pl.CostEstimate(flops=0, bytes_accessed=0, transcendentals=0)


def call(kernel, name, scalars, near, outs, flops, scratch=(), far=(), pin=False, spill=(), light=False, out=(), late=False):
    cuts = [one[1] if isinstance(one, tuple) else None for one in far]
    far = [one[0] if isinstance(one, tuple) else one for one in far]
    held_far = [
        shape((cut.stop - cut.start,) + a.shape[1:], a.dtype) if cut else a for a, cut in zip(far, cuts)
    ]
    moved = sum(nbytes(a.shape, a.dtype) for a in (*near, *far, *outs))
    scratch = [s if hasattr(s, "memory_space") or not hasattr(s, "shape") else pltpu.VMEM(s.shape, s.dtype) for s in scratch]
    held = moved + sum(nbytes(s.shape, s.dtype) for s in scratch if hasattr(s, "shape"))
    if pin:
        held -= moved - sum(nbytes(a.shape, a.dtype) for a in far)
        held += sum(nbytes(outs[k].shape, outs[k].dtype) for k in spill)
        near, far = [in_vmem(a) for a in near], [in_hbm(a) for a in far]
        outs = [
            o if k in spill else (pltpu.HBM if k in out else pltpu.VMEM)(o.shape, o.dtype)
            for k, o in enumerate(outs)
        ]
    before, after_far, last = len(scalars) + len(near), len(far), len(outs) + len(scratch)

    def body(*refs):
        sources, rest = refs[before : before + after_far], refs[before + after_far :]
        targets = rest[last : last + after_far]
        fars = [
            Far(a.at[cut] if cut else a, b, rest[-1].at[k])
            for k, (a, b, cut) in enumerate(zip(sources, targets, cuts))
        ]
        kernel(*refs[:before], *fars, *rest[:last])
        for one in fars:
            one.ready()

    return pl.pallas_call(
        body if far else kernel,
        name=name,
        out_shape=tuple(outs),
        in_specs=[SMEM] * len(scalars) + [VMEM] * len(near) + [ANY] * len(far),
        out_specs=tuple(ANY if k in out and not late else VMEM for k in range(len(outs))),
        scratch_shapes=scratch
        + [pltpu.VMEM(a.shape, a.dtype) for a in held_far]
        + ([pltpu.SemaphoreType.DMA((len(far),))] if far else []),
        compiler_params=pltpu.CompilerParams(vmem_limit_bytes=held + (8 << 20)),
        cost_estimate=LIGHT if light else pl.CostEstimate(flops=flops, bytes_accessed=moved, transcendentals=0),
    )(*scalars, *near, *far)


def first_conv(view, above, w_down, pin):
    slots, _, cells, both = view.shape
    half = both // 2
    full = w_down.shape[-1]
    taps = w_down.reshape(3, 3 * half, full)
    if pin:
        view, above, taps = in_vmem(view), in_vmem(above), in_hbm(taps)
    wide = 256
    count = full // wide

    def run(kernel, name, rows, values, out):
        return pl.pallas_call(
            kernel,
            name=name,
            out_shape=(pltpu.VMEM if pin else shape)(out.shape, out.dtype),
            in_specs=[VMEM] * len(values) + [ANY],
            out_specs=VMEM,
            scratch_shapes=[
                pltpu.VMEM((count, rows, 3 * half, wide), BF), pltpu.SemaphoreType.DMA((count,))
            ],
            compiler_params=pltpu.CompilerParams(vmem_limit_bytes=24 << 20),
            cost_estimate=pl.CostEstimate(
                flops=6 * rows * slots * cells * half * full,
                bytes_accessed=6 * rows * half * full,
                transcendentals=0,
            ),
        )(*values, taps)

    part = run(own_kernel, "own", 2, [view], shape((slots * cells, full)))
    part = in_vmem(part) if pin else part
    return run(above_kernel, "above", 1, [above, part], shape((slots, cells, full), BF))


def flipped(kernel):
    return jnp.swapaxes(jnp.flip(kernel, (0, 1)), 2, 3)


def on_device(
    inputs,
    image_counts,
    w_down,
    w_short,
    w_main,
    w_inner,
    w_spatial,
    w_trans,
    w_unite,
    gains_wide,
    gains_narrow,
    shifts_wide,
    shifts_narrow,
    grad_output,
):
    half = w_short.shape[1]
    full = 2 * half
    slots, height_dev, width, _ = grad_output.shape
    here = Plane()
    wide = here.chips == 4 and half % (128 * here.chips) == 0
    stage = functools.partial(call, pin=wide)
    groups, chips = here.groups, here.chips
    height = here.rows * height_dev
    cells = height * width
    batch = lax.axis_index("batch")
    view = inputs.reshape(slots, 2, width, 2 * half)
    below = [(i, i + 1) for i in range(here.rows - 1)]
    above = lax.ppermute(view[:, 1], "rows", below)
    params = jnp.concatenate(
        [gains_wide, shifts_wide]
        + [jnp.pad(p, ((0, 0), (0, half))) for p in (gains_narrow, shifts_narrow)]
    )
    down_rows = first_conv(view, above, w_down, wide)
    down_pieces = here.pieces(*here.split(down_rows))
    grad_mine, grad_other = here.split(grad_output.reshape(slots, width, full))
    down_pieces[1], params, grad_mine, grad_other = lax.optimization_barrier(
        (down_pieces[1], params, grad_mine, grad_other)
    )
    down_pre, down_keep, down_pay, scal = stage(
        whole_kernel,
        "whole",
        [image_counts],
        down_pieces,
        [
            shape((cells, full), BF), shape((cells, full), BF), shape((2, full)),
            shape((2 + 4 * groups, full)),
        ],
        10 * cells * full,
        out=(1,),
        scratch=[pltpu.SemaphoreType.DMA],
    )
    if wide:
        flat = after(view, down_pay).reshape(slots * 2 * width, 2 * half)
        source = lax.all_gather(flat, ("rows", "batch")).reshape(-1, *view.shape)
        grad_piece = jnp.concatenate([grad_mine, here.swap(after(grad_other, down_pay))], axis=0)
        grad_pieces = [grad_piece, here.chip_hop(grad_piece, 1), here.chip_hop(grad_piece, 2)]
        grad_pieces.append(here.chip_hop(grad_pieces[1], 2))
    else:
        grad_pieces = here.pieces(grad_mine, grad_other)
    sectioned, main_pre, main_keep, main_pay, down_coef = stage(
        functools.partial(main_kernel, groups),
        "main",
        [],
        [scal, *here.everywhere(down_pay), down_pre, params],
        [
            shape((cells, full), BF), shape((cells, half)), shape((cells, half)),
            shape((2, half)), shape((2, full)),
        ],
        2 * cells * full * half,
        far=[w_main],
        out=(2,),
        scratch=[pltpu.SemaphoreType.DMA],
    )

    if wide:
        main_pay = after(main_pay, *grad_pieces[:3])
    main_all = here.everywhere(main_pay)
    short_pre, short_pay = stage(
        short_kernel,
        "short",
        [],
        [scal, sectioned],
        [shape((cells, half)), shape((2, half))],
        2 * cells * full * half,
        far=[w_short],
    )
    mainline, inner_pre, inner_pay, main_coef = stage(
        functools.partial(inner_kernel, groups),
        "inner",
        [],
        [scal, *main_all, main_pre, params],
        [shape((cells, half), BF), shape((cells, half)), shape((2, half)), shape((2, half))],
        2 * cells * half * half,
        far=[w_inner],
    )
    inner_all = here.everywhere(inner_pay)
    rim, spatial_pre, spatial_pay, inner_coef = stage(
        functools.partial(spatial_kernel, groups, width),
        "spatial",
        [],
        [scal, *inner_all, inner_pre, params],
        [
            shape((cells + 2 * width, 3 * half), BF), shape((cells, half)),
            shape((2, half)), shape((2, half)),
        ],
        18 * cells * half * half,
        far=[w_spatial.reshape(9 * half, half)],
    )
    if wide:
        spatial_pay = after(spatial_pay, grad_pieces[3])
    both_all = here.everywhere(jnp.concatenate([spatial_pay, short_pay], axis=1))
    spatial_all = [b[:, :half] for b in both_all]
    short_all = [b[:, half:] for b in both_all]
    merged, trans_pre, trans_pay, spatial_coef = stage(
        functools.partial(trans_kernel, groups),
        "trans",
        [],
        [scal, *spatial_all, spatial_pre, mainline, params],
        [shape((cells, half), BF), shape((cells, half)), shape((2, half)), shape((2, half))],
        2 * cells * half * half,
        far=[w_trans],
    )
    trans_all = here.everywhere(trans_pay)
    shortcut, unite_part, short_coef = stage(
        functools.partial(shortcut_kernel, groups),
        "shortcut",
        [],
        [scal, *short_all, short_pre, params],
        [shape((cells, half), BF), shape((cells, full)), shape((2, half))],
        2 * cells * half * full,
        far=[(w_unite, slice(0, half))],
    )
    transition, unite_pre, unite_pay, trans_coef = stage(
        functools.partial(unite_kernel, groups),
        "unite",
        [],
        [scal, *trans_all, trans_pre, unite_part, params],
        [shape((cells, half), BF), shape((cells, full)), shape((2, full)), shape((2, half))],
        2 * cells * half * full,
        far=[(w_unite, slice(half, full))],
    )
    unite_all = here.everywhere(unite_pay)
    unite_pushed, mine, other, unite_pay, unite_coef = stage(
        functools.partial(turn_kernel, groups, chips),
        "turn",
        [],
        [scal, *unite_all, unite_pre, params],
        [
            shape((cells, full)), shape((width, full), BF), shape((width, full), BF),
            shape((2, full)), shape((2, full)),
        ],
        40 * cells * full,
        far=grad_pieces,
        spill=(1, 2),
    )
    output_rows = (mine, here.swap(other))

    unite_all = here.everywhere(unite_pay)
    grad_unite_pre, unite_sums, trans_pushed, trans_pay = stage(
        functools.partial(back_trans_kernel, groups),
        "back_trans",
        [],
        [scal, *unite_all, unite_pushed, unite_pre, unite_coef, params, trans_pre, trans_coef],
        [shape((cells, full), BF), shape((2, full)), shape((cells, half)), shape((2, half))],
        2 * cells * half * full,
        [shape((cells, half))],
        far=[(w_unite, slice(half, full))],
    )
    trans_all = here.everywhere(trans_pay)
    if wide:

        def of_pair(pair):
            mine, other = pair
            return (mine.astype(F32) + here.swap(other).astype(F32)).astype(BF)

        share_unite = of_pair(
            stage(
                share_unite_kernel,
                "share_unite",
                [],
                [shortcut, transition, grad_unite_pre],
                [shape((full, full // chips // 2), BF)] * 2,
                2 * cells * full * full // chips,
            )
        )
    short_pushed, short_pay = stage(
        back_short_kernel,
        "back_short",
        [],
        [grad_unite_pre, short_pre, short_coef, params],
        [shape((cells, half)), shape((2, half))],
        2 * cells * half * full,
        [shape((cells, half))],
        far=[(w_unite, slice(0, half))],
    )
    grad_trans_pre, trans_sums, grad_merged, spatial_pushed, spatial_pay = stage(
        functools.partial(back_spatial_kernel, groups),
        "back_spatial",
        [],
        [scal, *trans_all, trans_pushed, trans_pre, trans_coef, spatial_pre, spatial_coef, params],
        [
            shape((cells, half), BF), shape((2, half)), shape((cells, half)), shape((cells, half)),
            shape((2, half)),
        ],
        2 * cells * half * half,
        far=[w_trans],
    )
    both_all = here.everywhere(jnp.concatenate([spatial_pay, short_pay], axis=1))
    spatial_all = [b[:, :half] for b in both_all]
    short_all = [b[:, half:] for b in both_all]
    grad_spatial_pre, spatial_sums, inner_pushed, inner_pay = stage(
        functools.partial(back_inner_kernel, groups, width),
        "back_inner",
        [],
        [scal,
            *spatial_all, spatial_pushed, spatial_pre, spatial_coef, inner_pre, inner_coef, params,
        ],
        [shape((cells, half), BF), shape((2, half)), shape((cells, half)), shape((2, half))],
        18 * cells * half * half,
        [shape((cells + 2 * width, 3 * half), BF), shape((cells, half))],
        far=[w_spatial.reshape(9 * half, half)],
    )
    inner_all = here.everywhere(inner_pay)
    grad_short_pre, short_sums = stage(
        functools.partial(settle_short_kernel, groups),
        "settle_short",
        [],
        [scal, *short_all, short_pushed, short_pre, short_coef, params],
        [shape((cells, half), BF), shape((2, half))],
        10 * cells * half,
    )
    if wide:
        lean = half // chips // 2
        share_spatial = of_pair(
            stage(
                functools.partial(share_spatial_kernel, cells),
                "share_spatial",
                [],
                [rim, grad_spatial_pre],
                [shape((lean, 9 * half), BF)] * 2,
                18 * cells * half * half // chips,
            )
        )
        share_pack = of_pair(
            stage(
                share_pack_kernel,
                "share_pack",
                [],
                [sectioned, grad_short_pre, merged, grad_trans_pre],
                [shape((lean, full + half), BF)] * 2,
                6 * cells * half * half // chips,
            )
        )
        inner_all[0], source, *shares = lax.optimization_barrier(
            (inner_all[0], source, share_unite, share_pack, share_spatial)
        )
        shares = lax.psum(tuple(shares), "batch")
    grad_inner_pre, inner_sums, main_pushed, main_pay = stage(
        functools.partial(back_main_kernel, groups),
        "back_main",
        [],
        [scal, *inner_all, inner_pushed, inner_pre, inner_coef, grad_merged, main_pre, main_coef, params],
        [shape((cells, half), BF), shape((2, half)), shape((cells, half)), shape((2, half))],
        2 * cells * half * half,
        [shape((cells, half))],
        far=[w_inner],
    )
    main_all = here.everywhere(main_pay)
    grad_main_pre, main_sums, down_pushed, down_pay = stage(
        functools.partial(back_down_kernel, groups),
        "back_down",
        [],
        [scal, *main_all, main_pushed, main_coef, down_coef, params],
        [shape((cells, half), BF), shape((2, half)), shape((cells, full)), shape((2, full))],
        4 * cells * half * full,
        [shape((cells, full))],
        far=[main_keep, w_main, grad_short_pre, w_short, down_keep], light=True)
    down_all = here.everywhere(down_pay)
    spare = width
    if wide:
        grad_cut = stage(
            functools.partial(cut_down_kernel, groups),
            "cut_down",
            [],
            [scal, *down_all, down_pushed, down_pre, down_coef, params],
            [shape((cells, full // chips), BF)],
            10 * cells * full // chips, light=True)[0]
        cuts = here.plane_hops(grad_cut)
    grad_down_pre, down_sums = stage(
        functools.partial(settle_down_kernel, groups),
        "settle_down",
        [],
        [scal, *down_all, down_pushed, down_pre, down_coef, params],
        [shape((cells + spare, full), BF), shape((2, full))],
        10 * cells * full, light=True)
    if not wide:
        output = jnp.stack(here.by_core(*output_rows)).reshape(grad_output.shape)
    norm_grads = stage(
        functools.partial(norm_sums_kernel, 2),
        "norm_sums",
        [],
        [down_sums, unite_sums, short_sums, main_sums, inner_sums, spatial_sums, trans_sums],
        [shape((2, full)), shape((5, half))] * 2,
        0,
        spill=range(4), light=True)
    if wide:
        near = pl.pallas_call(
            functools.partial(back_input_kernel, width),
            name="back_input",
            grid=(half // 128,),
            out_shape=shape((2, 2, 2 * width, half)),
            in_specs=[
                pl.BlockSpec((cells + spare, full), lambda n: (0, 0)),
                pl.BlockSpec((9, 128, full), lambda n: (0, n, 0)),
            ],
            out_specs=pl.BlockSpec((2, 2, 2 * width, 128), lambda n: (0, 0, 0, n)),
            scratch_shapes=[pltpu.VMEM((3 * width, full), BF)] * 2,
            compiler_params=pltpu.CompilerParams(vmem_limit_bytes=16 << 20),
            cost_estimate=LIGHT,
        )(grad_down_pre, in_hbm(w_down.reshape(9, half, full)))
        share_main = of_pair(
            stage(
                share_main_kernel,
                "share_main",
                [],
                [grad_main_pre, grad_inner_pre],
                [shape((lean, full + half), BF)] * 2,
                6 * cells * half * half // chips,
                far=[sectioned, mainline],
                light=True,
            )
        )
        columns = full // chips
        sums_here = [shape((full, 4 * columns)), shape((full, 4 * columns))]
        halves = [shape((9 * half, columns // 2), BF)] * 2

        def share_down(steps, earlier):
            outs = halves if earlier else sums_here
            near = [*(cuts[step] for step in steps), *earlier]
            scratch = [
                pltpu.VMEM((cells + spare, columns), BF),
                pltpu.VMEM((cells, 4 * columns), BF),
                pltpu.VMEM((len(steps), 2 * chips, 2, width, full), BF),
                pltpu.SemaphoreType.DMA((len(steps), 2 * chips)),
            ]
            if earlier:
                scratch = [pltpu.VMEM(a.shape, F32) for a in sums_here] + scratch
            return pl.pallas_call(
                functools.partial(share_down_kernel, steps, chips, width, int(bool(earlier))),
                name="share_down",
                out_shape=tuple(pltpu.VMEM(o.shape, o.dtype) for o in outs),
                in_specs=[VMEM] * len(near) + [ANY],
                out_specs=(VMEM,) * len(outs),
                scratch_shapes=scratch,
                compiler_params=pltpu.CompilerParams(vmem_limit_bytes=30 << 20),
                cost_estimate=LIGHT,
            )(*map(in_vmem, near), in_hbm(source))

        middle = (groups + 1) // 2
        cuts[:middle], near = lax.optimization_barrier((cuts[:middle], near))
        first_sums = share_down(range(middle), ())
        mains = here.plane_hops(after(share_main, grad_cut))
        cuts[middle:], first_sums = lax.optimization_barrier((cuts[middle:], first_sums))
        mine, other = share_down(range(middle, groups), first_sums)
        other, *tied = lax.optimization_barrier((other, *shares, *mains))
        shares, mains = tied[: len(shares)], tied[len(shares) :]
        grad_w_down = mine.astype(F32) + here.swap(other).astype(F32)
        outs = [
            shape((full, 2 * lean)), shape((lean, full)), shape((lean, half)), shape((lean, half)),
            shape((9, lean, half)), shape((lean, full)),
            shape(grad_output.shape, BF), shape(inputs.shape),
        ]
        placed = [*output_rows, near, here.swap(near)]
        early = pl.pallas_call(
            functools.partial(finish_kernel, groups),
            name="finish",
            out_shape=tuple(outs),
            in_specs=[VMEM] * (3 + groups) + [ANY] * 4,
            out_specs=(VMEM,) * 6 + (ANY,) * 2,
            scratch_shapes=[pltpu.SemaphoreType.DMA((4,))],
            compiler_params=pltpu.CompilerParams(vmem_limit_bytes=24 << 20),
            cost_estimate=LIGHT,
        )(*shares, *mains, *placed)
        output, grad_inputs = early[6:]
        early = [
            early[1].T, early[5].T, early[3].T, jnp.swapaxes(early[4], 1, 2), early[2].T, early[0],
        ]
    else:
        grad_down_pre = grad_down_pre[:cells]
        def share(values, grad):
            columns = grad.shape[1] // chips
            grad = lax.dynamic_slice_in_dim(grad, here.chip * columns, columns, 1)
            part = jnp.concatenate([dot_cells(v, grad) for v in values], axis=0)
            mine, other = here.split(part.reshape(part.shape[0], 2, columns // 2), 1)
            return (mine + here.swap(other.astype(BF)).astype(F32)).astype(BF)

        windows = [rim[i * width : i * width + cells] for i in range(3)]
        early = lax.psum(
            (
                share([sectioned], grad_short_pre),
                share([sectioned], grad_main_pre),
                share([mainline], grad_inner_pre),
                share(windows, grad_spatial_pre),
                share([merged], grad_trans_pre),
                jnp.concatenate([share([shortcut], grad_unite_pre), share([transition], grad_unite_pre)]),
            ),
            "batch",
        )
        early = [e.astype(F32) for e in early]

        mine, other = here.split(view)
        got = here.chip_hops(jnp.stack([mine, here.swap(other)], axis=1))
        source = jnp.zeros((2, here.rows, width, full), BF)
        for step, piece in enumerate(got):
            for side in range(2):
                source = lax.dynamic_update_slice_in_dim(
                    source, piece[:, side : side + 1], 2 * (here.chip ^ step) + (here.core ^ side), 1
                )
        grad_map = grad_down_pre.reshape(height, width, full)
        columns = full // chips
        grad_cut = lax.dynamic_slice_in_dim(grad_map, here.chip * columns, columns, 2)
        ahead = jnp.pad(grad_cut[:, 1:], ((0, 0), (0, 1), (0, 0)))
        upper = jnp.pad(grad_cut[1:], ((0, 1), (0, 0), (0, 0)))
        both_ahead = jnp.pad(ahead[1:], ((0, 1), (0, 0), (0, 0)))
        even_rows = source[0].reshape(cells, full)
        odd_rows = source[1].reshape(cells, full)

        def taps_of(rows, here_grad, ahead_grad):
            plain = dot_cells(rows, here_grad.reshape(cells, columns))
            before = dot_cells(rows[:, half:], ahead_grad.reshape(cells, columns))
            return [before, plain]

        part = jnp.concatenate(
            taps_of(odd_rows, upper, both_ahead)
            + taps_of(even_rows, grad_cut, ahead)
            + taps_of(odd_rows, grad_cut, ahead),
            axis=0,
        )
        mine, other = here.split(part.reshape(9 * half, 2, columns // 2), 1)
        part = (mine + here.swap(other.astype(BF)).astype(F32)).astype(BF)
        grad_w_down = lax.psum(part, "batch").astype(F32)

        pair_rows = 2 * height_dev
        grad_image = jnp.pad(grad_map, ((0, 1), (0, 0), (0, 0)))
        grad_block = lax.dynamic_slice_in_dim(grad_image, here.chip * pair_rows, pair_rows + 1, 0)
        widened = lax.conv_general_dilated(
            grad_block[None],
            flipped(w_down),
            (1, 1),
            ((1, 0), (1, 2)),
            lhs_dilation=(2, 2),
            dimension_numbers=("NHWC", "HWIO", "NHWC"),
            preferred_element_type=F32,
        )[0]
        mine = lax.dynamic_slice_in_dim(widened, here.core * pair_rows, pair_rows, 0)
        other = lax.dynamic_slice_in_dim(widened, (1 - here.core) * pair_rows, pair_rows, 0)
        grad_inputs = jnp.stack(here.by_core(mine, here.swap(other)))

    return (
        output,
        grad_inputs,
        grad_w_down.reshape(3, 3, half, -1),
        early[0],
        early[1],
        early[2],
        early[3].reshape(3, 3, half, -1),
        early[4],
        early[5],
        *norm_grads,
    )


def solution(mesh):
    placed = (P("batch", "rows", None, None),) + (P(),) * 12 + (P("batch", "rows", None, None),)
    return jax.shard_map(
        on_device,
        mesh=mesh,
        in_specs=placed,
        out_specs=(
            P("batch", "rows", None, None),
            P("batch", "rows", None, None),
            P(None, None, None, "rows"),
            P(None, "rows"),
            P(None, "rows"),
            P(None, "rows"),
            P(None, None, None, "rows"),
            P(None, "rows"),
            P(None, "rows"),
            P(),
            P(),
            P(),
            P(),
        ),
        check_vma=False,
    )
```

```python
import functools

import jax
import jax.numpy as jnp
from jax import lax
from jax.experimental import pallas as pl
from jax.experimental.pallas import tpu as pltpu
from jax.sharding import PartitionSpec as P

EPSILON = 1e-05
FAR = 20.0
CHUNK = 64
COLS = 256
BF = jnp.bfloat16
F32 = jnp.float32


def mish(values):
    grown = jnp.exp(jnp.minimum(values, FAR))
    wide = grown * (grown + 2.0)
    return values * (wide / (wide + 2.0))


def mish_slope(values):
    grown = jnp.exp(jnp.minimum(values, FAR))
    wide = grown * (grown + 2.0)
    share = 1.0 / (wide + 2.0)
    return wide * share + 4.0 * values * (grown * (grown + 1.0) * share) * share


def after(value, *others):
    return lax.optimization_barrier((value,) + others)[0]


def tree_sum(parts):
    while len(parts) > 1:
        parts = [parts[i] + parts[i + 1] for i in range(0, len(parts), 2)]
    return parts[0]


def dot(a, b):
    return jnp.dot(a, b, preferred_element_type=F32)


def dot_back(a, b):
    return lax.dot_general(a, b, (((1,), (1,)), ((), ())), preferred_element_type=F32)


def dot_cells(a, b):
    return lax.dot_general(a, b, (((0,), (0,)), ((), ())), preferred_element_type=F32)


class Plane:
    def __init__(self):
        self.rows = lax.axis_size("rows")
        self.groups = lax.axis_size("batch")
        self.chips = self.rows // 2
        self.place = lax.axis_index("rows")
        self.core = self.place % 2
        self.chip = self.place // 2

    def swap(self, value):
        return lax.ppermute(value, "rows", [(i, i ^ 1) for i in range(self.rows)])

    def chip_hops(self, value):
        return [value] + [
            lax.ppermute(value, "rows", [(i, i ^ (2 * step)) for i in range(self.rows)])
            for step in range(1, self.chips)
        ]

    def chip_hop(self, value, step):
        return lax.ppermute(value, "rows", [(i, i ^ (2 * step)) for i in range(self.rows)])

    def plane_hops(self, value):
        return [value] + [
            lax.ppermute(value, "batch", [(i, i ^ step) for i in range(self.groups)])
            for step in range(1, self.groups)
        ]

    def by_core(self, mine, got):
        first = self.core == 0
        return jnp.where(first, mine, got), jnp.where(first, got, mine)

    def split(self, block, axis=0):
        mine = lax.dynamic_index_in_dim(block, self.core, axis, keepdims=False)
        other = lax.dynamic_index_in_dim(block, 1 - self.core, axis, keepdims=False)
        return mine, other

    def pieces(self, mine, other):
        return self.chip_hops(jnp.concatenate([mine, self.swap(other)], axis=0))

    def plane_steps(self, value):
        found = {0: value}
        step = self.groups // 2
        while step:
            found |= {far + step: self.plane_hop(v, step) for far, v in found.items()}
            step //= 2
        return [found[k] for k in range(self.groups)]

    def plane_hop(self, value, step):
        return lax.ppermute(value, "batch", [(i, i ^ step) for i in range(self.groups)])

    def everywhere(self, pay):
        return self.plane_hops(jnp.concatenate([pay, self.swap(pay)], axis=0))


class Far:
    def __init__(self, source, target, semaphore):
        self.copy = pltpu.make_async_copy(source, target, semaphore)
        self.copy.start()
        self.target, self.waits = target, True

    def ready(self):
        if self.waits:
            self.copy.wait()
            self.waits = False
        return self.target


def rows_loop(total, body, carry=None, step=CHUNK):
    def turn(index, state):
        return body(pl.ds(pl.multiple_of(index * step, step), step), state)

    return lax.fori_loop(0, total // step, turn, carry, unroll=2)


GAIN_WIDE, SHIFT_WIDE, GAIN, SHIFT = 0, 2, 4, 9


def row_of(params, first, index, half=None):
    return params[first + index : first + index + 1, 0 : (half or params.shape[1])]


def finish_moments(scal, refs, cols=slice(None)):
    scal = [scal[k : k + 1, 0 : refs[0].shape[1]] for k in range(2 + 4 * len(refs))]
    pixels = scal[1]
    center = tree_sum([r[0:1, cols] + r[2:3, cols] for r in refs]) / pixels
    terms = []
    for k, r in enumerate(refs):
        ends = []
        for side in range(2):
            count, over = scal[2 + 4 * k + 2 * side], scal[3 + 4 * k + 2 * side]
            gap = r[2 * side : 2 * side + 1, cols] * over - center
            ends.append(gap * gap * count)
        terms.append((r[1:2, cols] + r[3:4, cols]) + (ends[0] + ends[1]))
    return center, lax.rsqrt(tree_sum(terms) / pixels + EPSILON)


def finish_sums(refs, cols=slice(None)):
    return (
        tree_sum([r[0:1, cols] + r[2:3, cols] for r in refs]),
        tree_sum([r[1:2, cols] + r[3:4, cols] for r in refs]),
    )


def put_moments(values, pay, cols, scal):
    weight = scal[0:1, cols]
    total = jnp.sum(values, axis=0, keepdims=True)
    off = values - total * (1.0 / values.shape[0])
    pay[0:1, cols] = total * weight
    pay[1:2, cols] = jnp.sum(off * off, axis=0, keepdims=True) * weight


def project(left, weights, pre, pay, scal, add=None):
    weights = weights.ready() if isinstance(weights, Far) else weights
    for start in range(0, pre.shape[1], COLS):
        cols = slice(start, start + COLS)
        out = dot(left[...], weights[:, cols])
        if add is not None:
            out = out + add[:, cols]
        pre[:, cols] = out
        put_moments(out, pay, cols, scal)


def fold(values):
    return jnp.sum(values.reshape(-1, 8, values.shape[-1]), axis=0)


def push(grad_of, pre, center, rstd, gain, offset, pushed, pay):
    def body(rows, sums):
        unit = (pre[rows, :].astype(F32) - center) * rstd
        out = grad_of(rows) * mish_slope(unit * gain + offset)
        pushed[rows, :] = out
        return sums[0] + fold(out), sums[1] + fold(out * unit)

    zero = jnp.zeros((8, pre.shape[1]), F32)
    first, second = rows_loop(pre.shape[0], body, (zero, zero), 32)
    pay[0:1, :] = jnp.sum(first, axis=0, keepdims=True)
    pay[1:2, :] = jnp.sum(second, axis=0, keepdims=True)


def settle(scal, refs, pushed, pre, coef, gain, out, sums):
    first, second = finish_sums(refs)
    sums[0:1, :] = first
    sums[1:2, :] = second
    width = pre.shape[1]
    over = 1.0 / scal[1:2, 0:width]
    center, rstd = coef[0:1, :], coef[1:2, :]
    scale = gain * rstd * scal[0:1, 0:width]
    level, tilt = first * over, second * over * rstd

    def body(rows, _):
        x = pre[rows, :].astype(F32) - center
        out[rows, :] = (scale * (pushed[rows, :] - level - x * tilt)).astype(BF)

    rows_loop(pre.shape[0], body)


def own_core():
    return lax.rem(lax.axis_index("rows"), 2)


def own_chip():
    return lax.div(lax.axis_index("rows"), 2)


def image_row(step, side):
    return 2 * (own_chip() ^ step) + (own_core() ^ side)


def put_scalars(cells, counts, scal):
    groups = counts.shape[0]
    core, batch = own_core(), lax.axis_index("batch")
    total = counts[0]
    for k in range(1, groups):
        total = total + counts[k]

    def put(k, value):
        scal[k : k + 1, :] = jnp.full((1, scal.shape[1]), value, F32)

    put(0, (core < counts[batch]).astype(F32))
    put(1, total.astype(F32) * cells)
    for step in range(groups):
        own = counts[batch ^ step]
        for side, slot in enumerate((core, 1 - core)):
            valid = (slot < own).astype(F32)
            put(2 + 4 * step + 2 * side, valid * cells)
            put(3 + 4 * step + 2 * side, valid * (1.0 / cells) + (1.0 - valid))


def shifted_row(both):
    half = both.shape[1] // 2
    odd = both[:, half:].astype(F32)
    first = lax.broadcasted_iota(jnp.int32, odd.shape, 0) == 0
    before = jnp.where(first, 0.0, pltpu.roll(odd, 1, 0)).astype(BF)
    return jnp.concatenate([before, both], axis=1)


def row_of_slots(values):
    return jnp.concatenate([shifted_row(values[slot]) for slot in range(values.shape[0])], axis=0)


def streamed(w, rows, held, semaphores):
    count, wide = held.shape[0], held.shape[-1]
    copies = [
        pltpu.make_async_copy(w.at[rows, :, n * wide : (n + 1) * wide], held.at[n], semaphores.at[n])
        for n in range(count)
    ]
    for copy in copies[:2]:
        copy.start()
    for n in range(count):
        copies[n].wait()
        if n + 2 < count:
            copies[n + 2].start()
        yield slice(n * wide, (n + 1) * wide), held.at[n]


def own_kernel(x, w, part, held, semaphores):
    blocks = streamed(w, slice(1, 3), held, semaphores)
    cols, block = next(blocks)
    lefts = [row_of_slots(x[:, row]) for row in range(2)]
    while cols is not None:
        part[:, cols] = dot(lefts[0], block[0]) + dot(lefts[1], block[1])
        cols, block = next(blocks, (None, None))


def above_kernel(above, part, w, rows, held, semaphores):
    cells = above.shape[1]
    blocks = streamed(w, slice(0, 1), held, semaphores)
    cols, block = next(blocks)
    left = row_of_slots(above[...])
    while cols is not None:
        out = part[:, cols] + dot(left, block[0])
        for slot in range(above.shape[0]):
            rows[slot, :, cols] = out[slot * cells : (slot + 1) * cells].astype(BF)
        cols, block = next(blocks, (None, None))


def whole_kernel(counts, *rest):
    parts, (down_pre, keep, pay, scal, semaphore) = rest[:-5], rest[-5:]
    put_scalars(down_pre.shape[0], counts, scal)
    total = jnp.zeros((8, down_pre.shape[1]), F32)
    for k, part in enumerate(parts):
        width = part.shape[0] // 2
        for side in range(2):
            start = image_row(k, side) * width

            def body(index, total, part=part, side=side, start=start, width=width):
                src = pl.ds(pl.multiple_of(side * width + index * CHUNK, CHUNK), CHUNK)
                dst = pl.ds(pl.multiple_of(start + index * CHUNK, CHUNK), CHUNK)
                down_pre[dst, :] = part[src, :]
                return total + fold(part[src, :].astype(F32))

            total = lax.fori_loop(0, width // CHUNK, body, total)
    copy = pltpu.make_async_copy(down_pre, keep, semaphore)
    copy.start()
    total = jnp.sum(total, axis=0, keepdims=True)
    mean = total * (1.0 / down_pre.shape[0])

    def spread(rows, squares):
        off = down_pre[rows, :].astype(F32) - mean
        return squares + fold(off * off)

    squares = rows_loop(down_pre.shape[0], spread, jnp.zeros((8, down_pre.shape[1]), F32))
    pay[0:1, :] = total * scal[0:1, :]
    pay[1:2, :] = jnp.sum(squares, axis=0, keepdims=True) * scal[0:1, :]
    copy.wait()


def main_kernel(groups, scal, *rest):
    refs = rest[:groups]
    down_pre, params, w_main, sectioned, main_pre, main_keep, pay, coef, semaphore = rest[groups:]
    center, rstd = finish_moments(scal, refs)
    coef[0:1, :] = center
    coef[1:2, :] = rstd
    scale, offset = rstd * row_of(params, GAIN_WIDE, 0), row_of(params, SHIFT_WIDE, 0)

    def body(rows, _):
        value = (down_pre[rows, :].astype(F32) - center) * scale + offset
        sectioned[rows, :] = mish(value).astype(BF)

    rows_loop(down_pre.shape[0], body)
    project(sectioned, w_main, main_pre, pay, scal)
    copy = pltpu.make_async_copy(main_pre, main_keep, semaphore)
    copy.start()
    copy.wait()


def short_kernel(scal, sectioned, w_short, short_pre, pay):
    project(sectioned, w_short, short_pre, pay, scal)


def inner_kernel(groups, scal, *rest):
    refs = rest[:groups]
    pre, params, w_inner, mainline, inner_pre, pay, coef = rest[groups:]
    half = pre.shape[1]
    center, rstd = finish_moments(scal, refs)
    coef[0:1, :] = center
    coef[1:2, :] = rstd
    scale, offset = rstd * row_of(params, GAIN, 1, half), row_of(params, SHIFT, 1, half)

    def body(rows, _):
        mainline[rows, :] = mish((pre[rows, :] - center) * scale + offset).astype(BF)

    rows_loop(pre.shape[0], body)
    project(mainline, w_inner, inner_pre, pay, scal)


def three_shifts(values, rim, start, forward):
    width, half = values.shape
    place = lax.broadcasted_iota(jnp.int32, values.shape, 0)
    before = jnp.where(place == 0, 0.0, pltpu.roll(values, 1, 0)).astype(BF)
    after = jnp.where(place == width - 1, 0.0, pltpu.roll(values, width - 1, 0)).astype(BF)
    sides = (before, after) if forward else (after, before)
    rows = pl.ds(start, width)
    rim[rows, 0:half] = sides[0]
    rim[rows, half : 2 * half] = values.astype(BF)
    rim[rows, 2 * half : 3 * half] = sides[1]


def spatial_kernel(groups, width, scal, *rest):
    refs = rest[:groups]
    pre, params, w_spatial, rim, spatial_pre, pay, coef = rest[groups:]
    cells, half = pre.shape
    center, rstd = finish_moments(scal, refs)
    coef[0:1, :] = center
    coef[1:2, :] = rstd
    scale, offset = rstd * row_of(params, GAIN, 2, half), row_of(params, SHIFT, 2, half)
    blank = jnp.zeros((width, 3 * half), BF)
    rim[0:width, :] = blank
    rim[width + cells :, :] = blank

    def body(index, _):
        start = pl.multiple_of(index * width, width)
        act = mish((pre[pl.ds(start, width), :] - center) * scale + offset)
        three_shifts(act, rim, pl.multiple_of(start + width, width), True)

    lax.fori_loop(0, cells // width, body, None)
    w_spatial = w_spatial.ready()
    for begin in range(0, half, COLS):
        cols = slice(begin, begin + COLS)
        out = sum(
            dot(
                rim[i * width : i * width + cells, :],
                w_spatial[i * 3 * half : (i + 1) * 3 * half, cols],
            )
            for i in range(3)
        )
        spatial_pre[:, cols] = out
        put_moments(out, pay, cols, scal)


def trans_kernel(groups, scal, *rest):
    refs = rest[:groups]
    pre, mainline, params, w_trans, merged, trans_pre, pay, coef = rest[groups:]
    half = pre.shape[1]
    center, rstd = finish_moments(scal, refs)
    coef[0:1, :] = center
    coef[1:2, :] = rstd
    scale, offset = rstd * row_of(params, GAIN, 3, half), row_of(params, SHIFT, 3, half)

    def body(rows, _):
        act = mish((pre[rows, :] - center) * scale + offset)
        merged[rows, :] = (mainline[rows, :].astype(F32) + act).astype(BF)

    rows_loop(pre.shape[0], body)
    project(merged, w_trans, trans_pre, pay, scal)


def shortcut_kernel(groups, scal, *rest):
    refs = rest[:groups]
    pre, params, w_unite, shortcut, part, coef = rest[groups:]
    half = pre.shape[1]
    center, rstd = finish_moments(scal, refs)
    coef[0:1, :] = center
    coef[1:2, :] = rstd
    scale, offset = rstd * row_of(params, GAIN, 0, half), row_of(params, SHIFT, 0, half)

    def body(rows, _):
        shortcut[rows, :] = mish((pre[rows, :] - center) * scale + offset).astype(BF)

    rows_loop(pre.shape[0], body)
    w_unite = w_unite.ready()
    for start in range(0, part.shape[1], COLS):
        cols = slice(start, start + COLS)
        part[:, cols] = dot(shortcut[...], w_unite[:, cols])


def unite_kernel(groups, scal, *rest):
    refs = rest[:groups]
    pre, part, params, w_unite, transition, unite_pre, pay, coef = rest[groups:]
    half = pre.shape[1]
    center, rstd = finish_moments(scal, refs)
    coef[0:1, :] = center
    coef[1:2, :] = rstd
    scale, offset = rstd * row_of(params, GAIN, 4, half), row_of(params, SHIFT, 4, half)

    def body(rows, _):
        transition[rows, :] = mish((pre[rows, :] - center) * scale + offset).astype(BF)

    rows_loop(pre.shape[0], body)
    project(transition, w_unite.ready(), unite_pre, pay, scal, part)


def turn_kernel(groups, pieces, scal, *rest):
    refs = rest[:groups]
    pre, params = rest[groups : groups + 2]
    parts = rest[groups + 2 : groups + 2 + pieces]
    pushed, *outputs, pay, coef = rest[groups + 2 + pieces :]
    center, rstd = finish_moments(scal, refs)
    coef[0:1, :] = center
    coef[1:2, :] = rstd
    gain, offset, weight = row_of(params, GAIN_WIDE, 1), row_of(params, SHIFT_WIDE, 1), scal[0:1, 0 : pre.shape[1]]
    sums = (jnp.zeros((8, pre.shape[1]), F32),) * 2
    for k, part in enumerate(parts):
        part = part.ready()
        width = part.shape[0] // 2
        for side in range(2):
            start = image_row(k, side) * width

            def body(index, sums, k=k, part=part, side=side, start=start, width=width):
                src = pl.ds(pl.multiple_of(side * width + index * 16, 16), 16)
                dst = pl.ds(pl.multiple_of(start + index * 16, 16), 16)
                unit = (pre[dst, :] - center) * rstd
                value = unit * gain + offset
                grown = jnp.exp(jnp.minimum(value, FAR))
                wide = grown * (grown + 2.0)
                share = 1.0 / (wide + 2.0)
                level = wide * share
                if k == 0:
                    rows = pl.ds(pl.multiple_of(index * 16, 16), 16)
                    outputs[side][rows, :] = (value * level * weight).astype(BF)
                slope = level + 4.0 * value * (grown * (grown + 1.0) * share) * share
                out = part[src, :].astype(F32) * weight * slope
                pushed[dst, :] = out
                return sums[0] + fold(out), sums[1] + fold(out * unit)

            sums = lax.fori_loop(0, width // 16, body, sums)
    pay[0:1, :] = jnp.sum(sums[0], axis=0, keepdims=True)
    pay[1:2, :] = jnp.sum(sums[1], axis=0, keepdims=True)


def back_trans_kernel(groups, scal, *rest):
    refs = rest[:groups]
    (
        unite_pushed, unite_pre, unite_coef, params, trans_pre, trans_coef, w_unite,
        grad_unite, sums, pushed, pay, scratch,
    ) = rest[groups:]
    half = trans_pre.shape[1]
    settle(scal, refs, unite_pushed, unite_pre, unite_coef, row_of(params, GAIN_WIDE, 1), grad_unite, sums)
    w_unite = w_unite.ready()
    for start in range(0, half, COLS):
        scratch[:, start : start + COLS] = dot_back(
            grad_unite[...], w_unite[start : start + COLS, :]
        )
    push(
        lambda rows: scratch[rows, :],
        trans_pre, trans_coef[0:1, :], trans_coef[1:2, :], row_of(params, GAIN, 4, half), row_of(params, SHIFT, 4, half),
        pushed, pay,
    )


def back_short_kernel(grad_unite, pre, coef, params, w_unite, pushed, pay, scratch):
    half = pre.shape[1]
    w_unite = w_unite.ready()
    for start in range(0, half, COLS):
        scratch[:, start : start + COLS] = dot_back(
            grad_unite[...], w_unite[start : start + COLS, :]
        )
    push(
        lambda rows: scratch[rows, :],
        pre, coef[0:1, :], coef[1:2, :], row_of(params, GAIN, 0, half), row_of(params, SHIFT, 0, half), pushed, pay,
    )


def back_spatial_kernel(groups, scal, *rest):
    refs = rest[:groups]
    (
        trans_pushed, trans_pre, trans_coef, spatial_pre, spatial_coef, params, w_trans,
        grad_trans, sums, grad_merged, pushed, pay,
    ) = rest[groups:]
    half = trans_pre.shape[1]
    settle(scal, refs, trans_pushed, trans_pre, trans_coef, row_of(params, GAIN, 4, half), grad_trans, sums)
    w_trans = w_trans.ready()
    for start in range(0, half, COLS):
        grad_merged[:, start : start + COLS] = dot_back(
            grad_trans[...], w_trans[start : start + COLS, :]
        )
    push(
        lambda rows: grad_merged[rows, :],
        spatial_pre, spatial_coef[0:1, :], spatial_coef[1:2, :], row_of(params, GAIN, 3, half), row_of(params, SHIFT, 3, half),
        pushed, pay,
    )


def back_inner_kernel(groups, width, scal, *rest):
    refs = rest[:groups]
    (
        spatial_pushed, spatial_pre, spatial_coef, inner_pre, inner_coef, params, w_spatial,
        grad_spatial, sums, pushed, pay, rim, scratch,
    ) = rest[groups:]
    cells, half = spatial_pre.shape
    settle(scal, refs, spatial_pushed, spatial_pre, spatial_coef, row_of(params, GAIN, 3, half), grad_spatial, sums)
    blank = jnp.zeros((width, 3 * half), BF)
    rim[0:width, :] = blank
    rim[width + cells :, :] = blank

    def body(index, _):
        start = pl.multiple_of(index * width, width)
        values = grad_spatial[pl.ds(start, width), :].astype(F32)
        three_shifts(values, rim, pl.multiple_of(start + width, width), False)

    lax.fori_loop(0, cells // width, body, None)
    w_spatial = w_spatial.ready()
    for start in range(0, half, COLS):
        scratch[:, start : start + COLS] = sum(
            dot_back(
                rim[(2 - i) * width : (2 - i) * width + cells, j * half : (j + 1) * half],
                w_spatial[(3 * i + j) * half + start : (3 * i + j) * half + start + COLS, :],
            )
            for i in range(3)
            for j in range(3)
        )
    push(
        lambda rows: scratch[rows, :],
        inner_pre, inner_coef[0:1, :], inner_coef[1:2, :], row_of(params, GAIN, 2, half), row_of(params, SHIFT, 2, half),
        pushed, pay,
    )


def back_main_kernel(groups, scal, *rest):
    refs = rest[:groups]
    (
        inner_pushed, inner_pre, inner_coef, grad_merged, main_pre, main_coef, params, w_inner,
        grad_inner, sums, pushed, pay, scratch,
    ) = rest[groups:]
    half = inner_pre.shape[1]
    settle(scal, refs, inner_pushed, inner_pre, inner_coef, row_of(params, GAIN, 2, half), grad_inner, sums)
    w_inner = w_inner.ready()
    for start in range(0, half, COLS):
        cols = slice(start, start + COLS)
        scratch[:, cols] = grad_merged[:, cols] + dot_back(grad_inner[...], w_inner[cols, :])
    push(
        lambda rows: scratch[rows, :],
        main_pre, main_coef[0:1, :], main_coef[1:2, :], row_of(params, GAIN, 1, half), row_of(params, SHIFT, 1, half),
        pushed, pay,
    )


def settle_short_kernel(groups, scal, *rest):
    refs = rest[:groups]
    pushed, pre, coef, params, grad_short, sums = rest[groups:]
    half = pre.shape[1]
    settle(scal, refs, pushed, pre, coef, row_of(params, GAIN, 0, half), grad_short, sums)


def back_down_kernel(groups, scal, *rest):
    refs = rest[:groups]
    (
        main_pushed, main_coef, down_coef, params, main_pre, w_main, grad_short, w_short, down_pre,
        grad_main, sums, pushed, pay, scratch,
    ) = rest[groups:]
    main_pre = main_pre.ready()
    half = main_pre.shape[1]
    settle(scal, refs, main_pushed, main_pre, main_coef, row_of(params, GAIN, 1, half), grad_main, sums)
    w_main, grad_short, w_short = w_main.ready(), grad_short.ready(), w_short.ready()
    for start in range(0, pushed.shape[1], COLS):
        cols = slice(start, start + COLS)
        scratch[:, cols] = dot_back(grad_short[...], w_short[cols, :]) + dot_back(
            grad_main[...], w_main[cols, :]
        )
    push(
        lambda rows: scratch[rows, :],
        down_pre.ready(), down_coef[0:1, :], down_coef[1:2, :],
        row_of(params, GAIN_WIDE, 0), row_of(params, SHIFT_WIDE, 0),
        pushed, pay,
    )


def settle_down_kernel(groups, scal, *rest):
    refs = rest[:groups]
    pushed, pre, coef, params, grad_down, sums = rest[groups:]
    settle(scal, refs, pushed, pre, coef, row_of(params, GAIN_WIDE, 0), grad_down, sums)
    cells = pre.shape[0]
    grad_down[cells:, :] = jnp.zeros((grad_down.shape[0] - cells, pre.shape[1]), BF)


def cut_down_kernel(groups, scal, *rest):
    refs = rest[:groups]
    pushed, pre, coef, params, cut = rest[groups:]
    width = cut.shape[1]
    cols = pl.ds(pl.multiple_of(own_chip() * width, width), width)
    first, second = finish_sums(refs, cols)
    over = 1.0 / scal[1:2, 0:width]
    center, rstd = coef[0:1, cols], coef[1:2, cols]
    scale = params[GAIN_WIDE : GAIN_WIDE + 1, cols] * rstd * scal[0:1, 0:width]
    level, tilt = first * over, second * over * rstd

    def body(rows, _):
        x = pre[rows, cols].astype(F32) - center
        cut[rows, :] = (scale * (pushed[rows, cols] - level - x * tilt)).astype(BF)

    rows_loop(pre.shape[0], body)


def by_place(first, second):
    low = own_core() == 0
    return jnp.where(low, first, second), jnp.where(low, second, first)


def share_unite_kernel(shortcut, transition, grad, mine, other):
    width = 2 * mine.shape[1]
    cut = grad[:, pl.ds(pl.multiple_of(own_chip() * width, width), width)]
    half = shortcut.shape[1]
    for k, values in enumerate((shortcut, transition)):
        out = dot_cells(values[...], cut)
        near, far = by_place(out[:, : width // 2], out[:, width // 2 :])
        mine[k * half : (k + 1) * half, :] = near.astype(BF)
        other[k * half : (k + 1) * half, :] = far.astype(BF)


def put_halves(cut, values, start, mine, other):
    out = dot_cells(cut, values)
    rows, cols = mine.shape[0], slice(start, start + out.shape[1])
    near, far = by_place(out[:rows], out[rows:])
    mine[:, cols] = near.astype(BF)
    other[:, cols] = far.astype(BF)


def chip_columns(mine):
    width = 2 * mine.shape[0]
    return pl.ds(pl.multiple_of(own_chip() * width, width), width)


def share_pack_kernel(*rest):
    pairs, (mine, other) = rest[:-2], rest[-2:]
    cols = chip_columns(mine)
    start = 0
    for values, grad in zip(pairs[::2], pairs[1::2]):
        put_halves(grad[:, cols], values[...], start, mine, other)
        start += values.shape[1]


def share_spatial_kernel(cells, rim, grad, mine, other):
    cut = grad[:, chip_columns(mine)]
    line, side = (rim.shape[0] - cells) // 2, rim.shape[1]
    for row in range(3):
        put_halves(cut, rim[row * line : row * line + cells, :], row * side, mine, other)


def share_main_kernel(grad, grad_inner, sectioned, mainline, mine, other):
    cols = chip_columns(mine)
    sectioned, mainline = sectioned.ready(), mainline.ready()
    put_halves(grad[:, cols], sectioned[...], 0, mine, other)
    put_halves(grad_inner[:, cols], mainline[...], sectioned.shape[1], mine, other)


def finish_kernel(planes, unite, pack, taps, *rest):
    mains, (mine, got, near, far) = rest[:planes], rest[planes : planes + 4]
    rest = rest[planes + 4 :]
    w_unite, w_short, w_trans, w_inner, w_spatial, w_main, output, grad_inputs = rest[:8]
    *held, semaphores = rest[8:]
    sums = [Far(a, b, semaphores.at[4 + k]) for k, (a, b) in enumerate(zip((unite, pack, taps), held))]
    core = own_core()
    copies = [
        pltpu.make_async_copy(mine, output.at[core, 0], semaphores.at[0]),
        pltpu.make_async_copy(got, output.at[1 - core, 0], semaphores.at[1]),
        pltpu.make_async_copy(near.at[0], grad_inputs.at[core], semaphores.at[2]),
        pltpu.make_async_copy(far.at[1], grad_inputs.at[1 - core], semaphores.at[3]),
    ]
    for copy in copies:
        copy.start()
    unite, pack, taps = (one.ready() for one in sums)
    w_unite[...] = unite[...].astype(F32)
    for outs, values in (
        ((w_short, w_trans), pack[...].astype(F32)),
        ((w_main, w_inner), tree_sum([main[...].astype(F32) for main in mains])),
    ):
        start = 0
        for out in outs:
            out[...] = values[:, start : start + out.shape[1]]
            start += out.shape[1]
    half = w_trans.shape[1]
    for tap in range(w_spatial.shape[0]):
        w_spatial[tap] = taps[:, tap * half : (tap + 1) * half].astype(F32)
    for copy in copies:
        copy.wait()


def norm_sums_kernel(wide_count, *refs):
    sums, outs = refs[:-4], refs[-4:]
    for k, pair in enumerate(sums):
        index = k if k < wide_count else k - wide_count
        for row, out in ((1, outs[0 if k < wide_count else 1]), (0, outs[2 if k < wide_count else 3])):
            out[index : index + 1, :] = pair[row : row + 1, :]


def share_down_kernel(steps, chips, width, last_call, *rest):
    grads = rest[: len(steps)]
    earlier = rest[len(steps) : len(steps) + 2 * last_call]
    rest = rest[len(steps) + 2 * last_call :]
    source, outs, rest = rest[0], rest[1:3], rest[3:]
    if last_call:
        odd_acc, even_acc = rest[:2]
        rest = rest[2:]
    else:
        odd_acc, even_acc = outs
    padded, sides, held, semaphores = rest
    cells, columns = grads[0].shape
    half = source.shape[-1] // 2
    planes = source.shape[0] // (2 * chips)
    copies = []
    for k, step in enumerate(steps):
        plane = lax.axis_index("batch") ^ step
        copies.append(
            [
                pltpu.make_async_copy(
                    source.at[row * planes + plane, own_core()], held.at[k, row], semaphores.at[k, row]
                )
                for row in range(2 * chips)
            ]
        )
        for copy in copies[-1]:
            copy.start()
    padded[cells:, :] = jnp.zeros((padded.shape[0] - cells, columns), BF)
    last = lax.broadcasted_iota(jnp.int32, (width, columns), 0) == width - 1

    def ahead(values):
        return jnp.where(last, 0.0, pltpu.roll(values.astype(F32), width - 1, 0)).astype(BF)

    for k in range(len(steps)):
        padded[0:cells, :] = grads[k][...]
        for block in range(2 * chips):
            rows = slice(block * width, (block + 1) * width)
            here = padded[rows, :]
            upper = padded[(block + 1) * width : (block + 2) * width, :]
            sides[rows, 0:columns] = upper
            sides[rows, columns : 2 * columns] = here
            sides[rows, 2 * columns : 3 * columns] = ahead(here)
            sides[rows, 3 * columns : 4 * columns] = ahead(upper)
        for copy in copies[k]:
            copy.wait()

        def add(which, side, start, values, k=k):
            rows, cols = slice(side * half, (side + 1) * half), slice(start, start + columns)
            acc = (even_acc, odd_acc)[which]
            if k > 0:
                values = values + acc[rows, cols]
            elif last_call:
                values = values + earlier[1 - which][rows, cols]
            acc[rows, cols] = values

        for which in range(2):
            for side in range(2):
                left = held[k, :, which, :, side * half : (side + 1) * half].reshape(cells, half)
                for block in range(4):
                    if (which == 0 and block in (0, 3)) or (side == 0 and block in (2, 3)):
                        continue
                    start = block * columns
                    add(which, side, start, dot_cells(left, sides[:, start : start + columns]))
    if not last_call:
        return
    mine, other = outs
    places = (
        (odd_acc, 1, 3), (odd_acc, 0, 0), (odd_acc, 1, 0),
        (even_acc, 1, 2), (even_acc, 0, 1), (even_acc, 1, 1),
        (odd_acc, 1, 2), (odd_acc, 0, 1), (odd_acc, 1, 1),
    )
    for tap, (acc, side, block) in enumerate(places):
        values = acc[side * half : (side + 1) * half, block * columns : (block + 1) * columns]
        near, far = by_place(values[:, : columns // 2], values[:, columns // 2 :])
        mine[tap * half : (tap + 1) * half, :] = near.astype(BF)
        other[tap * half : (tap + 1) * half, :] = far.astype(BF)


def back_input_kernel(width, grad, w, out, near, far):
    cells = 2 * width
    full = grad.shape[1]

    @pl.when(pl.program_id(0) == 0)
    def _():
        last = lax.broadcasted_iota(jnp.int32, (width, full), 0) == width - 1
        for block in range(3):
            start = pl.multiple_of(own_chip() * cells + block * width, width)
            values = grad[pl.ds(start, width), :]
            rows = slice(block * width, (block + 1) * width)
            near[rows, :] = values
            far[rows, :] = jnp.where(
                last, 0.0, pltpu.roll(values.astype(F32), width - 1, 0)
            ).astype(BF)

    low, high = slice(0, cells), slice(width, width + cells)

    def term(values, rows, i, j):
        return dot_back(values[rows, :], w[3 * i + j])

    def put(parity, column, values):
        for row in range(2):
            out[row ^ own_core(), parity, pl.ds(column, width, stride=2), :] = values[
                row * width : (row + 1) * width
            ]

    put(0, 0, term(near, low, 1, 1))
    put(0, 1, term(near, low, 1, 2) + term(far, low, 1, 0))
    put(1, 0, term(near, high, 0, 1) + term(near, low, 2, 1))
    put(
        1,
        1,
        term(near, high, 0, 2) + term(far, high, 0, 0) + term(near, low, 2, 2) + term(far, low, 2, 0),
    )


SMEM = pl.BlockSpec(memory_space=pltpu.SMEM)
VMEM = pl.BlockSpec(memory_space=pltpu.VMEM)
ANY = pl.BlockSpec(memory_space=pl.ANY)


def shape(dims, dtype=F32):
    return jax.ShapeDtypeStruct(dims, dtype)


def nbytes(dims, dtype):
    count = 1
    for d in dims:
        count *= d
    return count * jnp.dtype(dtype).itemsize


def in_vmem(value):
    return pltpu.with_memory_space_constraint(value, pltpu.VMEM)


def in_hbm(value):
    return pltpu.with_memory_space_constraint(value, pltpu.HBM)


LIGHT = pl.CostEstimate(flops=0, bytes_accessed=0, transcendentals=0)


def call(kernel, name, scalars, near, outs, flops, scratch=(), far=(), pin=False, spill=(), light=False, out=(), late=False):
    cuts = [one[1] if isinstance(one, tuple) else None for one in far]
    far = [one[0] if isinstance(one, tuple) else one for one in far]
    held_far = [
        shape((cut.stop - cut.start,) + a.shape[1:], a.dtype) if cut else a for a, cut in zip(far, cuts)
    ]
    moved = sum(nbytes(a.shape, a.dtype) for a in (*near, *far, *outs))
    scratch = [s if hasattr(s, "memory_space") or not hasattr(s, "shape") else pltpu.VMEM(s.shape, s.dtype) for s in scratch]
    held = moved + sum(nbytes(s.shape, s.dtype) for s in scratch if hasattr(s, "shape"))
    if pin:
        held -= moved - sum(nbytes(a.shape, a.dtype) for a in far)
        held += sum(nbytes(outs[k].shape, outs[k].dtype) for k in spill)
        near, far = [in_vmem(a) for a in near], [in_hbm(a) for a in far]
        outs = [
            o if k in spill else (pltpu.HBM if k in out else pltpu.VMEM)(o.shape, o.dtype)
            for k, o in enumerate(outs)
        ]
    before, after_far, last = len(scalars) + len(near), len(far), len(outs) + len(scratch)

    def body(*refs):
        sources, rest = refs[before : before + after_far], refs[before + after_far :]
        targets = rest[last : last + after_far]
        fars = [
            Far(a.at[cut] if cut else a, b, rest[-1].at[k])
            for k, (a, b, cut) in enumerate(zip(sources, targets, cuts))
        ]
        kernel(*refs[:before], *fars, *rest[:last])
        for one in fars:
            one.ready()

    return pl.pallas_call(
        body if far else kernel,
        name=name,
        out_shape=tuple(outs),
        in_specs=[SMEM] * len(scalars) + [VMEM] * len(near) + [ANY] * len(far),
        out_specs=tuple(ANY if k in out and not late else VMEM for k in range(len(outs))),
        scratch_shapes=scratch
        + [pltpu.VMEM(a.shape, a.dtype) for a in held_far]
        + ([pltpu.SemaphoreType.DMA((len(far),))] if far else []),
        compiler_params=pltpu.CompilerParams(vmem_limit_bytes=held + (8 << 20)),
        cost_estimate=LIGHT if light else pl.CostEstimate(flops=flops, bytes_accessed=moved, transcendentals=0),
    )(*scalars, *near, *far)


def first_conv(view, above, w_down, pin):
    slots, _, cells, both = view.shape
    half = both // 2
    full = w_down.shape[-1]
    taps = w_down.reshape(3, 3 * half, full)
    if pin:
        view, above, taps = in_vmem(view), in_vmem(above), in_hbm(taps)
    wide = 256
    count = full // wide

    def run(kernel, name, rows, values, out):
        return pl.pallas_call(
            kernel,
            name=name,
            out_shape=(pltpu.VMEM if pin else shape)(out.shape, out.dtype),
            in_specs=[VMEM] * len(values) + [ANY],
            out_specs=VMEM,
            scratch_shapes=[
                pltpu.VMEM((count, rows, 3 * half, wide), BF), pltpu.SemaphoreType.DMA((count,))
            ],
            compiler_params=pltpu.CompilerParams(vmem_limit_bytes=24 << 20),
            cost_estimate=pl.CostEstimate(
                flops=6 * rows * slots * cells * half * full,
                bytes_accessed=6 * rows * half * full,
                transcendentals=0,
            ),
        )(*values, taps)

    part = run(own_kernel, "own", 2, [view], shape((slots * cells, full)))
    part = in_vmem(part) if pin else part
    return run(above_kernel, "above", 1, [above, part], shape((slots, cells, full), BF))


def flipped(kernel):
    return jnp.swapaxes(jnp.flip(kernel, (0, 1)), 2, 3)


def on_device(
    inputs,
    image_counts,
    w_down,
    w_short,
    w_main,
    w_inner,
    w_spatial,
    w_trans,
    w_unite,
    gains_wide,
    gains_narrow,
    shifts_wide,
    shifts_narrow,
    grad_output,
):
    half = w_short.shape[1]
    full = 2 * half
    slots, height_dev, width, _ = grad_output.shape
    here = Plane()
    wide = here.chips == 4 and half % (128 * here.chips) == 0
    stage = functools.partial(call, pin=wide)
    groups, chips = here.groups, here.chips
    height = here.rows * height_dev
    cells = height * width
    batch = lax.axis_index("batch")
    view = inputs.reshape(slots, 2, width, 2 * half)
    below = [(i, i + 1) for i in range(here.rows - 1)]
    above = lax.ppermute(view[:, 1], "rows", below)
    params = jnp.concatenate(
        [gains_wide, shifts_wide]
        + [jnp.pad(p, ((0, 0), (0, half))) for p in (gains_narrow, shifts_narrow)]
    )
    down_rows = first_conv(view, above, w_down, wide)
    down_pieces = here.pieces(*here.split(down_rows))
    grad_mine, grad_other = here.split(grad_output.reshape(slots, width, full))
    down_pieces[1], params, grad_mine, grad_other = lax.optimization_barrier(
        (down_pieces[1], params, grad_mine, grad_other)
    )
    down_pre, down_keep, down_pay, scal = stage(
        whole_kernel,
        "whole",
        [image_counts],
        down_pieces,
        [
            shape((cells, full), BF), shape((cells, full), BF), shape((2, full)),
            shape((2 + 4 * groups, full)),
        ],
        10 * cells * full,
        out=(1,),
        scratch=[pltpu.SemaphoreType.DMA],
    )
    if wide:
        flat = after(view, down_pay).reshape(slots * 2 * width, 2 * half)
        source = lax.all_gather(flat, ("rows", "batch")).reshape(-1, *view.shape)
        grad_piece = jnp.concatenate([grad_mine, here.swap(after(grad_other, down_pay))], axis=0)
        grad_pieces = [grad_piece, here.chip_hop(grad_piece, 1), here.chip_hop(grad_piece, 2)]
        grad_pieces.append(here.chip_hop(grad_pieces[1], 2))
    else:
        grad_pieces = here.pieces(grad_mine, grad_other)
    sectioned, main_pre, main_keep, main_pay, down_coef = stage(
        functools.partial(main_kernel, groups),
        "main",
        [],
        [scal, *here.everywhere(down_pay), down_pre, params],
        [
            shape((cells, full), BF), shape((cells, half)), shape((cells, half)),
            shape((2, half)), shape((2, full)),
        ],
        2 * cells * full * half,
        far=[w_main],
        out=(2,),
        scratch=[pltpu.SemaphoreType.DMA],
    )

    if wide:
        main_pay = after(main_pay, *grad_pieces[:3])
    main_all = here.everywhere(main_pay)
    short_pre, short_pay = stage(
        short_kernel,
        "short",
        [],
        [scal, sectioned],
        [shape((cells, half)), shape((2, half))],
        2 * cells * full * half,
        far=[w_short],
    )
    mainline, inner_pre, inner_pay, main_coef = stage(
        functools.partial(inner_kernel, groups),
        "inner",
        [],
        [scal, *main_all, main_pre, params],
        [shape((cells, half), BF), shape((cells, half)), shape((2, half)), shape((2, half))],
        2 * cells * half * half,
        far=[w_inner],
    )
    inner_all = here.everywhere(inner_pay)
    rim, spatial_pre, spatial_pay, inner_coef = stage(
        functools.partial(spatial_kernel, groups, width),
        "spatial",
        [],
        [scal, *inner_all, inner_pre, params],
        [
            shape((cells + 2 * width, 3 * half), BF), shape((cells, half)),
            shape((2, half)), shape((2, half)),
        ],
        18 * cells * half * half,
        far=[w_spatial.reshape(9 * half, half)],
    )
    if wide:
        spatial_pay = after(spatial_pay, grad_pieces[3])
    both_all = here.everywhere(jnp.concatenate([spatial_pay, short_pay], axis=1))
    spatial_all = [b[:, :half] for b in both_all]
    short_all = [b[:, half:] for b in both_all]
    merged, trans_pre, trans_pay, spatial_coef = stage(
        functools.partial(trans_kernel, groups),
        "trans",
        [],
        [scal, *spatial_all, spatial_pre, mainline, params],
        [shape((cells, half), BF), shape((cells, half)), shape((2, half)), shape((2, half))],
        2 * cells * half * half,
        far=[w_trans],
    )
    trans_all = here.everywhere(trans_pay)
    shortcut, unite_part, short_coef = stage(
        functools.partial(shortcut_kernel, groups),
        "shortcut",
        [],
        [scal, *short_all, short_pre, params],
        [shape((cells, half), BF), shape((cells, full)), shape((2, half))],
        2 * cells * half * full,
        far=[(w_unite, slice(0, half))],
    )
    transition, unite_pre, unite_pay, trans_coef = stage(
        functools.partial(unite_kernel, groups),
        "unite",
        [],
        [scal, *trans_all, trans_pre, unite_part, params],
        [shape((cells, half), BF), shape((cells, full)), shape((2, full)), shape((2, half))],
        2 * cells * half * full,
        far=[(w_unite, slice(half, full))],
    )
    unite_all = here.everywhere(unite_pay)
    unite_pushed, mine, other, unite_pay, unite_coef = stage(
        functools.partial(turn_kernel, groups, chips),
        "turn",
        [],
        [scal, *unite_all, unite_pre, params],
        [
            shape((cells, full)), shape((width, full), BF), shape((width, full), BF),
            shape((2, full)), shape((2, full)),
        ],
        40 * cells * full,
        far=grad_pieces,
        spill=(1, 2),
    )
    output_rows = (mine, here.swap(other))

    unite_all = here.everywhere(unite_pay)
    grad_unite_pre, unite_sums, trans_pushed, trans_pay = stage(
        functools.partial(back_trans_kernel, groups),
        "back_trans",
        [],
        [scal, *unite_all, unite_pushed, unite_pre, unite_coef, params, trans_pre, trans_coef],
        [shape((cells, full), BF), shape((2, full)), shape((cells, half)), shape((2, half))],
        2 * cells * half * full,
        [shape((cells, half))],
        far=[(w_unite, slice(half, full))],
    )
    trans_all = here.everywhere(trans_pay)
    if wide:

        def of_pair(pair):
            mine, other = pair
            return (mine.astype(F32) + here.swap(other).astype(F32)).astype(BF)

        share_unite = of_pair(
            stage(
                share_unite_kernel,
                "share_unite",
                [],
                [shortcut, transition, grad_unite_pre],
                [shape((full, full // chips // 2), BF)] * 2,
                2 * cells * full * full // chips,
            )
        )
    short_pushed, short_pay = stage(
        back_short_kernel,
        "back_short",
        [],
        [grad_unite_pre, short_pre, short_coef, params],
        [shape((cells, half)), shape((2, half))],
        2 * cells * half * full,
        [shape((cells, half))],
        far=[(w_unite, slice(0, half))],
    )
    grad_trans_pre, trans_sums, grad_merged, spatial_pushed, spatial_pay = stage(
        functools.partial(back_spatial_kernel, groups),
        "back_spatial",
        [],
        [scal, *trans_all, trans_pushed, trans_pre, trans_coef, spatial_pre, spatial_coef, params],
        [
            shape((cells, half), BF), shape((2, half)), shape((cells, half)), shape((cells, half)),
            shape((2, half)),
        ],
        2 * cells * half * half,
        far=[w_trans],
    )
    both_all = here.everywhere(jnp.concatenate([spatial_pay, short_pay], axis=1))
    spatial_all = [b[:, :half] for b in both_all]
    short_all = [b[:, half:] for b in both_all]
    grad_spatial_pre, spatial_sums, inner_pushed, inner_pay = stage(
        functools.partial(back_inner_kernel, groups, width),
        "back_inner",
        [],
        [scal,
            *spatial_all, spatial_pushed, spatial_pre, spatial_coef, inner_pre, inner_coef, params,
        ],
        [shape((cells, half), BF), shape((2, half)), shape((cells, half)), shape((2, half))],
        18 * cells * half * half,
        [shape((cells + 2 * width, 3 * half), BF), shape((cells, half))],
        far=[w_spatial.reshape(9 * half, half)],
    )
    inner_all = here.everywhere(inner_pay)
    grad_short_pre, short_sums = stage(
        functools.partial(settle_short_kernel, groups),
        "settle_short",
        [],
        [scal, *short_all, short_pushed, short_pre, short_coef, params],
        [shape((cells, half), BF), shape((2, half))],
        10 * cells * half,
    )
    if wide:
        lean = half // chips // 2
        share_spatial = of_pair(
            stage(
                functools.partial(share_spatial_kernel, cells),
                "share_spatial",
                [],
                [rim, grad_spatial_pre],
                [shape((lean, 9 * half), BF)] * 2,
                18 * cells * half * half // chips,
            )
        )
        share_pack = of_pair(
            stage(
                share_pack_kernel,
                "share_pack",
                [],
                [sectioned, grad_short_pre, merged, grad_trans_pre],
                [shape((lean, full + half), BF)] * 2,
                6 * cells * half * half // chips,
            )
        )
        inner_all[0], source, *shares = lax.optimization_barrier(
            (inner_all[0], source, share_unite, share_pack, share_spatial)
        )
        shares = lax.psum(tuple(shares), "batch")
    grad_inner_pre, inner_sums, main_pushed, main_pay = stage(
        functools.partial(back_main_kernel, groups),
        "back_main",
        [],
        [scal, *inner_all, inner_pushed, inner_pre, inner_coef, grad_merged, main_pre, main_coef, params],
        [shape((cells, half), BF), shape((2, half)), shape((cells, half)), shape((2, half))],
        2 * cells * half * half,
        [shape((cells, half))],
        far=[w_inner],
    )
    main_all = here.everywhere(main_pay)
    grad_main_pre, main_sums, down_pushed, down_pay = stage(
        functools.partial(back_down_kernel, groups),
        "back_down",
        [],
        [scal, *main_all, main_pushed, main_coef, down_coef, params],
        [shape((cells, half), BF), shape((2, half)), shape((cells, full)), shape((2, full))],
        4 * cells * half * full,
        [shape((cells, full))],
        far=[main_keep, w_main, grad_short_pre, w_short, down_keep], light=True)
    down_all = here.everywhere(down_pay)
    spare = width
    if wide:
        grad_cut = stage(
            functools.partial(cut_down_kernel, groups),
            "cut_down",
            [],
            [scal, *down_all, down_pushed, down_pre, down_coef, params],
            [shape((cells, full // chips), BF)],
            10 * cells * full // chips, light=True)[0]
        cuts = here.plane_hops(grad_cut)
    grad_down_pre, down_sums = stage(
        functools.partial(settle_down_kernel, groups),
        "settle_down",
        [],
        [scal, *down_all, down_pushed, down_pre, down_coef, params],
        [shape((cells + spare, full), BF), shape((2, full))],
        10 * cells * full, light=True)
    if not wide:
        output = jnp.stack(here.by_core(*output_rows)).reshape(grad_output.shape)
    norm_grads = stage(
        functools.partial(norm_sums_kernel, 2),
        "norm_sums",
        [],
        [down_sums, unite_sums, short_sums, main_sums, inner_sums, spatial_sums, trans_sums],
        [shape((2, full)), shape((5, half))] * 2,
        0,
        spill=range(4), light=True)
    if wide:
        near = pl.pallas_call(
            functools.partial(back_input_kernel, width),
            name="back_input",
            grid=(half // 128,),
            out_shape=shape((2, 2, 2 * width, half)),
            in_specs=[
                pl.BlockSpec((cells + spare, full), lambda n: (0, 0)),
                pl.BlockSpec((9, 128, full), lambda n: (0, n, 0)),
            ],
            out_specs=pl.BlockSpec((2, 2, 2 * width, 128), lambda n: (0, 0, 0, n)),
            scratch_shapes=[pltpu.VMEM((3 * width, full), BF)] * 2,
            compiler_params=pltpu.CompilerParams(vmem_limit_bytes=16 << 20),
            cost_estimate=LIGHT,
        )(grad_down_pre, in_hbm(w_down.reshape(9, half, full)))
        share_main = of_pair(
            stage(
                share_main_kernel,
                "share_main",
                [],
                [grad_main_pre, grad_inner_pre],
                [shape((lean, full + half), BF)] * 2,
                6 * cells * half * half // chips,
                far=[sectioned, mainline],
                light=True,
            )
        )
        columns = full // chips
        sums_here = [shape((full, 4 * columns)), shape((full, 4 * columns))]
        halves = [shape((9 * half, columns // 2), BF)] * 2

        def share_down(steps, earlier):
            outs = halves if earlier else sums_here
            near = [*(cuts[step] for step in steps), *earlier]
            scratch = [
                pltpu.VMEM((cells + spare, columns), BF),
                pltpu.VMEM((cells, 4 * columns), BF),
                pltpu.VMEM((len(steps), 2 * chips, 2, width, full), BF),
                pltpu.SemaphoreType.DMA((len(steps), 2 * chips)),
            ]
            if earlier:
                scratch = [pltpu.VMEM(a.shape, F32) for a in sums_here] + scratch
            return pl.pallas_call(
                functools.partial(share_down_kernel, steps, chips, width, int(bool(earlier))),
                name="share_down",
                out_shape=tuple(pltpu.VMEM(o.shape, o.dtype) for o in outs),
                in_specs=[VMEM] * len(near) + [ANY],
                out_specs=(VMEM,) * len(outs),
                scratch_shapes=scratch,
                compiler_params=pltpu.CompilerParams(vmem_limit_bytes=30 << 20),
                cost_estimate=LIGHT,
            )(*map(in_vmem, near), in_hbm(source))

        middle = (groups + 1) // 2
        cuts[:middle], near = lax.optimization_barrier((cuts[:middle], near))
        first_sums = share_down(range(middle), ())
        mains = here.plane_hops(after(share_main, grad_cut))
        cuts[middle:], first_sums = lax.optimization_barrier((cuts[middle:], first_sums))
        mine, other = share_down(range(middle, groups), first_sums)
        other, *tied = lax.optimization_barrier((other, *shares, *mains))
        shares, mains = tied[: len(shares)], tied[len(shares) :]
        grad_w_down = mine.astype(F32) + here.swap(other).astype(F32)
        outs = [
            shape((full, 2 * lean)), shape((lean, full)), shape((lean, half)), shape((lean, half)),
            shape((9, lean, half)), shape((lean, full)),
            shape(grad_output.shape, BF), shape(inputs.shape),
        ]
        placed = [*output_rows, near, here.swap(near)]
        early = pl.pallas_call(
            functools.partial(finish_kernel, groups),
            name="finish",
            out_shape=tuple(outs),
            in_specs=[ANY] * 3 + [VMEM] * groups + [ANY] * 4,
            out_specs=(VMEM,) * 6 + (ANY,) * 2,
            scratch_shapes=[pltpu.VMEM(one.shape, one.dtype) for one in shares]
            + [pltpu.SemaphoreType.DMA((7,))],
            compiler_params=pltpu.CompilerParams(vmem_limit_bytes=24 << 20),
            cost_estimate=LIGHT,
        )(*map(in_hbm, shares), *mains, *placed)
        output, grad_inputs = early[6:]
        early = [
            early[1].T, early[5].T, early[3].T, jnp.swapaxes(early[4], 1, 2), early[2].T, early[0],
        ]
    else:
        grad_down_pre = grad_down_pre[:cells]
        def share(values, grad):
            columns = grad.shape[1] // chips
            grad = lax.dynamic_slice_in_dim(grad, here.chip * columns, columns, 1)
            part = jnp.concatenate([dot_cells(v, grad) for v in values], axis=0)
            mine, other = here.split(part.reshape(part.shape[0], 2, columns // 2), 1)
            return (mine + here.swap(other.astype(BF)).astype(F32)).astype(BF)

        windows = [rim[i * width : i * width + cells] for i in range(3)]
        early = lax.psum(
            (
                share([sectioned], grad_short_pre),
                share([sectioned], grad_main_pre),
                share([mainline], grad_inner_pre),
                share(windows, grad_spatial_pre),
                share([merged], grad_trans_pre),
                jnp.concatenate([share([shortcut], grad_unite_pre), share([transition], grad_unite_pre)]),
            ),
            "batch",
        )
        early = [e.astype(F32) for e in early]

        mine, other = here.split(view)
        got = here.chip_hops(jnp.stack([mine, here.swap(other)], axis=1))
        source = jnp.zeros((2, here.rows, width, full), BF)
        for step, piece in enumerate(got):
            for side in range(2):
                source = lax.dynamic_update_slice_in_dim(
                    source, piece[:, side : side + 1], 2 * (here.chip ^ step) + (here.core ^ side), 1
                )
        grad_map = grad_down_pre.reshape(height, width, full)
        columns = full // chips
        grad_cut = lax.dynamic_slice_in_dim(grad_map, here.chip * columns, columns, 2)
        ahead = jnp.pad(grad_cut[:, 1:], ((0, 0), (0, 1), (0, 0)))
        upper = jnp.pad(grad_cut[1:], ((0, 1), (0, 0), (0, 0)))
        both_ahead = jnp.pad(ahead[1:], ((0, 1), (0, 0), (0, 0)))
        even_rows = source[0].reshape(cells, full)
        odd_rows = source[1].reshape(cells, full)

        def taps_of(rows, here_grad, ahead_grad):
            plain = dot_cells(rows, here_grad.reshape(cells, columns))
            before = dot_cells(rows[:, half:], ahead_grad.reshape(cells, columns))
            return [before, plain]

        part = jnp.concatenate(
            taps_of(odd_rows, upper, both_ahead)
            + taps_of(even_rows, grad_cut, ahead)
            + taps_of(odd_rows, grad_cut, ahead),
            axis=0,
        )
        mine, other = here.split(part.reshape(9 * half, 2, columns // 2), 1)
        part = (mine + here.swap(other.astype(BF)).astype(F32)).astype(BF)
        grad_w_down = lax.psum(part, "batch").astype(F32)

        pair_rows = 2 * height_dev
        grad_image = jnp.pad(grad_map, ((0, 1), (0, 0), (0, 0)))
        grad_block = lax.dynamic_slice_in_dim(grad_image, here.chip * pair_rows, pair_rows + 1, 0)
        widened = lax.conv_general_dilated(
            grad_block[None],
            flipped(w_down),
            (1, 1),
            ((1, 0), (1, 2)),
            lhs_dilation=(2, 2),
            dimension_numbers=("NHWC", "HWIO", "NHWC"),
            preferred_element_type=F32,
        )[0]
        mine = lax.dynamic_slice_in_dim(widened, here.core * pair_rows, pair_rows, 0)
        other = lax.dynamic_slice_in_dim(widened, (1 - here.core) * pair_rows, pair_rows, 0)
        grad_inputs = jnp.stack(here.by_core(mine, here.swap(other)))

    return (
        output,
        grad_inputs,
        grad_w_down.reshape(3, 3, half, -1),
        early[0],
        early[1],
        early[2],
        early[3].reshape(3, 3, half, -1),
        early[4],
        early[5],
        *norm_grads,
    )


def solution(mesh):
    placed = (P("batch", "rows", None, None),) + (P(),) * 12 + (P("batch", "rows", None, None),)
    return jax.shard_map(
        on_device,
        mesh=mesh,
        in_specs=placed,
        out_specs=(
            P("batch", "rows", None, None),
            P("batch", "rows", None, None),
            P(None, None, None, "rows"),
            P(None, "rows"),
            P(None, "rows"),
            P(None, "rows"),
            P(None, None, None, "rows"),
            P(None, "rows"),
            P(None, "rows"),
            P(),
            P(),
            P(),
            P(),
        ),
        check_vma=False,
    )
```

```python
import functools

import jax
import jax.numpy as jnp
from jax import lax
from jax.experimental import pallas as pl
from jax.experimental.pallas import tpu as pltpu
from jax.sharding import PartitionSpec as P

EPSILON = 1e-05
FAR = 20.0
CHUNK = 64
COLS = 256
BF = jnp.bfloat16
F32 = jnp.float32


def mish(values):
    grown = jnp.exp(jnp.minimum(values, FAR))
    wide = grown * (grown + 2.0)
    return values * (wide / (wide + 2.0))


def mish_slope(values):
    grown = jnp.exp(jnp.minimum(values, FAR))
    wide = grown * (grown + 2.0)
    share = 1.0 / (wide + 2.0)
    return wide * share + 4.0 * values * (grown * (grown + 1.0) * share) * share


def after(value, *others):
    return lax.optimization_barrier((value,) + others)[0]


def tree_sum(parts):
    while len(parts) > 1:
        parts = [parts[i] + parts[i + 1] for i in range(0, len(parts), 2)]
    return parts[0]


def dot(a, b):
    return jnp.dot(a, b, preferred_element_type=F32)


def dot_back(a, b):
    return lax.dot_general(a, b, (((1,), (1,)), ((), ())), preferred_element_type=F32)


def dot_cells(a, b):
    return lax.dot_general(a, b, (((0,), (0,)), ((), ())), preferred_element_type=F32)


class Plane:
    def __init__(self):
        self.rows = lax.axis_size("rows")
        self.groups = lax.axis_size("batch")
        self.chips = self.rows // 2
        self.place = lax.axis_index("rows")
        self.core = self.place % 2
        self.chip = self.place // 2

    def swap(self, value):
        return lax.ppermute(value, "rows", [(i, i ^ 1) for i in range(self.rows)])

    def chip_hops(self, value):
        return [value] + [
            lax.ppermute(value, "rows", [(i, i ^ (2 * step)) for i in range(self.rows)])
            for step in range(1, self.chips)
        ]

    def chip_hop(self, value, step):
        return lax.ppermute(value, "rows", [(i, i ^ (2 * step)) for i in range(self.rows)])

    def plane_hops(self, value):
        return [value] + [
            lax.ppermute(value, "batch", [(i, i ^ step) for i in range(self.groups)])
            for step in range(1, self.groups)
        ]

    def by_core(self, mine, got):
        first = self.core == 0
        return jnp.where(first, mine, got), jnp.where(first, got, mine)

    def split(self, block, axis=0):
        mine = lax.dynamic_index_in_dim(block, self.core, axis, keepdims=False)
        other = lax.dynamic_index_in_dim(block, 1 - self.core, axis, keepdims=False)
        return mine, other

    def pieces(self, mine, other):
        return self.chip_hops(jnp.concatenate([mine, self.swap(other)], axis=0))

    def plane_steps(self, value):
        found = {0: value}
        step = self.groups // 2
        while step:
            found |= {far + step: self.plane_hop(v, step) for far, v in found.items()}
            step //= 2
        return [found[k] for k in range(self.groups)]

    def plane_hop(self, value, step):
        return lax.ppermute(value, "batch", [(i, i ^ step) for i in range(self.groups)])

    def everywhere(self, pay):
        return self.plane_hops(jnp.concatenate([pay, self.swap(pay)], axis=0))


class Far:
    def __init__(self, source, target, semaphore):
        self.copy = pltpu.make_async_copy(source, target, semaphore)
        self.copy.start()
        self.target, self.waits = target, True

    def ready(self):
        if self.waits:
            self.copy.wait()
            self.waits = False
        return self.target


def rows_loop(total, body, carry=None, step=CHUNK):
    def turn(index, state):
        return body(pl.ds(pl.multiple_of(index * step, step), step), state)

    return lax.fori_loop(0, total // step, turn, carry, unroll=2)


GAIN_WIDE, SHIFT_WIDE, GAIN, SHIFT = 0, 2, 4, 9


def row_of(params, first, index, half=None):
    return params[first + index : first + index + 1, 0 : (half or params.shape[1])]


def finish_moments(scal, refs, cols=slice(None)):
    scal = [scal[k : k + 1, 0 : refs[0].shape[1]] for k in range(2 + 4 * len(refs))]
    pixels = scal[1]
    center = tree_sum([r[0:1, cols] + r[2:3, cols] for r in refs]) / pixels
    terms = []
    for k, r in enumerate(refs):
        ends = []
        for side in range(2):
            count, over = scal[2 + 4 * k + 2 * side], scal[3 + 4 * k + 2 * side]
            gap = r[2 * side : 2 * side + 1, cols] * over - center
            ends.append(gap * gap * count)
        terms.append((r[1:2, cols] + r[3:4, cols]) + (ends[0] + ends[1]))
    return center, lax.rsqrt(tree_sum(terms) / pixels + EPSILON)


def finish_sums(refs, cols=slice(None)):
    return (
        tree_sum([r[0:1, cols] + r[2:3, cols] for r in refs]),
        tree_sum([r[1:2, cols] + r[3:4, cols] for r in refs]),
    )


def put_moments(values, pay, cols, scal):
    weight = scal[0:1, cols]
    total = jnp.sum(values, axis=0, keepdims=True)
    off = values - total * (1.0 / values.shape[0])
    pay[0:1, cols] = total * weight
    pay[1:2, cols] = jnp.sum(off * off, axis=0, keepdims=True) * weight


def project(left, weights, pre, pay, scal, add=None):
    weights = weights.ready() if isinstance(weights, Far) else weights
    for start in range(0, pre.shape[1], COLS):
        cols = slice(start, start + COLS)
        out = dot(left[...], weights[:, cols])
        if add is not None:
            out = out + add[:, cols]
        pre[:, cols] = out
        put_moments(out, pay, cols, scal)


def fold(values):
    return jnp.sum(values.reshape(-1, 8, values.shape[-1]), axis=0)


def push(grad_of, pre, center, rstd, gain, offset, pushed, pay):
    def body(rows, sums):
        unit = (pre[rows, :].astype(F32) - center) * rstd
        out = grad_of(rows) * mish_slope(unit * gain + offset)
        pushed[rows, :] = out
        return sums[0] + fold(out), sums[1] + fold(out * unit)

    zero = jnp.zeros((8, pre.shape[1]), F32)
    first, second = rows_loop(pre.shape[0], body, (zero, zero), 32)
    pay[0:1, :] = jnp.sum(first, axis=0, keepdims=True)
    pay[1:2, :] = jnp.sum(second, axis=0, keepdims=True)


def settle(scal, refs, pushed, pre, coef, gain, out, sums):
    first, second = finish_sums(refs)
    sums[0:1, :] = first
    sums[1:2, :] = second
    width = pre.shape[1]
    over = 1.0 / scal[1:2, 0:width]
    center, rstd = coef[0:1, :], coef[1:2, :]
    scale = gain * rstd * scal[0:1, 0:width]
    level, tilt = first * over, second * over * rstd

    def body(rows, _):
        x = pre[rows, :].astype(F32) - center
        out[rows, :] = (scale * (pushed[rows, :] - level - x * tilt)).astype(BF)

    rows_loop(pre.shape[0], body)


def own_core():
    return lax.rem(lax.axis_index("rows"), 2)


def own_chip():
    return lax.div(lax.axis_index("rows"), 2)


def image_row(step, side):
    return 2 * (own_chip() ^ step) + (own_core() ^ side)


def put_scalars(cells, counts, scal):
    groups = counts.shape[0]
    core, batch = own_core(), lax.axis_index("batch")
    total = counts[0]
    for k in range(1, groups):
        total = total + counts[k]

    def put(k, value):
        scal[k : k + 1, :] = jnp.full((1, scal.shape[1]), value, F32)

    put(0, (core < counts[batch]).astype(F32))
    put(1, total.astype(F32) * cells)
    for step in range(groups):
        own = counts[batch ^ step]
        for side, slot in enumerate((core, 1 - core)):
            valid = (slot < own).astype(F32)
            put(2 + 4 * step + 2 * side, valid * cells)
            put(3 + 4 * step + 2 * side, valid * (1.0 / cells) + (1.0 - valid))


def shifted_row(both):
    half = both.shape[1] // 2
    odd = both[:, half:].astype(F32)
    first = lax.broadcasted_iota(jnp.int32, odd.shape, 0) == 0
    before = jnp.where(first, 0.0, pltpu.roll(odd, 1, 0)).astype(BF)
    return jnp.concatenate([before, both], axis=1)


def row_of_slots(values):
    return jnp.concatenate([shifted_row(values[slot]) for slot in range(values.shape[0])], axis=0)


def streamed(w, rows, held, semaphores):
    count, wide = held.shape[0], held.shape[-1]
    copies = [
        pltpu.make_async_copy(w.at[rows, :, n * wide : (n + 1) * wide], held.at[n], semaphores.at[n])
        for n in range(count)
    ]
    for copy in copies[:2]:
        copy.start()
    for n in range(count):
        copies[n].wait()
        if n + 2 < count:
            copies[n + 2].start()
        yield slice(n * wide, (n + 1) * wide), held.at[n]


def own_kernel(x, w, part, held, semaphores):
    blocks = streamed(w, slice(1, 3), held, semaphores)
    cols, block = next(blocks)
    lefts = [row_of_slots(x[:, row]) for row in range(2)]
    while cols is not None:
        part[:, cols] = dot(lefts[0], block[0]) + dot(lefts[1], block[1])
        cols, block = next(blocks, (None, None))


def above_kernel(above, part, w, rows, held, semaphores):
    cells = above.shape[1]
    blocks = streamed(w, slice(0, 1), held, semaphores)
    cols, block = next(blocks)
    left = row_of_slots(above[...])
    while cols is not None:
        out = part[:, cols] + dot(left, block[0])
        for slot in range(above.shape[0]):
            rows[slot, :, cols] = out[slot * cells : (slot + 1) * cells].astype(BF)
        cols, block = next(blocks, (None, None))


def whole_kernel(counts, *rest):
    parts, (down_pre, keep, pay, scal, semaphore) = rest[:-5], rest[-5:]
    put_scalars(down_pre.shape[0], counts, scal)
    total = jnp.zeros((8, down_pre.shape[1]), F32)
    for k, part in enumerate(parts):
        width = part.shape[0] // 2
        for side in range(2):
            start = image_row(k, side) * width

            def body(index, total, part=part, side=side, start=start, width=width):
                src = pl.ds(pl.multiple_of(side * width + index * CHUNK, CHUNK), CHUNK)
                dst = pl.ds(pl.multiple_of(start + index * CHUNK, CHUNK), CHUNK)
                down_pre[dst, :] = part[src, :]
                return total + fold(part[src, :].astype(F32))

            total = lax.fori_loop(0, width // CHUNK, body, total)
    copy = pltpu.make_async_copy(down_pre, keep, semaphore)
    copy.start()
    total = jnp.sum(total, axis=0, keepdims=True)
    mean = total * (1.0 / down_pre.shape[0])

    def spread(rows, squares):
        off = down_pre[rows, :].astype(F32) - mean
        return squares + fold(off * off)

    squares = rows_loop(down_pre.shape[0], spread, jnp.zeros((8, down_pre.shape[1]), F32))
    pay[0:1, :] = total * scal[0:1, :]
    pay[1:2, :] = jnp.sum(squares, axis=0, keepdims=True) * scal[0:1, :]
    copy.wait()


def main_kernel(groups, scal, *rest):
    refs = rest[:groups]
    down_pre, params, w_main, sectioned, main_pre, main_keep, pay, coef, semaphore = rest[groups:]
    center, rstd = finish_moments(scal, refs)
    coef[0:1, :] = center
    coef[1:2, :] = rstd
    scale, offset = rstd * row_of(params, GAIN_WIDE, 0), row_of(params, SHIFT_WIDE, 0)

    def body(rows, _):
        value = (down_pre[rows, :].astype(F32) - center) * scale + offset
        sectioned[rows, :] = mish(value).astype(BF)

    rows_loop(down_pre.shape[0], body)
    project(sectioned, w_main, main_pre, pay, scal)
    copy = pltpu.make_async_copy(main_pre, main_keep, semaphore)
    copy.start()
    copy.wait()


def short_kernel(scal, sectioned, w_short, short_pre, pay):
    project(sectioned, w_short, short_pre, pay, scal)


def inner_kernel(groups, scal, *rest):
    refs = rest[:groups]
    pre, params, w_inner, mainline, inner_pre, pay, coef = rest[groups:]
    half = pre.shape[1]
    center, rstd = finish_moments(scal, refs)
    coef[0:1, :] = center
    coef[1:2, :] = rstd
    scale, offset = rstd * row_of(params, GAIN, 1, half), row_of(params, SHIFT, 1, half)

    def body(rows, _):
        mainline[rows, :] = mish((pre[rows, :] - center) * scale + offset).astype(BF)

    rows_loop(pre.shape[0], body)
    project(mainline, w_inner, inner_pre, pay, scal)


def three_shifts(values, rim, start, forward):
    width, half = values.shape
    place = lax.broadcasted_iota(jnp.int32, values.shape, 0)
    before = jnp.where(place == 0, 0.0, pltpu.roll(values, 1, 0)).astype(BF)
    after = jnp.where(place == width - 1, 0.0, pltpu.roll(values, width - 1, 0)).astype(BF)
    sides = (before, after) if forward else (after, before)
    rows = pl.ds(start, width)
    rim[rows, 0:half] = sides[0]
    rim[rows, half : 2 * half] = values.astype(BF)
    rim[rows, 2 * half : 3 * half] = sides[1]


def spatial_kernel(groups, width, scal, *rest):
    refs = rest[:groups]
    pre, params, w_spatial, rim, spatial_pre, pay, coef = rest[groups:]
    cells, half = pre.shape
    center, rstd = finish_moments(scal, refs)
    coef[0:1, :] = center
    coef[1:2, :] = rstd
    scale, offset = rstd * row_of(params, GAIN, 2, half), row_of(params, SHIFT, 2, half)
    blank = jnp.zeros((width, 3 * half), BF)
    rim[0:width, :] = blank
    rim[width + cells :, :] = blank

    def body(index, _):
        start = pl.multiple_of(index * width, width)
        act = mish((pre[pl.ds(start, width), :] - center) * scale + offset)
        three_shifts(act, rim, pl.multiple_of(start + width, width), True)

    lax.fori_loop(0, cells // width, body, None)
    w_spatial = w_spatial.ready()
    for begin in range(0, half, COLS):
        cols = slice(begin, begin + COLS)
        out = sum(
            dot(
                rim[i * width : i * width + cells, :],
                w_spatial[i * 3 * half : (i + 1) * 3 * half, cols],
            )
            for i in range(3)
        )
        spatial_pre[:, cols] = out
        put_moments(out, pay, cols, scal)


def trans_kernel(groups, scal, *rest):
    refs = rest[:groups]
    pre, mainline, params, w_trans, merged, trans_pre, pay, coef = rest[groups:]
    half = pre.shape[1]
    center, rstd = finish_moments(scal, refs)
    coef[0:1, :] = center
    coef[1:2, :] = rstd
    scale, offset = rstd * row_of(params, GAIN, 3, half), row_of(params, SHIFT, 3, half)

    def body(rows, _):
        act = mish((pre[rows, :] - center) * scale + offset)
        merged[rows, :] = (mainline[rows, :].astype(F32) + act).astype(BF)

    rows_loop(pre.shape[0], body)
    project(merged, w_trans, trans_pre, pay, scal)


def shortcut_kernel(groups, scal, *rest):
    refs = rest[:groups]
    pre, params, w_unite, shortcut, part, coef = rest[groups:]
    half = pre.shape[1]
    center, rstd = finish_moments(scal, refs)
    coef[0:1, :] = center
    coef[1:2, :] = rstd
    scale, offset = rstd * row_of(params, GAIN, 0, half), row_of(params, SHIFT, 0, half)

    def body(rows, _):
        shortcut[rows, :] = mish((pre[rows, :] - center) * scale + offset).astype(BF)

    rows_loop(pre.shape[0], body)
    w_unite = w_unite.ready()
    for start in range(0, part.shape[1], COLS):
        cols = slice(start, start + COLS)
        part[:, cols] = dot(shortcut[...], w_unite[:, cols])


def unite_kernel(groups, scal, *rest):
    refs = rest[:groups]
    pre, part, params, w_unite, transition, unite_pre, pay, coef = rest[groups:]
    half = pre.shape[1]
    center, rstd = finish_moments(scal, refs)
    coef[0:1, :] = center
    coef[1:2, :] = rstd
    scale, offset = rstd * row_of(params, GAIN, 4, half), row_of(params, SHIFT, 4, half)

    def body(rows, _):
        transition[rows, :] = mish((pre[rows, :] - center) * scale + offset).astype(BF)

    rows_loop(pre.shape[0], body)
    project(transition, w_unite.ready(), unite_pre, pay, scal, part)


def turn_kernel(groups, pieces, scal, *rest):
    refs = rest[:groups]
    pre, params = rest[groups : groups + 2]
    parts = rest[groups + 2 : groups + 2 + pieces]
    pushed, *outputs, pay, coef = rest[groups + 2 + pieces :]
    center, rstd = finish_moments(scal, refs)
    coef[0:1, :] = center
    coef[1:2, :] = rstd
    gain, offset, weight = row_of(params, GAIN_WIDE, 1), row_of(params, SHIFT_WIDE, 1), scal[0:1, 0 : pre.shape[1]]
    sums = (jnp.zeros((8, pre.shape[1]), F32),) * 2
    for k, part in enumerate(parts):
        part = part.ready()
        width = part.shape[0] // 2
        for side in range(2):
            start = image_row(k, side) * width

            def body(index, sums, k=k, part=part, side=side, start=start, width=width):
                src = pl.ds(pl.multiple_of(side * width + index * (CHUNK // 2), CHUNK // 2), CHUNK // 2)
                dst = pl.ds(pl.multiple_of(start + index * (CHUNK // 2), CHUNK // 2), CHUNK // 2)
                unit = (pre[dst, :] - center) * rstd
                value = unit * gain + offset
                grown = jnp.exp(jnp.minimum(value, FAR))
                wide = grown * (grown + 2.0)
                share = 1.0 / (wide + 2.0)
                level = wide * share
                if k == 0:
                    rows = pl.ds(pl.multiple_of(index * (CHUNK // 2), CHUNK // 2), CHUNK // 2)
                    outputs[side][rows, :] = (value * level * weight).astype(BF)
                slope = level + 4.0 * value * (grown * (grown + 1.0) * share) * share
                out = part[src, :].astype(F32) * weight * slope
                pushed[dst, :] = out
                return sums[0] + fold(out), sums[1] + fold(out * unit)

            sums = lax.fori_loop(0, width // (CHUNK // 2), body, sums)
    pay[0:1, :] = jnp.sum(sums[0], axis=0, keepdims=True)
    pay[1:2, :] = jnp.sum(sums[1], axis=0, keepdims=True)


def back_trans_kernel(groups, scal, *rest):
    refs = rest[:groups]
    (
        unite_pushed, unite_pre, unite_coef, params, trans_pre, trans_coef, w_unite,
        grad_unite, sums, pushed, pay, scratch,
    ) = rest[groups:]
    half = trans_pre.shape[1]
    settle(scal, refs, unite_pushed, unite_pre, unite_coef, row_of(params, GAIN_WIDE, 1), grad_unite, sums)
    w_unite = w_unite.ready()
    for start in range(0, half, COLS):
        scratch[:, start : start + COLS] = dot_back(
            grad_unite[...], w_unite[start : start + COLS, :]
        )
    push(
        lambda rows: scratch[rows, :],
        trans_pre, trans_coef[0:1, :], trans_coef[1:2, :], row_of(params, GAIN, 4, half), row_of(params, SHIFT, 4, half),
        pushed, pay,
    )


def back_short_kernel(grad_unite, pre, coef, params, w_unite, pushed, pay, scratch):
    half = pre.shape[1]
    w_unite = w_unite.ready()
    for start in range(0, half, COLS):
        scratch[:, start : start + COLS] = dot_back(
            grad_unite[...], w_unite[start : start + COLS, :]
        )
    push(
        lambda rows: scratch[rows, :],
        pre, coef[0:1, :], coef[1:2, :], row_of(params, GAIN, 0, half), row_of(params, SHIFT, 0, half), pushed, pay,
    )


def back_spatial_kernel(groups, scal, *rest):
    refs = rest[:groups]
    (
        trans_pushed, trans_pre, trans_coef, spatial_pre, spatial_coef, params, w_trans,
        grad_trans, sums, grad_merged, pushed, pay,
    ) = rest[groups:]
    half = trans_pre.shape[1]
    settle(scal, refs, trans_pushed, trans_pre, trans_coef, row_of(params, GAIN, 4, half), grad_trans, sums)
    w_trans = w_trans.ready()
    for start in range(0, half, COLS):
        grad_merged[:, start : start + COLS] = dot_back(
            grad_trans[...], w_trans[start : start + COLS, :]
        )
    push(
        lambda rows: grad_merged[rows, :],
        spatial_pre, spatial_coef[0:1, :], spatial_coef[1:2, :], row_of(params, GAIN, 3, half), row_of(params, SHIFT, 3, half),
        pushed, pay,
    )


def back_inner_kernel(groups, width, scal, *rest):
    refs = rest[:groups]
    (
        spatial_pushed, spatial_pre, spatial_coef, inner_pre, inner_coef, params, w_spatial,
        grad_spatial, sums, pushed, pay, rim, scratch,
    ) = rest[groups:]
    cells, half = spatial_pre.shape
    settle(scal, refs, spatial_pushed, spatial_pre, spatial_coef, row_of(params, GAIN, 3, half), grad_spatial, sums)
    blank = jnp.zeros((width, 3 * half), BF)
    rim[0:width, :] = blank
    rim[width + cells :, :] = blank

    def body(index, _):
        start = pl.multiple_of(index * width, width)
        values = grad_spatial[pl.ds(start, width), :].astype(F32)
        three_shifts(values, rim, pl.multiple_of(start + width, width), False)

    lax.fori_loop(0, cells // width, body, None)
    w_spatial = w_spatial.ready()
    for start in range(0, half, COLS):
        scratch[:, start : start + COLS] = sum(
            dot_back(
                rim[(2 - i) * width : (2 - i) * width + cells, j * half : (j + 1) * half],
                w_spatial[(3 * i + j) * half + start : (3 * i + j) * half + start + COLS, :],
            )
            for i in range(3)
            for j in range(3)
        )
    push(
        lambda rows: scratch[rows, :],
        inner_pre, inner_coef[0:1, :], inner_coef[1:2, :], row_of(params, GAIN, 2, half), row_of(params, SHIFT, 2, half),
        pushed, pay,
    )


def back_main_kernel(groups, scal, *rest):
    refs = rest[:groups]
    (
        inner_pushed, inner_pre, inner_coef, grad_merged, main_pre, main_coef, params, w_inner,
        grad_inner, sums, pushed, pay, scratch,
    ) = rest[groups:]
    half = inner_pre.shape[1]
    settle(scal, refs, inner_pushed, inner_pre, inner_coef, row_of(params, GAIN, 2, half), grad_inner, sums)
    w_inner = w_inner.ready()
    for start in range(0, half, COLS):
        cols = slice(start, start + COLS)
        scratch[:, cols] = grad_merged[:, cols] + dot_back(grad_inner[...], w_inner[cols, :])
    push(
        lambda rows: scratch[rows, :],
        main_pre, main_coef[0:1, :], main_coef[1:2, :], row_of(params, GAIN, 1, half), row_of(params, SHIFT, 1, half),
        pushed, pay,
    )


def settle_short_kernel(groups, scal, *rest):
    refs = rest[:groups]
    pushed, pre, coef, params, grad_short, sums = rest[groups:]
    half = pre.shape[1]
    settle(scal, refs, pushed, pre, coef, row_of(params, GAIN, 0, half), grad_short, sums)


def back_down_kernel(groups, scal, *rest):
    refs = rest[:groups]
    (
        main_pushed, main_coef, down_coef, params, main_pre, w_main, grad_short, w_short, down_pre,
        grad_main, sums, pushed, pay, scratch,
    ) = rest[groups:]
    main_pre = main_pre.ready()
    half = main_pre.shape[1]
    settle(scal, refs, main_pushed, main_pre, main_coef, row_of(params, GAIN, 1, half), grad_main, sums)
    w_main, grad_short, w_short = w_main.ready(), grad_short.ready(), w_short.ready()
    for start in range(0, pushed.shape[1], COLS):
        cols = slice(start, start + COLS)
        scratch[:, cols] = dot_back(grad_short[...], w_short[cols, :]) + dot_back(
            grad_main[...], w_main[cols, :]
        )
    push(
        lambda rows: scratch[rows, :],
        down_pre.ready(), down_coef[0:1, :], down_coef[1:2, :],
        row_of(params, GAIN_WIDE, 0), row_of(params, SHIFT_WIDE, 0),
        pushed, pay,
    )


def settle_down_kernel(groups, scal, *rest):
    refs = rest[:groups]
    pushed, pre, coef, params, grad_down, sums = rest[groups:]
    settle(scal, refs, pushed, pre, coef, row_of(params, GAIN_WIDE, 0), grad_down, sums)
    cells = pre.shape[0]
    grad_down[cells:, :] = jnp.zeros((grad_down.shape[0] - cells, pre.shape[1]), BF)


def cut_down_kernel(groups, scal, *rest):
    refs = rest[:groups]
    pushed, pre, coef, params, cut = rest[groups:]
    width = cut.shape[1]
    cols = pl.ds(pl.multiple_of(own_chip() * width, width), width)
    first, second = finish_sums(refs, cols)
    over = 1.0 / scal[1:2, 0:width]
    center, rstd = coef[0:1, cols], coef[1:2, cols]
    scale = params[GAIN_WIDE : GAIN_WIDE + 1, cols] * rstd * scal[0:1, 0:width]
    level, tilt = first * over, second * over * rstd

    def body(rows, _):
        x = pre[rows, cols].astype(F32) - center
        cut[rows, :] = (scale * (pushed[rows, cols] - level - x * tilt)).astype(BF)

    rows_loop(pre.shape[0], body)


def by_place(first, second):
    low = own_core() == 0
    return jnp.where(low, first, second), jnp.where(low, second, first)


def share_unite_kernel(shortcut, transition, grad, mine, other):
    width = 2 * mine.shape[1]
    cut = grad[:, pl.ds(pl.multiple_of(own_chip() * width, width), width)]
    half = shortcut.shape[1]
    for k, values in enumerate((shortcut, transition)):
        out = dot_cells(values[...], cut)
        near, far = by_place(out[:, : width // 2], out[:, width // 2 :])
        mine[k * half : (k + 1) * half, :] = near.astype(BF)
        other[k * half : (k + 1) * half, :] = far.astype(BF)


def put_halves(cut, values, start, mine, other):
    out = dot_cells(cut, values)
    rows, cols = mine.shape[0], slice(start, start + out.shape[1])
    near, far = by_place(out[:rows], out[rows:])
    mine[:, cols] = near.astype(BF)
    other[:, cols] = far.astype(BF)


def chip_columns(mine):
    width = 2 * mine.shape[0]
    return pl.ds(pl.multiple_of(own_chip() * width, width), width)


def share_pack_kernel(*rest):
    pairs, (mine, other) = rest[:-2], rest[-2:]
    cols = chip_columns(mine)
    start = 0
    for values, grad in zip(pairs[::2], pairs[1::2]):
        put_halves(grad[:, cols], values[...], start, mine, other)
        start += values.shape[1]


def share_spatial_kernel(cells, rim, grad, mine, other):
    cut = grad[:, chip_columns(mine)]
    line, side = (rim.shape[0] - cells) // 2, rim.shape[1]
    for row in range(3):
        put_halves(cut, rim[row * line : row * line + cells, :], row * side, mine, other)


def share_main_kernel(grad, grad_inner, sectioned, mainline, mine, other):
    cols = chip_columns(mine)
    sectioned, mainline = sectioned.ready(), mainline.ready()
    put_halves(grad[:, cols], sectioned[...], 0, mine, other)
    put_halves(grad_inner[:, cols], mainline[...], sectioned.shape[1], mine, other)


def finish_kernel(planes, unite, pack, taps, *rest):
    mains, (mine, got, near, far) = rest[:planes], rest[planes : planes + 4]
    rest = rest[planes + 4 :]
    w_unite, w_short, w_trans, w_inner, w_spatial, w_main, output, grad_inputs = rest[:8]
    *held, semaphores = rest[8:]
    sums = [Far(a, b, semaphores.at[4 + k]) for k, (a, b) in enumerate(zip((unite, pack, taps), held))]
    core = own_core()
    copies = [
        pltpu.make_async_copy(mine, output.at[core, 0], semaphores.at[0]),
        pltpu.make_async_copy(got, output.at[1 - core, 0], semaphores.at[1]),
        pltpu.make_async_copy(near.at[0], grad_inputs.at[core], semaphores.at[2]),
        pltpu.make_async_copy(far.at[1], grad_inputs.at[1 - core], semaphores.at[3]),
    ]
    for copy in copies:
        copy.start()
    unite, pack, taps = (one.ready() for one in sums)
    w_unite[...] = unite[...].astype(F32)
    for outs, values in (
        ((w_short, w_trans), pack[...].astype(F32)),
        ((w_main, w_inner), tree_sum([main[...].astype(F32) for main in mains])),
    ):
        start = 0
        for out in outs:
            out[...] = values[:, start : start + out.shape[1]]
            start += out.shape[1]
    half = w_trans.shape[1]
    for tap in range(w_spatial.shape[0]):
        w_spatial[tap] = taps[:, tap * half : (tap + 1) * half].astype(F32)
    for copy in copies:
        copy.wait()


def norm_sums_kernel(wide_count, *refs):
    sums, outs = refs[:-4], refs[-4:]
    for k, pair in enumerate(sums):
        index = k if k < wide_count else k - wide_count
        for row, out in ((1, outs[0 if k < wide_count else 1]), (0, outs[2 if k < wide_count else 3])):
            out[index : index + 1, :] = pair[row : row + 1, :]


def share_down_kernel(steps, chips, width, last_call, *rest):
    grads = rest[: len(steps)]
    earlier = rest[len(steps) : len(steps) + 2 * last_call]
    rest = rest[len(steps) + 2 * last_call :]
    source, outs, rest = rest[0], rest[1:3], rest[3:]
    if last_call:
        odd_acc, even_acc = rest[:2]
        rest = rest[2:]
    else:
        odd_acc, even_acc = outs
    padded, sides, held, semaphores = rest
    cells, columns = grads[0].shape
    half = source.shape[-1] // 2
    planes = source.shape[0] // (2 * chips)
    copies = []
    for k, step in enumerate(steps):
        plane = lax.axis_index("batch") ^ step
        copies.append(
            [
                pltpu.make_async_copy(
                    source.at[row * planes + plane, own_core()], held.at[k, row], semaphores.at[k, row]
                )
                for row in range(2 * chips)
            ]
        )
        for copy in copies[-1]:
            copy.start()
    padded[cells:, :] = jnp.zeros((padded.shape[0] - cells, columns), BF)
    last = lax.broadcasted_iota(jnp.int32, (width, columns), 0) == width - 1

    def ahead(values):
        return jnp.where(last, 0.0, pltpu.roll(values.astype(F32), width - 1, 0)).astype(BF)

    for k in range(len(steps)):
        padded[0:cells, :] = grads[k][...]
        for block in range(2 * chips):
            rows = slice(block * width, (block + 1) * width)
            here = padded[rows, :]
            upper = padded[(block + 1) * width : (block + 2) * width, :]
            sides[rows, 0:columns] = upper
            sides[rows, columns : 2 * columns] = here
            sides[rows, 2 * columns : 3 * columns] = ahead(here)
            sides[rows, 3 * columns : 4 * columns] = ahead(upper)
        for copy in copies[k]:
            copy.wait()

        def add(which, side, start, values, k=k):
            rows, cols = slice(side * half, (side + 1) * half), slice(start, start + columns)
            acc = (even_acc, odd_acc)[which]
            if k > 0:
                values = values + acc[rows, cols]
            elif last_call:
                values = values + earlier[1 - which][rows, cols]
            acc[rows, cols] = values

        for which in range(2):
            for side in range(2):
                left = held[k, :, which, :, side * half : (side + 1) * half].reshape(cells, half)
                for block in range(4):
                    if (which == 0 and block in (0, 3)) or (side == 0 and block in (2, 3)):
                        continue
                    start = block * columns
                    add(which, side, start, dot_cells(left, sides[:, start : start + columns]))
    if not last_call:
        return
    mine, other = outs
    places = (
        (odd_acc, 1, 3), (odd_acc, 0, 0), (odd_acc, 1, 0),
        (even_acc, 1, 2), (even_acc, 0, 1), (even_acc, 1, 1),
        (odd_acc, 1, 2), (odd_acc, 0, 1), (odd_acc, 1, 1),
    )
    for tap, (acc, side, block) in enumerate(places):
        values = acc[side * half : (side + 1) * half, block * columns : (block + 1) * columns]
        near, far = by_place(values[:, : columns // 2], values[:, columns // 2 :])
        mine[tap * half : (tap + 1) * half, :] = near.astype(BF)
        other[tap * half : (tap + 1) * half, :] = far.astype(BF)


def back_input_kernel(width, grad, w, out, near, far):
    cells = 2 * width
    full = grad.shape[1]

    @pl.when(pl.program_id(0) == 0)
    def _():
        last = lax.broadcasted_iota(jnp.int32, (width, full), 0) == width - 1
        for block in range(3):
            start = pl.multiple_of(own_chip() * cells + block * width, width)
            values = grad[pl.ds(start, width), :]
            rows = slice(block * width, (block + 1) * width)
            near[rows, :] = values
            far[rows, :] = jnp.where(
                last, 0.0, pltpu.roll(values.astype(F32), width - 1, 0)
            ).astype(BF)

    low, high = slice(0, cells), slice(width, width + cells)

    def term(values, rows, i, j):
        return dot_back(values[rows, :], w[3 * i + j])

    def put(parity, column, values):
        for row in range(2):
            out[row ^ own_core(), parity, pl.ds(column, width, stride=2), :] = values[
                row * width : (row + 1) * width
            ]

    put(0, 0, term(near, low, 1, 1))
    put(0, 1, term(near, low, 1, 2) + term(far, low, 1, 0))
    put(1, 0, term(near, high, 0, 1) + term(near, low, 2, 1))
    put(
        1,
        1,
        term(near, high, 0, 2) + term(far, high, 0, 0) + term(near, low, 2, 2) + term(far, low, 2, 0),
    )


SMEM = pl.BlockSpec(memory_space=pltpu.SMEM)
VMEM = pl.BlockSpec(memory_space=pltpu.VMEM)
ANY = pl.BlockSpec(memory_space=pl.ANY)


def shape(dims, dtype=F32):
    return jax.ShapeDtypeStruct(dims, dtype)


def nbytes(dims, dtype):
    count = 1
    for d in dims:
        count *= d
    return count * jnp.dtype(dtype).itemsize


def in_vmem(value):
    return pltpu.with_memory_space_constraint(value, pltpu.VMEM)


def in_hbm(value):
    return pltpu.with_memory_space_constraint(value, pltpu.HBM)


LIGHT = pl.CostEstimate(flops=0, bytes_accessed=0, transcendentals=0)


def call(kernel, name, scalars, near, outs, flops, scratch=(), far=(), pin=False, spill=(), light=False, out=(), late=False):
    cuts = [one[1] if isinstance(one, tuple) else None for one in far]
    far = [one[0] if isinstance(one, tuple) else one for one in far]
    held_far = [
        shape((cut.stop - cut.start,) + a.shape[1:], a.dtype) if cut else a for a, cut in zip(far, cuts)
    ]
    moved = sum(nbytes(a.shape, a.dtype) for a in (*near, *far, *outs))
    scratch = [s if hasattr(s, "memory_space") or not hasattr(s, "shape") else pltpu.VMEM(s.shape, s.dtype) for s in scratch]
    held = moved + sum(nbytes(s.shape, s.dtype) for s in scratch if hasattr(s, "shape"))
    if pin:
        held -= moved - sum(nbytes(a.shape, a.dtype) for a in far)
        held += sum(nbytes(outs[k].shape, outs[k].dtype) for k in spill)
        near, far = [in_vmem(a) for a in near], [in_hbm(a) for a in far]
        outs = [
            o if k in spill else (pltpu.HBM if k in out else pltpu.VMEM)(o.shape, o.dtype)
            for k, o in enumerate(outs)
        ]
    before, after_far, last = len(scalars) + len(near), len(far), len(outs) + len(scratch)

    def body(*refs):
        sources, rest = refs[before : before + after_far], refs[before + after_far :]
        targets = rest[last : last + after_far]
        fars = [
            Far(a.at[cut] if cut else a, b, rest[-1].at[k])
            for k, (a, b, cut) in enumerate(zip(sources, targets, cuts))
        ]
        kernel(*refs[:before], *fars, *rest[:last])
        for one in fars:
            one.ready()

    return pl.pallas_call(
        body if far else kernel,
        name=name,
        out_shape=tuple(outs),
        in_specs=[SMEM] * len(scalars) + [VMEM] * len(near) + [ANY] * len(far),
        out_specs=tuple(ANY if k in out and not late else VMEM for k in range(len(outs))),
        scratch_shapes=scratch
        + [pltpu.VMEM(a.shape, a.dtype) for a in held_far]
        + ([pltpu.SemaphoreType.DMA((len(far),))] if far else []),
        compiler_params=pltpu.CompilerParams(vmem_limit_bytes=held + (8 << 20)),
        cost_estimate=LIGHT if light else pl.CostEstimate(flops=flops, bytes_accessed=moved, transcendentals=0),
    )(*scalars, *near, *far)


def first_conv(view, above, w_down, pin):
    slots, _, cells, both = view.shape
    half = both // 2
    full = w_down.shape[-1]
    taps = w_down.reshape(3, 3 * half, full)
    if pin:
        view, above, taps = in_vmem(view), in_vmem(above), in_hbm(taps)
    wide = 256
    count = full // wide

    def run(kernel, name, rows, values, out):
        return pl.pallas_call(
            kernel,
            name=name,
            out_shape=(pltpu.VMEM if pin else shape)(out.shape, out.dtype),
            in_specs=[VMEM] * len(values) + [ANY],
            out_specs=VMEM,
            scratch_shapes=[
                pltpu.VMEM((count, rows, 3 * half, wide), BF), pltpu.SemaphoreType.DMA((count,))
            ],
            compiler_params=pltpu.CompilerParams(vmem_limit_bytes=24 << 20),
            cost_estimate=pl.CostEstimate(
                flops=6 * rows * slots * cells * half * full,
                bytes_accessed=6 * rows * half * full,
                transcendentals=0,
            ),
        )(*values, taps)

    part = run(own_kernel, "own", 2, [view], shape((slots * cells, full)))
    part = in_vmem(part) if pin else part
    return run(above_kernel, "above", 1, [above, part], shape((slots, cells, full), BF))


def flipped(kernel):
    return jnp.swapaxes(jnp.flip(kernel, (0, 1)), 2, 3)


def on_device(
    inputs,
    image_counts,
    w_down,
    w_short,
    w_main,
    w_inner,
    w_spatial,
    w_trans,
    w_unite,
    gains_wide,
    gains_narrow,
    shifts_wide,
    shifts_narrow,
    grad_output,
):
    half = w_short.shape[1]
    full = 2 * half
    slots, height_dev, width, _ = grad_output.shape
    here = Plane()
    wide = here.chips == 4 and half % (128 * here.chips) == 0
    stage = functools.partial(call, pin=wide)
    groups, chips = here.groups, here.chips
    height = here.rows * height_dev
    cells = height * width
    batch = lax.axis_index("batch")
    view = inputs.reshape(slots, 2, width, 2 * half)
    below = [(i, i + 1) for i in range(here.rows - 1)]
    above = lax.ppermute(view[:, 1], "rows", below)
    params = jnp.concatenate(
        [gains_wide, shifts_wide]
        + [jnp.pad(p, ((0, 0), (0, half))) for p in (gains_narrow, shifts_narrow)]
    )
    down_rows = first_conv(view, above, w_down, wide)
    down_pieces = here.pieces(*here.split(down_rows))
    grad_mine, grad_other = here.split(grad_output.reshape(slots, width, full))
    down_pieces[1], params, grad_mine, grad_other = lax.optimization_barrier(
        (down_pieces[1], params, grad_mine, grad_other)
    )
    down_pre, down_keep, down_pay, scal = stage(
        whole_kernel,
        "whole",
        [image_counts],
        down_pieces,
        [
            shape((cells, full), BF), shape((cells, full), BF), shape((2, full)),
            shape((2 + 4 * groups, full)),
        ],
        10 * cells * full,
        out=(1,),
        scratch=[pltpu.SemaphoreType.DMA],
    )
    if wide:
        flat = after(view, down_pay).reshape(slots * 2 * width, 2 * half)
        source = lax.all_gather(flat, ("rows", "batch")).reshape(-1, *view.shape)
        grad_piece = jnp.concatenate([grad_mine, here.swap(after(grad_other, down_pay))], axis=0)
        grad_pieces = [grad_piece, here.chip_hop(grad_piece, 1), here.chip_hop(grad_piece, 2)]
        grad_pieces.append(here.chip_hop(grad_pieces[1], 2))
    else:
        grad_pieces = here.pieces(grad_mine, grad_other)
    sectioned, main_pre, main_keep, main_pay, down_coef = stage(
        functools.partial(main_kernel, groups),
        "main",
        [],
        [scal, *here.everywhere(down_pay), down_pre, params],
        [
            shape((cells, full), BF), shape((cells, half)), shape((cells, half)),
            shape((2, half)), shape((2, full)),
        ],
        2 * cells * full * half,
        far=[w_main],
        out=(2,),
        scratch=[pltpu.SemaphoreType.DMA],
    )

    if wide:
        main_pay = after(main_pay, *grad_pieces[:3])
    main_all = here.everywhere(main_pay)
    short_pre, short_pay = stage(
        short_kernel,
        "short",
        [],
        [scal, sectioned],
        [shape((cells, half)), shape((2, half))],
        2 * cells * full * half,
        far=[w_short],
    )
    mainline, inner_pre, inner_pay, main_coef = stage(
        functools.partial(inner_kernel, groups),
        "inner",
        [],
        [scal, *main_all, main_pre, params],
        [shape((cells, half), BF), shape((cells, half)), shape((2, half)), shape((2, half))],
        2 * cells * half * half,
        far=[w_inner],
    )
    inner_all = here.everywhere(inner_pay)
    rim, spatial_pre, spatial_pay, inner_coef = stage(
        functools.partial(spatial_kernel, groups, width),
        "spatial",
        [],
        [scal, *inner_all, inner_pre, params],
        [
            shape((cells + 2 * width, 3 * half), BF), shape((cells, half)),
            shape((2, half)), shape((2, half)),
        ],
        18 * cells * half * half,
        far=[w_spatial.reshape(9 * half, half)],
    )
    if wide:
        spatial_pay = after(spatial_pay, grad_pieces[3])
    both_all = here.everywhere(jnp.concatenate([spatial_pay, short_pay], axis=1))
    spatial_all = [b[:, :half] for b in both_all]
    short_all = [b[:, half:] for b in both_all]
    merged, trans_pre, trans_pay, spatial_coef = stage(
        functools.partial(trans_kernel, groups),
        "trans",
        [],
        [scal, *spatial_all, spatial_pre, mainline, params],
        [shape((cells, half), BF), shape((cells, half)), shape((2, half)), shape((2, half))],
        2 * cells * half * half,
        far=[w_trans],
    )
    trans_all = here.everywhere(trans_pay)
    shortcut, unite_part, short_coef = stage(
        functools.partial(shortcut_kernel, groups),
        "shortcut",
        [],
        [scal, *short_all, short_pre, params],
        [shape((cells, half), BF), shape((cells, full)), shape((2, half))],
        2 * cells * half * full,
        far=[(w_unite, slice(0, half))],
    )
    transition, unite_pre, unite_pay, trans_coef = stage(
        functools.partial(unite_kernel, groups),
        "unite",
        [],
        [scal, *trans_all, trans_pre, unite_part, params],
        [shape((cells, half), BF), shape((cells, full)), shape((2, full)), shape((2, half))],
        2 * cells * half * full,
        far=[(w_unite, slice(half, full))],
    )
    unite_all = here.everywhere(unite_pay)
    unite_pushed, mine, other, unite_pay, unite_coef = stage(
        functools.partial(turn_kernel, groups, chips),
        "turn",
        [],
        [scal, *unite_all, unite_pre, params],
        [
            shape((cells, full)), shape((width, full), BF), shape((width, full), BF),
            shape((2, full)), shape((2, full)),
        ],
        40 * cells * full,
        far=grad_pieces,
        spill=(1, 2),
    )
    output_rows = (mine, here.swap(other))

    unite_all = here.everywhere(unite_pay)
    grad_unite_pre, unite_sums, trans_pushed, trans_pay = stage(
        functools.partial(back_trans_kernel, groups),
        "back_trans",
        [],
        [scal, *unite_all, unite_pushed, unite_pre, unite_coef, params, trans_pre, trans_coef],
        [shape((cells, full), BF), shape((2, full)), shape((cells, half)), shape((2, half))],
        2 * cells * half * full,
        [shape((cells, half))],
        far=[(w_unite, slice(half, full))],
    )
    trans_all = here.everywhere(trans_pay)
    if wide:

        def of_pair(pair):
            mine, other = pair
            return (mine.astype(F32) + here.swap(other).astype(F32)).astype(BF)

        share_unite = of_pair(
            stage(
                share_unite_kernel,
                "share_unite",
                [],
                [shortcut, transition, grad_unite_pre],
                [shape((full, full // chips // 2), BF)] * 2,
                2 * cells * full * full // chips,
            )
        )
    short_pushed, short_pay = stage(
        back_short_kernel,
        "back_short",
        [],
        [grad_unite_pre, short_pre, short_coef, params],
        [shape((cells, half)), shape((2, half))],
        2 * cells * half * full,
        [shape((cells, half))],
        far=[(w_unite, slice(0, half))],
    )
    grad_trans_pre, trans_sums, grad_merged, spatial_pushed, spatial_pay = stage(
        functools.partial(back_spatial_kernel, groups),
        "back_spatial",
        [],
        [scal, *trans_all, trans_pushed, trans_pre, trans_coef, spatial_pre, spatial_coef, params],
        [
            shape((cells, half), BF), shape((2, half)), shape((cells, half)), shape((cells, half)),
            shape((2, half)),
        ],
        2 * cells * half * half,
        far=[w_trans],
    )
    both_all = here.everywhere(jnp.concatenate([spatial_pay, short_pay], axis=1))
    spatial_all = [b[:, :half] for b in both_all]
    short_all = [b[:, half:] for b in both_all]
    grad_spatial_pre, spatial_sums, inner_pushed, inner_pay = stage(
        functools.partial(back_inner_kernel, groups, width),
        "back_inner",
        [],
        [scal,
            *spatial_all, spatial_pushed, spatial_pre, spatial_coef, inner_pre, inner_coef, params,
        ],
        [shape((cells, half), BF), shape((2, half)), shape((cells, half)), shape((2, half))],
        18 * cells * half * half,
        [shape((cells + 2 * width, 3 * half), BF), shape((cells, half))],
        far=[w_spatial.reshape(9 * half, half)],
    )
    inner_all = here.everywhere(inner_pay)
    grad_short_pre, short_sums = stage(
        functools.partial(settle_short_kernel, groups),
        "settle_short",
        [],
        [scal, *short_all, short_pushed, short_pre, short_coef, params],
        [shape((cells, half), BF), shape((2, half))],
        10 * cells * half,
    )
    if wide:
        lean = half // chips // 2
        share_spatial = of_pair(
            stage(
                functools.partial(share_spatial_kernel, cells),
                "share_spatial",
                [],
                [rim, grad_spatial_pre],
                [shape((lean, 9 * half), BF)] * 2,
                18 * cells * half * half // chips,
            )
        )
        share_pack = of_pair(
            stage(
                share_pack_kernel,
                "share_pack",
                [],
                [sectioned, grad_short_pre, merged, grad_trans_pre],
                [shape((lean, full + half), BF)] * 2,
                6 * cells * half * half // chips,
            )
        )
        inner_all[0], source, *shares = lax.optimization_barrier(
            (inner_all[0], source, share_unite, share_pack, share_spatial)
        )
        shares = lax.psum(tuple(shares), "batch")
    grad_inner_pre, inner_sums, main_pushed, main_pay = stage(
        functools.partial(back_main_kernel, groups),
        "back_main",
        [],
        [scal, *inner_all, inner_pushed, inner_pre, inner_coef, grad_merged, main_pre, main_coef, params],
        [shape((cells, half), BF), shape((2, half)), shape((cells, half)), shape((2, half))],
        2 * cells * half * half,
        [shape((cells, half))],
        far=[w_inner],
    )
    main_all = here.everywhere(main_pay)
    grad_main_pre, main_sums, down_pushed, down_pay = stage(
        functools.partial(back_down_kernel, groups),
        "back_down",
        [],
        [scal, *main_all, main_pushed, main_coef, down_coef, params],
        [shape((cells, half), BF), shape((2, half)), shape((cells, full)), shape((2, full))],
        4 * cells * half * full,
        [shape((cells, full))],
        far=[main_keep, w_main, grad_short_pre, w_short, down_keep], light=True)
    down_all = here.everywhere(down_pay)
    spare = width
    if wide:
        grad_cut = stage(
            functools.partial(cut_down_kernel, groups),
            "cut_down",
            [],
            [scal, *down_all, down_pushed, down_pre, down_coef, params],
            [shape((cells, full // chips), BF)],
            10 * cells * full // chips, light=True)[0]
        cuts = here.plane_hops(grad_cut)
    grad_down_pre, down_sums = stage(
        functools.partial(settle_down_kernel, groups),
        "settle_down",
        [],
        [scal, *down_all, down_pushed, down_pre, down_coef, params],
        [shape((cells + spare, full), BF), shape((2, full))],
        10 * cells * full, light=True)
    if not wide:
        output = jnp.stack(here.by_core(*output_rows)).reshape(grad_output.shape)
    norm_grads = stage(
        functools.partial(norm_sums_kernel, 2),
        "norm_sums",
        [],
        [down_sums, unite_sums, short_sums, main_sums, inner_sums, spatial_sums, trans_sums],
        [shape((2, full)), shape((5, half))] * 2,
        0,
        spill=range(4), light=True)
    if wide:
        near = pl.pallas_call(
            functools.partial(back_input_kernel, width),
            name="back_input",
            grid=(half // 128,),
            out_shape=shape((2, 2, 2 * width, half)),
            in_specs=[
                pl.BlockSpec((cells + spare, full), lambda n: (0, 0)),
                pl.BlockSpec((9, 128, full), lambda n: (0, n, 0)),
            ],
            out_specs=pl.BlockSpec((2, 2, 2 * width, 128), lambda n: (0, 0, 0, n)),
            scratch_shapes=[pltpu.VMEM((3 * width, full), BF)] * 2,
            compiler_params=pltpu.CompilerParams(vmem_limit_bytes=16 << 20),
            cost_estimate=LIGHT,
        )(grad_down_pre, in_hbm(w_down.reshape(9, half, full)))
        share_main = of_pair(
            stage(
                share_main_kernel,
                "share_main",
                [],
                [grad_main_pre, grad_inner_pre],
                [shape((lean, full + half), BF)] * 2,
                6 * cells * half * half // chips,
                far=[sectioned, mainline],
                light=True,
            )
        )
        columns = full // chips
        sums_here = [shape((full, 4 * columns)), shape((full, 4 * columns))]
        halves = [shape((9 * half, columns // 2), BF)] * 2

        def share_down(steps, earlier):
            outs = halves if earlier else sums_here
            near = [*(cuts[step] for step in steps), *earlier]
            scratch = [
                pltpu.VMEM((cells + spare, columns), BF),
                pltpu.VMEM((cells, 4 * columns), BF),
                pltpu.VMEM((len(steps), 2 * chips, 2, width, full), BF),
                pltpu.SemaphoreType.DMA((len(steps), 2 * chips)),
            ]
            if earlier:
                scratch = [pltpu.VMEM(a.shape, F32) for a in sums_here] + scratch
            return pl.pallas_call(
                functools.partial(share_down_kernel, steps, chips, width, int(bool(earlier))),
                name="share_down",
                out_shape=tuple(pltpu.VMEM(o.shape, o.dtype) for o in outs),
                in_specs=[VMEM] * len(near) + [ANY],
                out_specs=(VMEM,) * len(outs),
                scratch_shapes=scratch,
                compiler_params=pltpu.CompilerParams(vmem_limit_bytes=30 << 20),
                cost_estimate=LIGHT,
            )(*map(in_vmem, near), in_hbm(source))

        middle = (groups + 1) // 2
        cuts[:middle], near = lax.optimization_barrier((cuts[:middle], near))
        first_sums = share_down(range(middle), ())
        mains = here.plane_hops(after(share_main, grad_cut))
        cuts[middle:], first_sums = lax.optimization_barrier((cuts[middle:], first_sums))
        mine, other = share_down(range(middle, groups), first_sums)
        other, *tied = lax.optimization_barrier((other, *shares, *mains))
        shares, mains = tied[: len(shares)], tied[len(shares) :]
        grad_w_down = mine.astype(F32) + here.swap(other).astype(F32)
        outs = [
            shape((full, 2 * lean)), shape((lean, full)), shape((lean, half)), shape((lean, half)),
            shape((9, lean, half)), shape((lean, full)),
            shape(grad_output.shape, BF), shape(inputs.shape),
        ]
        placed = [*output_rows, near, here.swap(near)]
        early = pl.pallas_call(
            functools.partial(finish_kernel, groups),
            name="finish",
            out_shape=tuple(outs),
            in_specs=[ANY] * 3 + [VMEM] * groups + [ANY] * 4,
            out_specs=(VMEM,) * 6 + (ANY,) * 2,
            scratch_shapes=[pltpu.VMEM(one.shape, one.dtype) for one in shares]
            + [pltpu.SemaphoreType.DMA((7,))],
            compiler_params=pltpu.CompilerParams(vmem_limit_bytes=24 << 20),
            cost_estimate=LIGHT,
        )(*map(in_hbm, shares), *mains, *placed)
        output, grad_inputs = early[6:]
        early = [
            early[1].T, early[5].T, early[3].T, jnp.swapaxes(early[4], 1, 2), early[2].T, early[0],
        ]
    else:
        grad_down_pre = grad_down_pre[:cells]
        def share(values, grad):
            columns = grad.shape[1] // chips
            grad = lax.dynamic_slice_in_dim(grad, here.chip * columns, columns, 1)
            part = jnp.concatenate([dot_cells(v, grad) for v in values], axis=0)
            mine, other = here.split(part.reshape(part.shape[0], 2, columns // 2), 1)
            return (mine + here.swap(other.astype(BF)).astype(F32)).astype(BF)

        windows = [rim[i * width : i * width + cells] for i in range(3)]
        early = lax.psum(
            (
                share([sectioned], grad_short_pre),
                share([sectioned], grad_main_pre),
                share([mainline], grad_inner_pre),
                share(windows, grad_spatial_pre),
                share([merged], grad_trans_pre),
                jnp.concatenate([share([shortcut], grad_unite_pre), share([transition], grad_unite_pre)]),
            ),
            "batch",
        )
        early = [e.astype(F32) for e in early]

        mine, other = here.split(view)
        got = here.chip_hops(jnp.stack([mine, here.swap(other)], axis=1))
        source = jnp.zeros((2, here.rows, width, full), BF)
        for step, piece in enumerate(got):
            for side in range(2):
                source = lax.dynamic_update_slice_in_dim(
                    source, piece[:, side : side + 1], 2 * (here.chip ^ step) + (here.core ^ side), 1
                )
        grad_map = grad_down_pre.reshape(height, width, full)
        columns = full // chips
        grad_cut = lax.dynamic_slice_in_dim(grad_map, here.chip * columns, columns, 2)
        ahead = jnp.pad(grad_cut[:, 1:], ((0, 0), (0, 1), (0, 0)))
        upper = jnp.pad(grad_cut[1:], ((0, 1), (0, 0), (0, 0)))
        both_ahead = jnp.pad(ahead[1:], ((0, 1), (0, 0), (0, 0)))
        even_rows = source[0].reshape(cells, full)
        odd_rows = source[1].reshape(cells, full)

        def taps_of(rows, here_grad, ahead_grad):
            plain = dot_cells(rows, here_grad.reshape(cells, columns))
            before = dot_cells(rows[:, half:], ahead_grad.reshape(cells, columns))
            return [before, plain]

        part = jnp.concatenate(
            taps_of(odd_rows, upper, both_ahead)
            + taps_of(even_rows, grad_cut, ahead)
            + taps_of(odd_rows, grad_cut, ahead),
            axis=0,
        )
        mine, other = here.split(part.reshape(9 * half, 2, columns // 2), 1)
        part = (mine + here.swap(other.astype(BF)).astype(F32)).astype(BF)
        grad_w_down = lax.psum(part, "batch").astype(F32)

        pair_rows = 2 * height_dev
        grad_image = jnp.pad(grad_map, ((0, 1), (0, 0), (0, 0)))
        grad_block = lax.dynamic_slice_in_dim(grad_image, here.chip * pair_rows, pair_rows + 1, 0)
        widened = lax.conv_general_dilated(
            grad_block[None],
            flipped(w_down),
            (1, 1),
            ((1, 0), (1, 2)),
            lhs_dilation=(2, 2),
            dimension_numbers=("NHWC", "HWIO", "NHWC"),
            preferred_element_type=F32,
        )[0]
        mine = lax.dynamic_slice_in_dim(widened, here.core * pair_rows, pair_rows, 0)
        other = lax.dynamic_slice_in_dim(widened, (1 - here.core) * pair_rows, pair_rows, 0)
        grad_inputs = jnp.stack(here.by_core(mine, here.swap(other)))

    return (
        output,
        grad_inputs,
        grad_w_down.reshape(3, 3, half, -1),
        early[0],
        early[1],
        early[2],
        early[3].reshape(3, 3, half, -1),
        early[4],
        early[5],
        *norm_grads,
    )


def solution(mesh):
    placed = (P("batch", "rows", None, None),) + (P(),) * 12 + (P("batch", "rows", None, None),)
    return jax.shard_map(
        on_device,
        mesh=mesh,
        in_specs=placed,
        out_specs=(
            P("batch", "rows", None, None),
            P("batch", "rows", None, None),
            P(None, None, None, "rows"),
            P(None, "rows"),
            P(None, "rows"),
            P(None, "rows"),
            P(None, None, None, "rows"),
            P(None, "rows"),
            P(None, "rows"),
            P(),
            P(),
            P(),
            P(),
        ),
        check_vma=False,
    )
```
